32 devices in a mesh: space: 8 (over z, x), modes: 4 (over y, core).
Axes of the slice: x: 2, y: 2, z: 4, core: 2. Of those that a mesh axis runs over, the one named last changes fastest.
Arguments:
- mode_field: bfloat16 [16, 128, 256, 256], P('space', 'modes'), may hold values from -8 to 8
- diffusion: float32 [16, 256, 256], P('space'), may hold values from 0.1 to 0.16
- joule_load: float32 [16, 256, 256], P('space'), may hold values from 0.5 to 1.5
- chaos_basis: bfloat16 [343, 128], replicated, may hold values from -0.5 to 0.5
- quad_weight: float32 [343], replicated, may hold values from 0.25 to 1
- base_conductivity: float32 [343], replicated, may hold values from 0.5 to 2
- thermal_slope: float32 [343], replicated, may hold values from 0.2 to 0.8
Outputs:
- advanced: bfloat16 [16, 128, 256, 256], P('space', 'modes')
The draws below stay inside these ranges and needn't reach their ends.
All inputs are finite; a program needn't handle non-finite values.
Results may differ from the reference program's by a relative error of at most 0.0054.
Values may be sent and summed in bfloat16 or wider, within the bound.
No kernel may reach another device: no remote copies, remote signals or barrier semaphores. Data moves between devices by JAX's collectives and lax.ppermute only.
A program may use at most 128 MiB of HBM per device.

```python
import math
import jax
import jax.numpy as jnp
from jax import lax

MODES = 128
Q = 343
NX = 256
NY = 256
NZ = 16


def draw_mode_field(key, part):
    noise_key = jax.random.fold_in(key, 11)
    amplitude_key = jax.random.fold_in(key, 12)
    count_key = jax.random.fold_in(key, 13)
    phase_key = jax.random.fold_in(key, 14)
    full_shape = (NZ, MODES, NX, NY)
    rough_part = jnp.clip(jax.random.normal(noise_key, full_shape, jnp.float32), -2.5, 2.5)
    amplitude = jax.random.uniform(amplitude_key, (MODES,), jnp.float32, 0.6, 2.0)
    wave_count = jax.random.randint(count_key, (3, MODES), 1, 3).astype(jnp.float32)
    phase_shift = jax.random.uniform(phase_key, (3, MODES), jnp.float32, 0.0, 2.0 * math.pi)
    depth_coord = (jnp.arange(NZ, dtype=jnp.float32) + 0.5) / NZ
    row_coord = (jnp.arange(NX, dtype=jnp.float32) + 0.5) / NX
    column_coord = (jnp.arange(NY, dtype=jnp.float32) + 0.5) / NY
    depth_wave = jnp.sin(2.0 * math.pi * depth_coord[:, None] * wave_count[0][None, :] + phase_shift[0][None, :])
    row_wave = jnp.sin(2.0 * math.pi * wave_count[1][:, None] * row_coord[None, :] + phase_shift[1][:, None])
    column_wave = jnp.sin(2.0 * math.pi * wave_count[2][:, None] * column_coord[None, :] + phase_shift[2][:, None])
    summed_waves = depth_wave[:, :, None, None] + row_wave[None, :, :, None] + column_wave[None, :, None, :]
    smooth_part = amplitude[None, :, None, None] * summed_waves / 1.2247
    return (smooth_part + rough_part).astype(jnp.bfloat16)


def level_of(key, extent, pieces, least, top_value):
    def one(dim, parts):
        draws = jax.random.uniform(jax.random.fold_in(jax.random.fold_in(key, 6), dim), (parts,), jnp.float32, least / len(pieces), top_value / len(pieces))
        return jnp.repeat(jnp.exp(draws), extent[dim] // parts).reshape((-1,) + (1,) * (len(extent) - dim - 1))

    level = one(*pieces[0])
    for cut in pieces[1:]:
        level = level * one(*cut)
    return level


def bell_draw(rng, dims, width, bound, held_as=jnp.bfloat16):
    entries = jax.random.normal(rng, dims, jnp.float32) * width
    return jnp.minimum(jnp.maximum(entries, -bound), bound).astype(held_as)


def setup_inputs(seed: int = 0) -> dict:
    seeds = jax.random.split(jax.random.key(seed), 8)
    return {
        "mode_field": draw_mode_field(jax.random.fold_in(seeds[7], 71), 0),
        "diffusion": jnp.clip(0.1 + 0.059999995 * jax.random.uniform(seeds[1], (NZ, NX, NY), jnp.float32) ** level_of(seeds[1], (NZ, NX, NY), ((0, 8),), -0.2, 0.2), 0.1, 0.16),
        "joule_load": jnp.clip(0.5 + 1.0 * jax.random.uniform(seeds[2], (NZ, NX, NY), jnp.float32) ** level_of(seeds[2], (NZ, NX, NY), ((0, 8),), -0.2, 0.2), 0.5, 1.5),
        "chaos_basis": bell_draw(seeds[3], (Q, MODES), MODES ** -0.5, 0.5),
        "quad_weight": jnp.clip(jnp.exp(jax.random.uniform(seeds[4], (Q,), jnp.float32, math.log(0.25), math.log(1.0))), 0.25, 1.0),
        "base_conductivity": jnp.clip(jnp.exp(jax.random.uniform(seeds[5], (Q,), jnp.float32, math.log(0.5), math.log(2.0))), 0.5, 2.0),
        "thermal_slope": jnp.clip(jax.random.uniform(seeds[6], (Q,), jnp.float32, 0.2, 0.8), 0.2, 0.8),
    }


def transport(values, diffusion):
    for sweep in range(2):
        padded = jnp.pad(values, 1)
        beside = padded[2:, 1:-1, 1:-1] + padded[:-2, 1:-1, 1:-1]
        beside = beside + padded[1:-1, 2:, 1:-1] + padded[1:-1, :-2, 1:-1]
        beside = beside + padded[1:-1, 1:-1, 2:] + padded[1:-1, 1:-1, :-2]
        values = values + diffusion * (beside - 6.0 * values)
    return values.astype(jnp.bfloat16)


def reference(mode_field, diffusion, joule_load, chaos_basis, quad_weight, base_conductivity, thermal_slope):
    moved = lax.map(lambda single: transport(single.astype(jnp.float32), diffusion), jnp.swapaxes(mode_field, 0, 1))
    moved = jnp.swapaxes(moved, 0, 1)
    basis_wide = chaos_basis.astype(jnp.float32)

    def per_plane(pair):
        plane, load_plane = pair
        point_temp = jnp.einsum("qm,mxy->qxy", basis_wide, plane.astype(jnp.float32), precision=lax.Precision.HIGHEST)
        conductivity = base_conductivity[:, None, None] * (1.0 + thermal_slope[:, None, None] * jnp.tanh(point_temp))
        weighted = (quad_weight[:, None, None] * conductivity).astype(jnp.bfloat16)
        projected = jnp.einsum("qm,qxy->mxy", basis_wide, weighted.astype(jnp.float32), precision=lax.Precision.HIGHEST).astype(jnp.bfloat16)
        kept_modes = lax.optimization_barrier(plane).astype(jnp.float32)
        return (kept_modes + load_plane[None] * projected.astype(jnp.float32)).astype(jnp.bfloat16)

    return lax.map(per_plane, (moved, joule_load))
```

```python
import functools

import jax
import jax.numpy as jnp
from jax import lax
from jax.experimental import pallas as pl
from jax.experimental.pallas import tpu as pltpu
from jax.sharding import PartitionSpec as P

F32, BF16 = jnp.float32, jnp.bfloat16
ANY = pl.BlockSpec(memory_space=pl.ANY)
VMEM = pl.BlockSpec(memory_space=pltpu.VMEM)
SMEM = pl.BlockSpec(memory_space=pltpu.SMEM)
VMEM_LIMIT = 44 * 1024 * 1024
EDGE = 2
LANES = 128


def lanes(h):
    return pl.ds(h * LANES, LANES)


def params():
    return pltpu.CompilerParams(vmem_limit_bytes=VMEM_LIMIT)


def cost(flops, bytes_accessed):
    return pl.CostEstimate(flops=int(flops), bytes_accessed=int(bytes_accessed), transcendentals=0)


def to_bf16_rows(x):
    a, m, y = x.shape
    if m % 16 == 0:
        return x.astype(BF16).reshape(a * m, y)
    return x.astype(F32).reshape(a * m, y).astype(BF16)


def spread_kernel(pos, field, own, send, window, wide, sems, *, begin, skip):
    side = pos[0]
    _, planes, modes, depth, _ = window.shape
    size = field.shape[2]
    rows = own.shape[0]
    parts = wide.shape[2]
    copies = []
    for a in range(2):
        far = side if a == 0 else 1 - side
        start = jnp.where(far == 1, size - depth - begin, begin)
        start = pl.multiple_of(start, 16)
        copy = pltpu.make_async_copy(
            field.at[:, :, pl.ds(start, depth), :], window.at[a], sems.at[a]
        )
        copy.start()
        copies.append(copy)
    for a, out in ((1, send), (0, own)):
        far = side if a == 0 else 1 - side
        copies[a].wait()
        for z in range(planes):
            for h in range(parts):
                wide[a, z, h] = window[a, z, :, :, lanes(h)].astype(F32).reshape(modes * depth, LANES)

        def row(i, _):
            w = jnp.where(far == 1, depth - 1 - skip - i, skip + i)
            for z in range(planes):
                to = jnp.where(far == 1, z, planes - 1 - z)
                for h in range(parts):
                    out[i, to, :, lanes(h)] = wide[a, z, h, pl.ds(w, modes, stride=depth), :].astype(BF16)
            return 0

        lax.fori_loop(0, rows, row, 0)


def spread(pos, field, begin, skip, rows, depth):
    planes, modes, _, cols = field.shape
    piece = jax.ShapeDtypeStruct((rows, planes, modes, cols), BF16)
    return pl.pallas_call(
        functools.partial(spread_kernel, begin=begin, skip=skip),
        out_shape=(piece, piece),
        in_specs=[SMEM, ANY],
        out_specs=(VMEM, VMEM),
        scratch_shapes=[
            pltpu.VMEM((2, planes, modes, depth, cols), BF16),
            pltpu.VMEM((2, planes, cols // LANES, modes * depth, LANES), F32),
            pltpu.SemaphoreType.DMA((2,)),
        ],
        compiler_params=params(),
        cost_estimate=cost(3e9, 4 * rows * planes * modes * cols * 2),
        name="spread",
    )(pos, field)


def sweep_kernel(pos, rate, shift, *refs, begin, count, heads):
    group = 4
    blocks, refs = refs[:group], refs[group:]
    tails, refs = refs[:heads], refs[heads:]
    outs, (field, first, sems) = refs[:count], refs[count:]
    _, stack, modes, cols = field.shape
    planes = stack // group
    mine = stack - 2 * planes
    rows = first.shape[0] - 2
    lead = 2 * EDGE if heads else EDGE
    copies = []
    for g in range(group):
        to = pl.ds(g * planes, planes)
        copies.append(
            pltpu.make_async_copy(blocks[g], field.at[pl.ds(lead, rows + 2 * EDGE - lead), to], sems.at[g])
        )
        if heads:
            length = tails[g].shape[0]
            copies.append(
                pltpu.make_async_copy(
                    tails[g].at[pl.ds(length - lead, lead)], field.at[pl.ds(0, lead), to], sems.at[group + g]
                )
            )
    for copy in copies:
        copy.start()
    if not heads:
        field[pl.ds(0, lead)] = jnp.zeros((lead, stack, modes, cols), BF16)
    for copy in copies:
        copy.wait()
    low = planes - 1
    wide = mine + 2

    def pair(j, _):
        i = 2 * j
        middle = field[pl.ds(i + 1, 2), pl.ds(low, wide)]
        beside = jnp.dot(
            to_bf16_rows(middle.reshape(2 * wide, modes, cols)), shift[...], preferred_element_type=F32
        ).reshape(2, wide, modes, cols)
        for a in range(2):
            line = [field[i + 1 + a, low - 1 + p].astype(F32) for p in range(wide + 2)]
            for p in range(wide):
                centre = line[p + 1]
                around = beside[a, p] + (line[p] + line[p + 2])
                around = around + (field[i + a, low + p].astype(F32) + field[i + 2 + a, low + p].astype(F32))
                speed = rate[p, pl.ds(begin + i + a, 1), :]
                first[i + a, p] = centre + speed * (around - 6.0 * centre)
        return 0

    lax.fori_loop(0, (rows + 2) // 2, pair, 0)
    part = rows // count
    for k in range(count):
        base = jnp.bitwise_xor(pos[1], k) * part

        def row(i, _):
            g = base + i
            line = [first[g + 1, p] for p in range(wide)]
            beside = jnp.dot(
                to_bf16_rows(first[g + 1, pl.ds(1, mine)]), shift[...], preferred_element_type=F32
            ).reshape(mine, modes, cols)
            for p in range(mine):
                centre = line[p + 1]
                around = beside[p] + (line[p] + line[p + 2])
                around = around + (first[g, p + 1] + first[g + 2, p + 1])
                speed = rate[p + 1, pl.ds(begin + g + 1, 1), :]
                outs[k][i, p] = (centre + speed * (around - 6.0 * centre)).astype(BF16)
            return 0

        lax.fori_loop(0, part, row, 0)


def sweep(pos, rate, shift, blocks, tails, begin, rows, count):
    _, planes, modes, cols = blocks[0].shape
    mine = 2 * planes
    piece = jax.ShapeDtypeStruct((rows // count, mine, modes, cols), BF16)
    return pl.pallas_call(
        functools.partial(sweep_kernel, begin=begin, count=count, heads=len(tails)),
        out_shape=(piece,) * count,
        in_specs=[SMEM, VMEM, VMEM] + [ANY] * (4 + len(tails)),
        out_specs=(VMEM,) * count,
        scratch_shapes=[
            pltpu.VMEM((rows + 2 * EDGE, 4 * planes, modes, cols), BF16),
            pltpu.VMEM((rows + 2, mine + 2, modes, cols), F32),
            pltpu.SemaphoreType.DMA((8,)),
        ],
        compiler_params=params(),
        cost_estimate=cost(8e9, 3 * rows * mine * modes * cols * 2),
        name="sweep",
    )(pos, rate, shift, *blocks, *tails)


def points_kernel(pos, basis, basis_t, flat, swing, load, *refs, begin):
    count = len(refs) // 2
    blocks, outs = refs[:count], refs[count:]
    part, planes, modes, cols = blocks[0].shape
    copies = cols // flat.shape[1]

    def row(i, _):
        place = begin + pos[1] * part + i
        for p in range(planes):
            if modes % 16 == 0:
                cells = jnp.concatenate([block[i, p] for block in blocks], axis=0)
            else:
                cells = jnp.concatenate([block[i, p].astype(F32) for block in blocks], axis=0).astype(BF16)
            heat = jnp.tanh(jnp.dot(basis[...], cells, preferred_element_type=F32))
            offset = jnp.concatenate([flat[...]] * copies, axis=1)
            slope = jnp.concatenate([swing[...]] * copies, axis=1)
            weighted = (offset + slope * heat).astype(BF16)
            source = jnp.dot(basis_t[...], weighted, preferred_element_type=F32).astype(BF16).astype(F32)
            done = cells.astype(F32) + load[p, pl.ds(place, 1), :] * source
            for k in range(count):
                outs[k][i, p] = done[k * modes : (k + 1) * modes].astype(BF16)
        return 0

    lax.fori_loop(0, part, row, 0)


def points(pos, basis, basis_t, flat, swing, load, blocks, begin):
    count = len(blocks)
    size = sum(block.size for block in blocks)
    return pl.pallas_call(
        functools.partial(points_kernel, begin=begin),
        out_shape=tuple(jax.ShapeDtypeStruct(block.shape, BF16) for block in blocks),
        in_specs=[SMEM] + [VMEM] * (5 + count),
        out_specs=(VMEM,) * count,
        compiler_params=params(),
        cost_estimate=cost(8e9, 4 * size),
        name="points",
    )(pos, basis, basis_t, flat, swing, load, *blocks)


def collect_kernel(pos, *refs):
    *blocks, out, sems = refs
    part, planes = blocks[0].shape[0], out.shape[1]
    copies = []
    for k, block in enumerate(blocks):
        base = jnp.bitwise_xor(pos[1], k) * part
        copies.append(
            pltpu.make_async_copy(block.at[:, pl.ds(0, planes)], out.at[pl.ds(base, part)], sems.at[k])
        )
    for copy in copies:
        copy.start()
    for copy in copies:
        copy.wait()


def collect(pos, blocks):
    part, planes, modes, cols = blocks[0].shape
    count = len(blocks)
    shape = (part * count, planes // 2, modes, cols)
    return pl.pallas_call(
        collect_kernel,
        out_shape=jax.ShapeDtypeStruct(shape, BF16),
        in_specs=[SMEM] + [ANY] * count,
        out_specs=ANY,
        scratch_shapes=[pltpu.SemaphoreType.DMA((count,))],
        compiler_params=params(),
        cost_estimate=cost(1e9, 2 * blocks[0].size * count),
        name="collect",
    )(pos, *blocks)


def settle_kernel(pos, *refs, begin, count, chained):
    if chained:
        refs = refs[1:]
    blocks, other = refs[:count], refs[count]
    out, wide, final, sems = refs[count + 1 :]
    side = pos[0]
    part = blocks[0].shape[0]
    rows, planes, modes, cols = other.shape
    size = out.shape[2]
    parts = wide.shape[2]

    for k in range(count):
        base = jnp.bitwise_xor(pos[1], k) * part

        def own_row(i, _):
            r = base + i
            to = jnp.where(side == 1, rows - 1 - r, r)
            for z in range(planes):
                place = jnp.where(side == 1, z, planes - 1 - z)
                for h in range(parts):
                    wide[0, place, h, pl.ds(pl.multiple_of(to * modes, modes), modes), :] = blocks[k][
                        i, planes + z, :, lanes(h)
                    ].astype(F32)
            return 0

        lax.fori_loop(0, part, own_row, 0)

    def other_row(r, _):
        to = jnp.where(side == 0, rows - 1 - r, r)
        for z in range(planes):
            place = jnp.where(side == 0, z, planes - 1 - z)
            for h in range(parts):
                wide[1, place, h, pl.ds(pl.multiple_of(to * modes, modes), modes), :] = other[
                    r, z, :, lanes(h)
                ].astype(F32)
        return 0

    lax.fori_loop(0, rows, other_row, 0)

    def mode(m, _):
        for a in range(2):
            for z in range(planes):
                for h in range(parts):
                    final[a, z, m, :, lanes(h)] = wide[a, z, h, pl.ds(m, rows, stride=modes), :].astype(BF16)
        return 0

    lax.fori_loop(0, modes, mode, 0)
    copies = []
    for a in range(2):
        far = side if a == 0 else 1 - side
        start = pl.multiple_of(jnp.where(far == 1, size - rows - begin, begin), 16)
        copies.append(pltpu.make_async_copy(final.at[a], out.at[:, :, pl.ds(start, rows), :], sems.at[a]))
    for copy in copies:
        copy.start()
    for copy in copies:
        copy.wait()


def settle(pos, result, blocks, other, begin, shape):
    count = len(blocks)
    rows, planes, modes, cols = other.shape
    chained = result is not None
    return pl.pallas_call(
        functools.partial(settle_kernel, begin=begin, count=count, chained=chained),
        out_shape=jax.ShapeDtypeStruct(shape, BF16),
        in_specs=[SMEM] + ([ANY] if chained else []) + [VMEM] * (count + 1),
        out_specs=ANY,
        scratch_shapes=[
            pltpu.VMEM((2, planes, cols // LANES, rows * modes, LANES), F32),
            pltpu.VMEM((2, planes, modes, rows, cols), BF16),
            pltpu.SemaphoreType.DMA((2,)),
        ],
        input_output_aliases={1: 0} if chained else {},
        compiler_params=params(),
        cost_estimate=cost(3e9, 4 * rows * planes * modes * cols * 2),
        name="settle",
    )(pos, *([result] if chained else []), *blocks, other)


def chunk_rows(half):
    return [half // 4] * 4


def on_device(field, diffusion, joule, basis, quad_weight, base_conductivity, thermal_slope):
    planes, modes, size, cols = field.shape
    half = size // 2
    spaces, count = lax.axis_size("space"), lax.axis_size("modes")
    side = lax.axis_index("space") % 2
    me = lax.axis_index("modes")
    pos = jnp.stack([side, me]).astype(jnp.int32)

    swap = [(i, i ^ 1) for i in range(spaces)]
    ahead = [(i, i + 4 * (i % 2) - 2) for i in range(spaces)]
    ahead = [(i, j) for i, j in ahead if 0 <= j < spaces]
    back = [(j, i) for i, j in ahead]

    def across(x):
        return lax.ppermute(x, "space", swap)

    def halo(own, other):
        return lax.ppermute(own, "space", ahead), lax.ppermute(other, "space", back)

    def exchange(pieces):
        moved = [pieces[0]]
        for k in range(1, count):
            moved.append(lax.ppermute(pieces[k], "modes", [(j, j ^ k) for j in range(count)]))
        return moved

    def logical(x, length):
        rows_back, planes_back = jnp.flip(x, 1)[:, :length], jnp.flip(x, 0)[:, :length]
        own = jnp.where(side == 1, rows_back, planes_back)
        return own, across(jnp.where(side == 1, planes_back, rows_back))

    own_rate, other_rate = logical(diffusion, half + EDGE)
    before, after = halo(own_rate[-1:], other_rate[:1])
    rate = jnp.concatenate([before, other_rate, own_rate, after], axis=0)
    rate = jnp.pad(rate, ((0, 0), (1, -(half + EDGE + 1) % 8), (0, 0)))
    own_load, other_load = logical(joule, half)
    load = jnp.concatenate([other_load, own_load], axis=0)

    lane = jnp.arange(cols)
    shift = (jnp.abs(lane[:, None] - lane[None, :]) == 1).astype(BF16)

    points_count = basis.shape[0]
    extra = -points_count % 32
    turned = jnp.concatenate(
        [lax.dynamic_slice_in_dim(basis, (me ^ k) * modes, modes, axis=1) for k in range(count)], axis=1
    )
    turned = jnp.pad(turned, ((0, extra), (0, 0)))
    turned_t = turned.T
    level = quad_weight * base_conductivity
    spread_out = lambda v: jnp.broadcast_to(jnp.pad(v, (0, extra))[:, None], (points_count + extra, 128))
    flat, swing = spread_out(level), spread_out(level * thermal_slope)

    rows_of = chunk_rows(half)
    begins = [sum(rows_of[:c]) for c in range(len(rows_of))]
    result = None
    tails = ()
    for begin, rows in zip(begins, rows_of):
        skip = EDGE if begin else 0
        own, send = spread(pos, field, begin, skip, rows + EDGE - skip, rows + 16)
        other = across(send)
        before, after = halo(own, other)
        blocks = (before, other, own, after)
        pieces = sweep(pos, rate, shift, blocks, tails, begin, rows, count)
        tails = blocks
        cells = exchange(pieces)
        stepped = points(pos, turned, turned_t, flat, swing, load, cells, begin)
        home = exchange(stepped)
        theirs = across(collect(pos, home))
        result = settle(pos, result, home, theirs, begin, field.shape)
    return result


def solution(mesh):
    return jax.shard_map(
        on_device,
        mesh=mesh,
        in_specs=(
            P("space", "modes", None, None),
            P("space", None, None),
            P("space", None, None),
            P(),
            P(),
            P(),
            P(),
        ),
        out_specs=P("space", "modes", None, None),
        check_vma=False,
    )
```

```python
import functools

import jax
import jax.numpy as jnp
from jax import lax
from jax.experimental import pallas as pl
from jax.experimental.pallas import tpu as pltpu
from jax.sharding import PartitionSpec as P

F32, BF16 = jnp.float32, jnp.bfloat16
ANY = pl.BlockSpec(memory_space=pl.ANY)
VMEM = pl.BlockSpec(memory_space=pltpu.VMEM)
SMEM = pl.BlockSpec(memory_space=pltpu.SMEM)
VMEM_LIMIT = 58 * 1024 * 1024
TOKEN = jax.ShapeDtypeStruct((2,), jnp.int32)
COST = pl.CostEstimate(flops=1, bytes_accessed=1, transcendentals=0)
EDGE = 2
TILE = 16


def params():
    return pltpu.CompilerParams(vmem_limit_bytes=VMEM_LIMIT)


def from_rows(y, group):
    if group % 16 == 0:
        return y.astype(BF16).reshape(-1, group, y.shape[1])
    return y.reshape(-1, group, y.shape[1]).astype(BF16)


def to_bf16_rows(x):
    a, m, y = x.shape
    if m % 16 == 0:
        return x.astype(BF16).reshape(a * m, y)
    return x.astype(F32).reshape(a * m, y).astype(BF16)


def spread_kernel(pos, field, turn, *refs, begin, skip):
    own, send, token, window, sems = refs[-5:]
    side = pos[0]
    token[0], token[1] = pos[0], pos[1]
    _, planes, modes, depth, cols = window.shape
    size = field.shape[2]
    rows = own.shape[0]
    group = turn.shape[1] // TILE
    copies = []
    for a in range(2):
        far = 1 - side if a == 0 else side
        start = jnp.where(far == 1, size - depth - begin, begin)
        start = pl.multiple_of(start, TILE)
        copy = pltpu.make_async_copy(
            field.at[:, :, pl.ds(start, depth), :], window.at[a], sems.at[a]
        )
        copy.start()
        copies.append(copy)
    for a, out in ((0, send), (1, own)):
        far = 1 - side if a == 0 else side
        copies[a].wait()
        for z in range(planes):
            to = jnp.where(far == 1, z, planes - 1 - z)
            for g in range(depth // TILE):
                block = jnp.where(far == 1, depth // TILE - 1 - g, g)
                low, high = max(0, skip - g * TILE), min(TILE, rows + skip - g * TILE)
                if high <= low:
                    continue
                for h in range(modes // group):
                    there = pl.ds(h * group, group)
                    x = window[a, z, there, pl.ds(pl.multiple_of(block * TILE, TILE), TILE), :]
                    y = jnp.dot(turn[far], x.reshape(group * TILE, cols), preferred_element_type=F32)
                    y = from_rows(y, group)
                    out[pl.ds(g * TILE + low - skip, high - low), to, there, :] = y[low:high]


def spread(pos, field, turn, after, begin, skip, rows, depth):
    planes, modes, _, cols = field.shape
    piece = jax.ShapeDtypeStruct((rows, planes, modes, cols), BF16)
    return pl.pallas_call(
        functools.partial(spread_kernel, begin=begin, skip=skip),
        out_shape=(piece, piece, TOKEN),
        in_specs=[SMEM, ANY, VMEM] + [ANY] * len(after),
        out_specs=(VMEM, VMEM, SMEM),
        scratch_shapes=[
            pltpu.VMEM((2, planes, modes, depth, cols), BF16),
            pltpu.SemaphoreType.DMA((2,)),
        ],
        compiler_params=params(),
        cost_estimate=COST,
        name="spread",
    )(pos, field, turn, *after)


def sweep_kernel(pos, rate, shift, *refs, begin, count, heads):
    group = 4
    blocks, refs = refs[:group], refs[group:]
    tails, refs = refs[:heads], refs[heads:]
    outs, (token, field, first, aside, final, sems) = refs[:count], refs[count:]
    token[0], token[1] = pos[0], pos[1]
    _, stack, modes, cols = field.shape
    planes = stack // group
    mine = stack - 2 * planes
    rows = final.shape[0]
    lead = 2 * EDGE if heads else EDGE
    copies = []
    for g in range(group):
        to = pl.ds(g * planes, planes)
        copies.append(
            pltpu.make_async_copy(blocks[g], field.at[pl.ds(lead, rows + 2 * EDGE - lead), to], sems.at[g])
        )
        if heads:
            length = tails[g].shape[0]
            copies.append(
                pltpu.make_async_copy(
                    tails[g].at[pl.ds(length - lead, lead)], field.at[pl.ds(0, lead), to], sems.at[group + g]
                )
            )
    for copy in copies:
        copy.start()
    if not heads:
        field[pl.ds(0, lead)] = jnp.zeros((lead, stack, modes, cols), BF16)
    for copy in copies:
        copy.wait()
    low = planes - 1
    wide = mine + 2
    piece = min(modes, 16)

    def beside(x):
        return jnp.dot(
            to_bf16_rows(x.reshape(-1, modes, cols)), shift[...], preferred_element_type=F32
        ).reshape(x.shape[:2] + (modes, cols))

    def look(j, slot):
        aside[slot] = beside(field[pl.ds(2 * j + 1, 2), pl.ds(low, wide)])

    look(0, 0)

    def pair(j, _):
        slot = j % 2
        i = 2 * j

        look(jnp.minimum(j + 1, (rows + 2) // 2 - 1), 1 - slot)
        for a in range(2):
            speeds = [rate[p, pl.ds(begin + i + a, 1), :] for p in range(wide)]
            for h in range(modes // piece):
                some = pl.ds(h * piece, piece)
                line = [field[i + 1 + a, low - 1 + p, some].astype(F32) for p in range(wide + 2)]
                for p in range(wide):
                    centre = line[p + 1]
                    around = aside[slot, a, p, some] + (line[p] + line[p + 2])
                    around = around + (
                        field[i + a, low + p, some].astype(F32) + field[i + 2 + a, low + p, some].astype(F32)
                    )
                    first[i + a, p, some] = centre + speeds[p] * (around - 6.0 * centre)
        return 0

    lax.fori_loop(0, (rows + 2) // 2, pair, 0)

    def look_again(j, slot):
        aside[slot, :, pl.ds(0, mine)] = beside(first[pl.ds(2 * j + 1, 2), pl.ds(1, mine)])

    look_again(0, 0)

    def pair_again(j, _):
        slot = j % 2
        i = 2 * j

        look_again(jnp.minimum(j + 1, rows // 2 - 1), 1 - slot)
        for a in range(2):
            speeds = [rate[p + 1, pl.ds(begin + i + a + 1, 1), :] for p in range(mine)]
            for h in range(modes // piece):
                some = pl.ds(h * piece, piece)
                line = [first[i + 1 + a, p, some] for p in range(wide)]
                for p in range(mine):
                    centre = line[p + 1]
                    around = aside[slot, a, p, some] + (line[p] + line[p + 2])
                    around = around + (first[i + a, p + 1, some] + first[i + 2 + a, p + 1, some])
                    final[i + a, p, some] = (centre + speeds[p] * (around - 6.0 * centre)).astype(BF16)
        return 0

    lax.fori_loop(0, rows // 2, pair_again, 0)
    part = rows // count
    copies = []
    for k in range(count):
        base = jnp.bitwise_xor(pos[1], k) * part
        copies.append(pltpu.make_async_copy(final.at[pl.ds(base, part)], outs[k], sems.at[2 * group + k]))
    for copy in copies:
        copy.start()
    for copy in copies:
        copy.wait()


def sweep(pos, rate, shift, blocks, tails, begin, rows, count):
    _, planes, modes, cols = blocks[0].shape
    mine = 2 * planes
    piece = jax.ShapeDtypeStruct((rows // count, mine, modes, cols), BF16)
    return pl.pallas_call(
        functools.partial(sweep_kernel, begin=begin, count=count, heads=len(tails)),
        out_shape=(piece,) * count + (TOKEN,),
        in_specs=[SMEM, VMEM, VMEM] + [ANY] * (4 + len(tails)),
        out_specs=(ANY,) * count + (SMEM,),
        scratch_shapes=[
            pltpu.VMEM((rows + 2 * EDGE, 4 * planes, modes, cols), BF16),
            pltpu.VMEM((rows + 2, mine + 2, modes, cols), F32),
            pltpu.VMEM((2, 2, mine + 2, modes, cols), F32),
            pltpu.VMEM((rows, mine, modes, cols), BF16),
            pltpu.SemaphoreType.DMA((8 + count,)),
        ],
        compiler_params=params(),
        cost_estimate=COST,
        name="sweep",
    )(pos, rate, shift, *blocks, *tails)


def points_kernel(pos, basis, basis_t, flat, swing, load, *refs, begin):
    *refs, token = refs
    token[0], token[1] = pos[0], pos[1]
    count = len(refs) // 2
    blocks, outs = refs[:count], refs[count:]
    part, planes, modes, cols = blocks[0].shape
    copies = cols // flat.shape[1]

    def row(i, _):
        place = begin + pos[1] * part + i
        for p in range(planes):
            if modes % 16 == 0:
                cells = jnp.concatenate([block[i, p] for block in blocks], axis=0)
            else:
                cells = jnp.concatenate([block[i, p].astype(F32) for block in blocks], axis=0).astype(BF16)
            heat = jnp.tanh(jnp.dot(basis[...], cells, preferred_element_type=F32))
            offset = jnp.concatenate([flat[...]] * copies, axis=1)
            slope = jnp.concatenate([swing[...]] * copies, axis=1)
            weighted = (offset + slope * heat).astype(BF16)
            source = jnp.dot(basis_t[...], weighted, preferred_element_type=F32).astype(BF16).astype(F32)
            done = cells.astype(F32) + load[p, pl.ds(place, 1), :] * source
            for k in range(count):
                outs[k][i, p] = done[k * modes : (k + 1) * modes].astype(BF16)
        return 0

    lax.fori_loop(0, part, row, 0)


def points(pos, basis, basis_t, flat, swing, load, blocks, begin):
    count = len(blocks)
    return pl.pallas_call(
        functools.partial(points_kernel, begin=begin),
        out_shape=tuple(jax.ShapeDtypeStruct(block.shape, BF16) for block in blocks) + (TOKEN,),
        in_specs=[SMEM] + [VMEM] * (5 + count),
        out_specs=(VMEM,) * count + (SMEM,),
        compiler_params=params(),
        cost_estimate=COST,
        name="points",
    )(pos, basis, basis_t, flat, swing, load, *blocks)


def collect_kernel(pos, *refs):
    *blocks, out, token, sems = refs
    token[0], token[1] = pos[0], pos[1]
    part, planes = blocks[0].shape[0], out.shape[1]
    copies = []
    for k, block in enumerate(blocks):
        base = jnp.bitwise_xor(pos[1], k) * part
        copies.append(
            pltpu.make_async_copy(block.at[:, pl.ds(0, planes)], out.at[pl.ds(base, part)], sems.at[k])
        )
    for copy in copies:
        copy.start()
    for copy in copies:
        copy.wait()


def collect(pos, blocks):
    part, planes, modes, cols = blocks[0].shape
    count = len(blocks)
    shape = (part * count, planes // 2, modes, cols)
    return pl.pallas_call(
        collect_kernel,
        out_shape=(jax.ShapeDtypeStruct(shape, BF16), TOKEN),
        in_specs=[SMEM] + [ANY] * count,
        out_specs=(ANY, SMEM),
        scratch_shapes=[pltpu.SemaphoreType.DMA((count,))],
        compiler_params=params(),
        cost_estimate=COST,
        name="collect",
    )(pos, *blocks)


def settle_kernel(pos, turn, *refs, begin, count, chained):
    if chained:
        refs = refs[1:]
    blocks, other = refs[:count], refs[count]
    out, token, both, final, sems = refs[count + 1 :]
    token[0], token[1] = pos[0], pos[1]
    side = pos[0]
    part = blocks[0].shape[0]
    _, rows, planes, modes, cols = both.shape
    size = out.shape[2]
    group = turn.shape[1] // TILE
    incoming = [pltpu.make_async_copy(other, both.at[1], sems.at[count])]
    for k in range(count):
        base = jnp.bitwise_xor(pos[1], k) * part
        incoming.append(
            pltpu.make_async_copy(blocks[k].at[:, pl.ds(planes, planes)], both.at[0, pl.ds(base, part)], sems.at[k])
        )
    for copy in incoming:
        copy.start()
    outgoing = []
    for a in (1, 0):
        for copy in incoming[:1] if a else incoming[1:]:
            copy.wait()
        far = side if a == 0 else 1 - side
        for z in range(planes):
            to = jnp.where(far == 1, z, planes - 1 - z)
            for g in range(rows // TILE):
                block = jnp.where(far == 1, rows // TILE - 1 - g, g)
                for h in range(modes // group):
                    there = pl.ds(h * group, group)
                    x = both[a, pl.ds(g * TILE, TILE), z, there, :]
                    y = jnp.dot(turn[far], to_bf16_rows(x), preferred_element_type=F32).astype(BF16)
                    final[a, to, there, pl.ds(pl.multiple_of(block * TILE, TILE), TILE), :] = y.reshape(
                        group, TILE, cols
                    )
        start = pl.multiple_of(jnp.where(far == 1, size - rows - begin, begin), TILE)
        copy = pltpu.make_async_copy(final.at[a], out.at[:, :, pl.ds(start, rows), :], sems.at[count + 1 + a])
        copy.start()
        outgoing.append(copy)
    for copy in outgoing:
        copy.wait()


def settle(pos, turn, result, blocks, other, begin, shape):
    count = len(blocks)
    rows, planes, modes, cols = other.shape
    chained = result is not None
    return pl.pallas_call(
        functools.partial(settle_kernel, begin=begin, count=count, chained=chained),
        out_shape=(jax.ShapeDtypeStruct(shape, BF16), TOKEN),
        in_specs=[SMEM, VMEM] + [ANY] * (count + 1 + chained),
        out_specs=(ANY, SMEM),
        scratch_shapes=[
            pltpu.VMEM((2, rows, planes, modes, cols), BF16),
            pltpu.VMEM((2, planes, modes, rows, cols), BF16),
            pltpu.SemaphoreType.DMA((count + 3,)),
        ],
        input_output_aliases={2: 0} if chained else {},
        compiler_params=params(),
        cost_estimate=COST,
        name="settle",
    )(pos, turn, *([result] if chained else []), *blocks, other)


def chunk_rows(half):
    unit = half // 8
    return [unit, 2 * unit, 2 * unit, 2 * unit, unit]


ORDER = "T0 T1 T2 S0 T3 T4 P0 S1 C0 S2 P1 F0 S3 P2 S4 C1 P3 F1 C2 P4 F2 C3 F3 C4 F4".split()


def on_device(field, diffusion, joule, basis, quad_weight, base_conductivity, thermal_slope):
    planes, modes, size, cols = field.shape
    half = size // 2
    spaces, count = lax.axis_size("space"), lax.axis_size("modes")
    side = lax.axis_index("space") % 2
    me = lax.axis_index("modes")
    pos = jnp.stack([side, me]).astype(jnp.int32)

    swap = [(i, i ^ 1) for i in range(spaces)]
    ahead = [(i, i + 4 * (i % 2) - 2) for i in range(spaces)]
    ahead = [(i, j) for i, j in ahead if 0 <= j < spaces]
    back = [(j, i) for i, j in ahead]

    def across(x):
        return lax.ppermute(x, "space", swap)

    def halo(own, other):
        return lax.ppermute(own, "space", ahead), lax.ppermute(other, "space", back)

    def exchange(pieces):
        moved = [pieces[0]]
        for k in range(1, count):
            moved.append(lax.ppermute(pieces[k], "modes", [(j, j ^ k) for j in range(count)]))
        return moved

    def logical(x, length, side, sent):
        rows_back, planes_back = jnp.flip(x, 1)[:, :length], jnp.flip(x, 0)[:, :length]
        own = jnp.where(side == 1, rows_back, planes_back)
        send = jnp.where(side == 1, planes_back, rows_back).astype(sent)
        return own, send

    own_rate, send_rate = logical(diffusion, half + EDGE, side, F32)
    other_rate = across(send_rate)
    before, after = halo(own_rate[-1:], other_rate[:1])
    rate = jnp.concatenate([before, other_rate, own_rate, after], axis=0)
    rate = jnp.pad(rate, ((0, 0), (1, -(half + EDGE + 1) % 8), (0, 0)))

    lane = jnp.arange(cols)
    shift = (jnp.abs(lane[:, None] - lane[None, :]) == 1).astype(BF16)

    group = min(modes, TILE)
    at = jnp.arange(group * TILE)
    row_first = (at // group, at % group)
    mode_first = (at % TILE, at // TILE)
    same = row_first[1][:, None] == mode_first[1][None, :]
    straight = row_first[0][:, None] == mode_first[0][None, :]
    reverse = row_first[0][:, None] == TILE - 1 - mode_first[0][None, :]
    to_rows = jnp.stack([same & straight, same & reverse]).astype(BF16)
    to_modes = jnp.stack([(same & straight).T, (same & reverse).T]).astype(BF16)

    points_count = basis.shape[0]
    extra = -points_count % 32
    turned = jnp.concatenate(
        [lax.dynamic_slice_in_dim(basis, (me ^ k) * modes, modes, axis=1) for k in range(count)], axis=1
    )
    turned = jnp.pad(turned, ((0, extra), (0, 0)))
    turned_t = turned.T
    level = quad_weight * base_conductivity
    spread_out = lambda v: jnp.broadcast_to(jnp.pad(v, (0, extra))[:, None], (points_count + extra, 128))
    flat, swing = spread_out(level), spread_out(level * thermal_slope)

    rows_of = chunk_rows(half)
    begins = [sum(rows_of[:c]) for c in range(len(rows_of))]
    own, other, blocks, cells, home, theirs = {}, {}, {}, {}, {}, {}
    result = None
    for step in ORDER:
        kind, c = step[0], int(step[1:])
        begin, rows = begins[c], rows_of[c]
        if kind == "T":
            skip = EDGE if c else 0
            after = () if c else (send_rate,)
            own[c], send, pos = spread(pos, field, to_rows, after, begin, skip, rows + EDGE - skip, rows + TILE)
            other[c] = across(send)
            before, after = halo(own[c], other[c])
            blocks[c] = (before, other[c], own[c], after)
            if c == 0:
                own_load, send_load = logical(joule, half, pos[0], BF16)
                load = jnp.concatenate([across(send_load).astype(F32), own_load], axis=0)
        elif kind == "S":
            *pieces, pos = sweep(pos, rate, shift, blocks[c], blocks.get(c - 1, ()), begin, rows, count)
            cells[c] = exchange(pieces)
        elif kind == "P":
            *stepped, pos = points(pos, turned, turned_t, flat, swing, load, cells[c], begin)
            home[c] = exchange(stepped)
        elif kind == "C":
            out, pos = collect(pos, home[c])
            theirs[c] = across(out)
        else:
            result, pos = settle(pos, to_modes, result, home[c], theirs[c], begin, field.shape)
    return result


def solution(mesh):
    return jax.shard_map(
        on_device,
        mesh=mesh,
        in_specs=(
            P("space", "modes", None, None),
            P("space", None, None),
            P("space", None, None),
            P(),
            P(),
            P(),
            P(),
        ),
        out_specs=P("space", "modes", None, None),
        check_vma=False,
    )
```

```python
import functools

import jax
import jax.numpy as jnp
import numpy as np
from jax import lax
from jax.experimental import pallas as pl
from jax.experimental.pallas import tpu as pltpu
from jax.sharding import PartitionSpec as P

F32, BF16 = jnp.float32, jnp.bfloat16
ANY = pl.BlockSpec(memory_space=pl.ANY)
VMEM = pl.BlockSpec(memory_space=pltpu.VMEM)
SMEM = pl.BlockSpec(memory_space=pltpu.SMEM)
TOKEN = jax.ShapeDtypeStruct((2,), jnp.int32)
COST = pl.CostEstimate(flops=1, bytes_accessed=1, transcendentals=0)
EDGE = 2
TILE = 16


def params(mebibytes):
    return pltpu.CompilerParams(vmem_limit_bytes=mebibytes * 1024 * 1024)


def from_rows(y, group):
    if group % 16 == 0:
        return y.astype(BF16).reshape(-1, group, y.shape[1])
    return y.reshape(-1, group, y.shape[1]).astype(BF16)


def to_bf16_rows(x):
    a, m, y = x.shape
    if m % 16 == 0:
        return x.astype(BF16).reshape(a * m, y)
    return x.astype(F32).reshape(a * m, y).astype(BF16)


def spread_kernel(pos, field, turn, *refs, begin, skip):
    own, send, token, window, sems = refs[-5:]
    side = pos[0]
    token[0], token[1] = pos[0], pos[1]
    _, planes, modes, depth, cols = window.shape
    size = field.shape[2]
    rows = own.shape[0]
    group = turn.shape[1] // TILE
    copies = []
    for a in range(2):
        far = 1 - side if a == 0 else side
        start = jnp.where(far == 1, size - depth - begin, begin)
        start = pl.multiple_of(start, TILE)
        copy = pltpu.make_async_copy(
            field.at[:, :, pl.ds(start, depth), :], window.at[a], sems.at[a]
        )
        copy.start()
        copies.append(copy)
    for a, out in ((0, send), (1, own)):
        far = 1 - side if a == 0 else side
        copies[a].wait()
        for z in range(planes):
            to = jnp.where(far == 1, z, planes - 1 - z)
            for g in range(depth // TILE):
                block = jnp.where(far == 1, depth // TILE - 1 - g, g)
                low, high = max(0, skip - g * TILE), min(TILE, rows + skip - g * TILE)
                if high <= low:
                    continue
                for h in range(modes // group):
                    there = pl.ds(h * group, group)
                    x = window[a, z, there, pl.ds(pl.multiple_of(block * TILE, TILE), TILE), :]
                    y = jnp.dot(turn[far], x.reshape(group * TILE, cols), preferred_element_type=F32)
                    y = from_rows(y, group)
                    out[pl.ds(g * TILE + low - skip, high - low), to, there, :] = y[low:high]


def spread(pos, field, turn, after, begin, skip, rows, depth):
    planes, modes, _, cols = field.shape
    piece = jax.ShapeDtypeStruct((rows, planes, modes, cols), BF16)
    return pl.pallas_call(
        functools.partial(spread_kernel, begin=begin, skip=skip),
        out_shape=(piece, piece, TOKEN),
        in_specs=[SMEM, ANY, VMEM] + [ANY] * len(after),
        out_specs=(VMEM, VMEM, SMEM),
        scratch_shapes=[
            pltpu.VMEM((2, planes, modes, depth, cols), BF16),
            pltpu.SemaphoreType.DMA((2,)),
        ],
        compiler_params=params(10),
        cost_estimate=COST,
        name="spread",
    )(pos, field, turn, *after)


def sweep_kernel(pos, rate, shift, *refs, begin, count, heads):
    group = 4
    blocks, refs = refs[:group], refs[group:]
    tails, refs = refs[:heads], refs[heads:]
    outs, (token, first, edge, sems) = refs[:count], refs[count:]
    token[0], token[1] = pos[0], pos[1]
    planes, modes, cols = blocks[0].shape[1:]
    mine = 2 * planes
    part = outs[0].shape[0]
    rows = part * count
    lead = 2 * EDGE if heads else EDGE
    copies = []
    for g in range(heads):
        length = tails[g].shape[0]
        copies.append(
            pltpu.make_async_copy(
                tails[g].at[pl.ds(length - lead, lead)], edge.at[:, pl.ds(g * planes, planes)], sems.at[g]
            )
        )
    for copy in copies:
        copy.start()
    for copy in copies:
        copy.wait()
    low = planes - 1
    wide = mine + 2
    piece = min(modes, 16)

    def field(row, p, some):
        if isinstance(row, int) and row < lead:
            if heads:
                return edge[row, p, some]
            return jnp.zeros((some.size, cols), BF16)
        return blocks[p // planes][row - lead, p % planes, some]

    def beside(parts, number):
        return jnp.dot(
            to_bf16_rows(jnp.stack(parts)), shift[...], preferred_element_type=F32
        ).reshape(number, -1, modes, cols)

    def once(i, number):
        every = pl.ds(0, modes)
        aside = beside([field(i + 1 + a, low + p, every) for a in range(number) for p in range(wide)], number)
        for a in range(number):
            speeds = [rate[p, pl.ds(begin + i + a, 1), :] for p in range(wide)]
            for h in range(modes // piece):
                some = pl.ds(h * piece, piece)
                line = [field(i + 1 + a, low - 1 + p, some).astype(F32) for p in range(wide + 2)]
                for p in range(wide):
                    centre = line[p + 1]
                    around = aside[a, p, h * piece : (h + 1) * piece] + (line[p] + line[p + 2])
                    around = around + (
                        field(i + a, low + p, some).astype(F32) + field(i + 2 + a, low + p, some).astype(F32)
                    )
                    first[i + a, p, some] = centre + speeds[p] * (around - 6.0 * centre)

    for i in range(0, lead, 2):
        once(i, 2)

    def pair(j, _):
        once(lead + 2 * j, 2)
        return 0

    lax.fori_loop(0, (rows + 2 - lead) // 2, pair, 0)
    number = 2 if part % 2 == 0 else 1
    for k in range(count):
        base = jnp.bitwise_xor(pos[1], k) * part

        def again(j, _):
            i = base + number * j
            aside = beside([first[i + 1 + a, 1 + p] for a in range(number) for p in range(mine)], number)
            for a in range(number):
                speeds = [rate[p + 1, pl.ds(begin + i + a + 1, 1), :] for p in range(mine)]
                for h in range(modes // piece):
                    some = pl.ds(h * piece, piece)
                    line = [first[i + 1 + a, p, some] for p in range(wide)]
                    for p in range(mine):
                        centre = line[p + 1]
                        around = aside[a, p, h * piece : (h + 1) * piece] + (line[p] + line[p + 2])
                        around = around + (first[i + a, p + 1, some] + first[i + 2 + a, p + 1, some])
                        outs[k][number * j + a, p, some] = (
                            centre + speeds[p] * (around - 6.0 * centre)
                        ).astype(BF16)
            return 0

        lax.fori_loop(0, part // number, again, 0)


def sweep(pos, rate, shift, blocks, tails, begin, rows, count):
    _, planes, modes, cols = blocks[0].shape
    mine = 2 * planes
    piece = jax.ShapeDtypeStruct((rows // count, mine, modes, cols), BF16)
    return pl.pallas_call(
        functools.partial(sweep_kernel, begin=begin, count=count, heads=len(tails)),
        out_shape=(piece,) * count + (TOKEN,),
        in_specs=[SMEM] + [VMEM] * 6 + [ANY] * len(tails),
        out_specs=(VMEM,) * count + (SMEM,),
        scratch_shapes=[
            pltpu.VMEM((rows + 2, mine + 2, modes, cols), F32),
            pltpu.VMEM((2 * EDGE, 4 * planes, modes, cols), BF16),
            pltpu.SemaphoreType.DMA((4,)),
        ],
        compiler_params=params(22),
        cost_estimate=COST,
        name="sweep",
    )(pos, rate, shift, *blocks, *tails)


def points_kernel(pos, basis, basis_t, flat, swing, load, *refs, begin):
    *refs, token = refs
    token[0], token[1] = pos[0], pos[1]
    count = len(refs) // 2
    blocks, outs = refs[:count], refs[count:]
    part, planes, modes, cols = blocks[0].shape
    copies = cols // flat.shape[1]

    def row(i, _):
        place = begin + pos[1] * part + i
        for p in range(planes):
            if modes % 16 == 0:
                cells = jnp.concatenate([block[i, p] for block in blocks], axis=0)
            else:
                cells = jnp.concatenate([block[i, p].astype(F32) for block in blocks], axis=0).astype(BF16)
            heat = jnp.tanh(jnp.dot(basis[...], cells, preferred_element_type=F32))
            offset = jnp.concatenate([flat[...]] * copies, axis=1)
            slope = jnp.concatenate([swing[...]] * copies, axis=1)
            weighted = (offset + slope * heat).astype(BF16)
            source = jnp.dot(basis_t[...], weighted, preferred_element_type=F32).astype(BF16).astype(F32)
            done = cells.astype(F32) + load[p, pl.ds(place, 1), :] * source
            for k in range(count):
                outs[k][i, p] = done[k * modes : (k + 1) * modes].astype(BF16)
        return 0

    lax.fori_loop(0, part, row, 0)


def points(pos, basis, basis_t, flat, swing, load, blocks, begin):
    count = len(blocks)
    return pl.pallas_call(
        functools.partial(points_kernel, begin=begin),
        out_shape=tuple(jax.ShapeDtypeStruct(block.shape, BF16) for block in blocks) + (TOKEN,),
        in_specs=[SMEM] + [VMEM] * (5 + count),
        out_specs=(VMEM,) * count + (SMEM,),
        compiler_params=params(14),
        cost_estimate=COST,
        name="points",
    )(pos, basis, basis_t, flat, swing, load, *blocks)


def collect_kernel(pos, *refs):
    *blocks, out, token, sems = refs
    token[0], token[1] = pos[0], pos[1]
    part, planes = blocks[0].shape[0], out.shape[1]
    copies = []
    for k, block in enumerate(blocks):
        base = jnp.bitwise_xor(pos[1], k) * part
        copies.append(
            pltpu.make_async_copy(block.at[:, pl.ds(0, planes)], out.at[pl.ds(base, part)], sems.at[k])
        )
    for copy in copies:
        copy.start()
    for copy in copies:
        copy.wait()


def collect(pos, blocks):
    part, planes, modes, cols = blocks[0].shape
    count = len(blocks)
    shape = (part * count, planes // 2, modes, cols)
    return pl.pallas_call(
        collect_kernel,
        out_shape=(jax.ShapeDtypeStruct(shape, BF16), TOKEN),
        in_specs=[SMEM] + [ANY] * count,
        out_specs=(VMEM, SMEM),
        scratch_shapes=[pltpu.SemaphoreType.DMA((count,))],
        compiler_params=params(6),
        cost_estimate=COST,
        name="collect",
    )(pos, *blocks)


def settle_kernel(pos, turn, *refs, begin, count, chained):
    if chained:
        refs = refs[1:]
    blocks, other = refs[:count], refs[count]
    out, token, both, final, sems = refs[count + 1 :]
    token[0], token[1] = pos[0], pos[1]
    side = pos[0]
    part = blocks[0].shape[0]
    _, rows, planes, modes, cols = both.shape
    size = out.shape[2]
    group = turn.shape[1] // TILE
    incoming = [pltpu.make_async_copy(other, both.at[1], sems.at[count])]
    for k in range(count):
        base = jnp.bitwise_xor(pos[1], k) * part
        incoming.append(
            pltpu.make_async_copy(blocks[k].at[:, pl.ds(planes, planes)], both.at[0, pl.ds(base, part)], sems.at[k])
        )
    for copy in incoming:
        copy.start()
    outgoing = []
    for a in (1, 0):
        for copy in incoming[:1] if a else incoming[1:]:
            copy.wait()
        far = side if a == 0 else 1 - side
        for z in range(planes):
            to = jnp.where(far == 1, z, planes - 1 - z)
            for g in range(rows // TILE):
                block = jnp.where(far == 1, rows // TILE - 1 - g, g)
                for h in range(modes // group):
                    there = pl.ds(h * group, group)
                    x = both[a, pl.ds(g * TILE, TILE), z, there, :]
                    y = jnp.dot(turn[far], to_bf16_rows(x), preferred_element_type=F32).astype(BF16)
                    final[a, to, there, pl.ds(pl.multiple_of(block * TILE, TILE), TILE), :] = y.reshape(
                        group, TILE, cols
                    )
        start = pl.multiple_of(jnp.where(far == 1, size - rows - begin, begin), TILE)
        copy = pltpu.make_async_copy(final.at[a], out.at[:, :, pl.ds(start, rows), :], sems.at[count + 1 + a])
        copy.start()
        outgoing.append(copy)
    for copy in outgoing:
        copy.wait()


def settle(pos, turn, result, blocks, other, begin, shape):
    count = len(blocks)
    rows, planes, modes, cols = other.shape
    chained = result is not None
    return pl.pallas_call(
        functools.partial(settle_kernel, begin=begin, count=count, chained=chained),
        out_shape=(jax.ShapeDtypeStruct(shape, BF16), TOKEN),
        in_specs=[SMEM, VMEM] + [ANY] * (count + 1 + chained),
        out_specs=(ANY, SMEM),
        scratch_shapes=[
            pltpu.VMEM((2, rows, planes, modes, cols), BF16),
            pltpu.VMEM((2, planes, modes, rows, cols), BF16),
            pltpu.SemaphoreType.DMA((count + 3,)),
        ],
        input_output_aliases={2: 0} if chained else {},
        compiler_params=params(10),
        cost_estimate=COST,
        name="settle",
    )(pos, turn, *([result] if chained else []), *blocks, other)


def chunk_rows(half):
    unit = half // 8
    return [unit, 2 * unit, 2 * unit, 2 * unit, unit]


ORDER = (
    ("T", 0), ("T", 1), ("T", 2), ("S", 0), ("T", 3),
    ("T", 4), ("P", 0), ("S", 1), ("C", 0), ("S", 2),
    ("P", 1), ("F", 0), ("S", 3), ("P", 2), ("S", 4),
    ("C", 1), ("P", 3), ("F", 1), ("C", 2), ("P", 4),
    ("F", 2), ("C", 3), ("F", 3), ("C", 4), ("F", 4),
)


def turns(group):
    at = np.arange(group * TILE)
    row, mode = at // group, at % group
    same = mode[:, None] == (at // TILE)[None, :]
    straight = same & (row[:, None] == (at % TILE)[None, :])
    reverse = same & (row[:, None] == TILE - 1 - (at % TILE)[None, :])
    to_rows = np.stack([straight, reverse])
    return jnp.asarray(to_rows, BF16), jnp.asarray(to_rows.transpose(0, 2, 1), BF16)


def on_device(field, diffusion, joule, basis, quad_weight, base_conductivity, thermal_slope):
    planes, modes, size, cols = field.shape
    half = size // 2
    spaces, count = lax.axis_size("space"), lax.axis_size("modes")
    side = lax.axis_index("space") % 2
    me = lax.axis_index("modes")
    pos = jnp.stack([side, me]).astype(jnp.int32)

    swap = [(i, i ^ 1) for i in range(spaces)]
    ahead = [(i, i + 4 * (i % 2) - 2) for i in range(spaces)]
    ahead = [(i, j) for i, j in ahead if 0 <= j < spaces]
    back = [(j, i) for i, j in ahead]

    def across(x):
        return lax.ppermute(x, "space", swap)

    def halo(own, other):
        return lax.ppermute(own, "space", ahead), lax.ppermute(other, "space", back)

    def exchange(pieces):
        moved = [pieces[0]]
        for k in range(1, count):
            moved.append(lax.ppermute(pieces[k], "modes", [(j, j ^ k) for j in range(count)]))
        return moved

    def logical(x, length, side, sent):
        rows_back, planes_back = jnp.flip(x, 1)[:, :length], jnp.flip(x, 0)[:, :length]
        own = jnp.where(side == 1, rows_back, planes_back)
        send = jnp.where(side == 1, planes_back, rows_back).astype(sent)
        return own, send

    lane = np.arange(cols)
    shift = jnp.asarray(np.abs(lane[:, None] - lane[None, :]) == 1, BF16)
    to_rows, to_modes = turns(min(modes, TILE))

    points_count = basis.shape[0]
    extra = -points_count % 32
    turned = jnp.concatenate(
        [lax.dynamic_slice_in_dim(basis, (me ^ k) * modes, modes, axis=1) for k in range(count)], axis=1
    )
    turned = jnp.pad(turned, ((0, extra), (0, 0)))
    turned_t = turned.T
    level = quad_weight * base_conductivity
    spread_out = lambda v: jnp.broadcast_to(jnp.pad(v, (0, extra))[:, None], (points_count + extra, 128))
    flat, swing = spread_out(level), spread_out(level * thermal_slope)

    rows_of = chunk_rows(half)
    begins = [sum(rows_of[:c]) for c in range(len(rows_of))]
    own, other, blocks, cells, home, theirs = {}, {}, {}, {}, {}, {}
    result = None
    for kind, c in ORDER:
        begin, rows = begins[c], rows_of[c]
        if kind == "T":
            skip = EDGE if c else 0
            after = ()
            if c == 1:
                own_rate, send_rate = logical(diffusion, half + EDGE, pos[0], F32)
                own_load, send_load = logical(joule, half, pos[0], BF16)
                other_rate, other_load = across(send_rate), across(send_load)
                before, behind = halo(own_rate[-1:], other_rate[:1])
                rate = jnp.concatenate([before, other_rate, own_rate, behind], axis=0)
                rate = jnp.pad(rate, ((0, 0), (1, -(half + EDGE + 1) % 8), (0, 0)))
                load = jnp.concatenate([other_load.astype(F32), own_load], axis=0)
                after = (send_rate, send_load)
            elif c == 2:
                after = (blocks[0][0], other_load)
            own[c], send, pos = spread(pos, field, to_rows, after, begin, skip, rows + EDGE - skip, rows + TILE)
            other[c] = across(send)
            before, after = halo(own[c], other[c])
            blocks[c] = (before, other[c], own[c], after)
        elif kind == "S":
            *pieces, pos = sweep(pos, rate, shift, blocks[c], blocks.get(c - 1, ()), begin, rows, count)
            cells[c] = exchange(pieces)
        elif kind == "P":
            *stepped, pos = points(pos, turned, turned_t, flat, swing, load, cells[c], begin)
            home[c] = exchange(stepped)
        elif kind == "C":
            out, pos = collect(pos, home[c])
            theirs[c] = across(out)
        else:
            result, pos = settle(pos, to_modes, result, home[c], theirs[c], begin, field.shape)
    return result


def solution(mesh):
    return jax.shard_map(
        on_device,
        mesh=mesh,
        in_specs=(
            P("space", "modes", None, None),
            P("space", None, None),
            P("space", None, None),
            P(),
            P(),
            P(),
            P(),
        ),
        out_specs=P("space", "modes", None, None),
        check_vma=False,
    )
```

```python
import functools

import jax
import jax.numpy as jnp
import numpy as np
from jax import lax
from jax.experimental import pallas as pl
from jax.experimental.pallas import tpu as pltpu
from jax.sharding import PartitionSpec as P

F32, BF16 = jnp.float32, jnp.bfloat16
ANY = pl.BlockSpec(memory_space=pl.ANY)
VMEM = pl.BlockSpec(memory_space=pltpu.VMEM)
HBM = pl.BlockSpec(memory_space=pltpu.HBM)
SMEM = pl.BlockSpec(memory_space=pltpu.SMEM)
TOKEN = jax.ShapeDtypeStruct((2,), jnp.int32)
COST = pl.CostEstimate(flops=1, bytes_accessed=1, transcendentals=0)
EDGE = 2
TILE = 16


def params(mebibytes):
    return pltpu.CompilerParams(vmem_limit_bytes=mebibytes * 1024 * 1024)


def from_rows(y, group):
    if group % 16 == 0:
        return y.astype(BF16).reshape(-1, group, y.shape[1])
    return y.reshape(-1, group, y.shape[1]).astype(BF16)


def to_bf16_rows(x):
    a, m, y = x.shape
    if m % 16 == 0:
        return x.astype(BF16).reshape(a * m, y)
    return x.astype(F32).reshape(a * m, y).astype(BF16)


def spread_kernel(pos, field, turn, *refs, begin, skip):
    own, send, token, window, sems = refs[-5:]
    side = pos[0]
    token[0], token[1] = pos[0], pos[1]
    _, planes, modes, depth, cols = window.shape
    size = field.shape[2]
    rows = own.shape[0]
    group = turn.shape[1] // TILE
    copies = []
    for a in range(2):
        far = 1 - side if a == 0 else side
        start = jnp.where(far == 1, size - depth - begin, begin)
        start = pl.multiple_of(start, TILE)
        copy = pltpu.make_async_copy(
            field.at[:, :, pl.ds(start, depth), :], window.at[a], sems.at[a]
        )
        copy.start()
        copies.append(copy)
    for a, out in ((0, send), (1, own)):
        far = 1 - side if a == 0 else side
        copies[a].wait()
        for z in range(planes):
            to = jnp.where(far == 1, z, planes - 1 - z)
            for g in range(depth // TILE):
                block = jnp.where(far == 1, depth // TILE - 1 - g, g)
                low, high = max(0, skip - g * TILE), min(TILE, rows + skip - g * TILE)
                if high <= low:
                    continue
                for h in range(modes // group):
                    there = pl.ds(h * group, group)
                    x = window[a, z, there, pl.ds(pl.multiple_of(block * TILE, TILE), TILE), :]
                    y = jnp.dot(turn[far], x.reshape(group * TILE, cols), preferred_element_type=F32)
                    y = from_rows(y, group)
                    out[pl.ds(g * TILE + low - skip, high - low), to, there, :] = y[low:high]


def spread(pos, field, turn, after, begin, skip, rows, depth):
    planes, modes, _, cols = field.shape
    piece = jax.ShapeDtypeStruct((rows, planes, modes, cols), BF16)
    return pl.pallas_call(
        functools.partial(spread_kernel, begin=begin, skip=skip),
        out_shape=(piece, piece, TOKEN),
        in_specs=[SMEM, HBM, VMEM] + [ANY] * len(after),
        out_specs=(VMEM, VMEM, SMEM),
        scratch_shapes=[
            pltpu.VMEM((2, planes, modes, depth, cols), BF16),
            pltpu.SemaphoreType.DMA((2,)),
        ],
        compiler_params=params(10),
        cost_estimate=COST,
        name="spread",
    )(pos, field, turn, *after)


def relay_kernel(pos, *refs):
    token = refs[-1]
    token[0], token[1] = pos[0], pos[1]


def relay(pos, passed, after):
    count = len(passed)
    return pl.pallas_call(
        relay_kernel,
        out_shape=tuple(jax.ShapeDtypeStruct(x.shape, x.dtype) for x in passed) + (TOKEN,),
        in_specs=[SMEM] + [ANY] * (count + len(after)),
        out_specs=(ANY,) * count + (SMEM,),
        input_output_aliases={1 + i: i for i in range(count)},
        compiler_params=params(1),
        cost_estimate=COST,
        name="relay",
    )(pos, *passed, *after)


def sweep_kernel(pos, rate, shift, *refs, begin, heads):
    group = 4
    blocks, refs = refs[:group], refs[group:]
    tails, refs = refs[:heads], refs[heads:]
    out, token, first, edge, sems = refs
    token[0], token[1] = pos[0], pos[1]
    planes, modes, cols = blocks[0].shape[1:]
    rows, mine = out.shape[:2]
    lead = 2 * EDGE if heads else EDGE
    copies = []
    for g in range(heads):
        length = tails[g].shape[0]
        copies.append(
            pltpu.make_async_copy(
                tails[g].at[pl.ds(length - lead, lead)], edge.at[:, pl.ds(g * planes, planes)], sems.at[g]
            )
        )
    for copy in copies:
        copy.start()
    for copy in copies:
        copy.wait()
    low = planes - 1
    wide = mine + 2
    piece = min(modes, 16)

    def field(row, p, some):
        if isinstance(row, int) and row < lead:
            if heads:
                return edge[row, p, some]
            return jnp.zeros((some.size, cols), BF16)
        return blocks[p // planes][row - lead, p % planes, some]

    def beside(parts, number):
        return jnp.dot(
            to_bf16_rows(jnp.stack(parts)), shift[...], preferred_element_type=F32
        ).reshape(number, -1, modes, cols)

    def once(i, number):
        every = pl.ds(0, modes)
        aside = beside([field(i + 1 + a, low + p, every) for a in range(number) for p in range(wide)], number)
        for a in range(number):
            speeds = [rate[p, pl.ds(begin + i + a, 1), :] for p in range(wide)]
            for h in range(modes // piece):
                some = pl.ds(h * piece, piece)
                line = [field(i + 1 + a, low - 1 + p, some).astype(F32) for p in range(wide + 2)]
                for p in range(wide):
                    centre = line[p + 1]
                    around = aside[a, p, h * piece : (h + 1) * piece] + (line[p] + line[p + 2])
                    around = around + (
                        field(i + a, low + p, some).astype(F32) + field(i + 2 + a, low + p, some).astype(F32)
                    )
                    first[i + a, p, some] = centre + speeds[p] * (around - 6.0 * centre)

    for i in range(0, lead, 2):
        once(i, 2)

    def pair(j, _):
        once(lead + 2 * j, 2)
        return 0

    lax.fori_loop(0, (rows + 2 - lead) // 2, pair, 0)

    def again(j, _):
        i = 2 * j
        aside = beside([first[i + 1 + a, 1 + p] for a in range(2) for p in range(mine)], 2)
        for a in range(2):
            speeds = [rate[p + 1, pl.ds(begin + i + a + 1, 1), :] for p in range(mine)]
            for h in range(modes // piece):
                some = pl.ds(h * piece, piece)
                line = [first[i + 1 + a, p, some] for p in range(wide)]
                for p in range(mine):
                    centre = line[p + 1]
                    around = aside[a, p, h * piece : (h + 1) * piece] + (line[p] + line[p + 2])
                    around = around + (first[i + a, p + 1, some] + first[i + 2 + a, p + 1, some])
                    out[i + a, p, some] = (centre + speeds[p] * (around - 6.0 * centre)).astype(BF16)
        return 0

    lax.fori_loop(0, rows // 2, again, 0)


def sweep(pos, rate, shift, blocks, tails, begin, rows):
    _, planes, modes, cols = blocks[0].shape
    mine = 2 * planes
    return pl.pallas_call(
        functools.partial(sweep_kernel, begin=begin, heads=len(tails)),
        out_shape=(jax.ShapeDtypeStruct((rows, mine, modes, cols), BF16), TOKEN),
        in_specs=[SMEM] + [VMEM] * 6 + [ANY] * len(tails),
        out_specs=(VMEM, SMEM),
        scratch_shapes=[
            pltpu.VMEM((rows + 2, mine + 2, modes, cols), F32),
            pltpu.VMEM((2 * EDGE, 4 * planes, modes, cols), BF16),
            pltpu.SemaphoreType.DMA((4,)),
        ],
        compiler_params=params(22),
        cost_estimate=COST,
        name="sweep",
    )(pos, rate, shift, *blocks, *tails)


def points_kernel(pos, basis, basis_t, flat, swing, load, field, theirs, mine, token, *, begin):
    token[0], token[1] = pos[0], pos[1]
    rows, planes, modes, cols = field.shape
    count = basis.shape[1] // modes
    part = rows // count
    copies = cols // flat.shape[1]

    def row(i, _):
        place = begin + pos[1] * part + i
        for p in range(planes):
            cells = [field[k * part + i, p] for k in range(count)]
            cells = to_bf16_rows(jnp.stack(cells))
            heat = jnp.tanh(jnp.dot(basis[...], cells, preferred_element_type=F32))
            offset = jnp.concatenate([flat[...]] * copies, axis=1)
            slope = jnp.concatenate([swing[...]] * copies, axis=1)
            weighted = (offset + slope * heat).astype(BF16)
            source = jnp.dot(basis_t[...], weighted, preferred_element_type=F32).astype(BF16).astype(F32)
            done = cells.astype(F32) + load[p, pl.ds(place, 1), :] * source
            half = planes // 2
            for k in range(count):
                out = theirs if p < half else mine
                out[k * part + i, p % half] = done[k * modes : (k + 1) * modes].astype(BF16)
        return 0

    lax.fori_loop(0, part, row, 0)


def points(pos, basis, basis_t, flat, swing, load, field, begin):
    rows, planes, modes, cols = field.shape
    piece = jax.ShapeDtypeStruct((rows, planes // 2, modes, cols), BF16)
    return pl.pallas_call(
        functools.partial(points_kernel, begin=begin),
        out_shape=(piece, piece, TOKEN),
        in_specs=[SMEM] + [VMEM] * 6,
        out_specs=(VMEM, VMEM, SMEM),
        compiler_params=params(14),
        cost_estimate=COST,
        name="points",
    )(pos, basis, basis_t, flat, swing, load, field)


def settle_kernel(pos, turn, *refs, begin):
    mine, theirs, out, token, final, sems = refs[-6:]
    token[0], token[1] = pos[0], pos[1]
    side = pos[0]
    rows, planes, modes, cols = mine.shape
    size = out.shape[2]
    group = turn.shape[1] // TILE
    copies = []
    for a, source in ((0, mine), (1, theirs)):
        far = side if a == 0 else 1 - side
        for z in range(planes):
            to = jnp.where(far == 1, z, planes - 1 - z)
            for g in range(rows // TILE):
                block = jnp.where(far == 1, rows // TILE - 1 - g, g)
                for h in range(modes // group):
                    there = pl.ds(h * group, group)
                    x = source[pl.ds(g * TILE, TILE), z, there, :]
                    y = jnp.dot(turn[far], to_bf16_rows(x), preferred_element_type=F32).astype(BF16)
                    final[a, to, there, pl.ds(pl.multiple_of(block * TILE, TILE), TILE), :] = y.reshape(
                        group, TILE, cols
                    )
        start = pl.multiple_of(jnp.where(far == 1, size - rows - begin, begin), TILE)
        copy = pltpu.make_async_copy(final.at[a], out.at[:, :, pl.ds(start, rows), :], sems.at[a])
        copy.start()
        copies.append(copy)
    for copy in copies:
        copy.wait()


def settle(pos, turn, result, mine, theirs, begin, shape):
    rows, planes, modes, cols = mine.shape
    chained = result is not None
    return pl.pallas_call(
        functools.partial(settle_kernel, begin=begin),
        out_shape=(jax.ShapeDtypeStruct(shape, BF16), TOKEN),
        in_specs=[SMEM, VMEM] + [HBM] * chained + [VMEM, VMEM],
        out_specs=(HBM, SMEM),
        scratch_shapes=[
            pltpu.VMEM((2, planes, modes, rows, cols), BF16),
            pltpu.SemaphoreType.DMA((2,)),
        ],
        input_output_aliases={2: 0} if chained else {},
        compiler_params=params(10),
        cost_estimate=COST,
        name="settle",
    )(pos, turn, *([result] if chained else []), mine, theirs)


def chunk_rows(half):
    unit = half // 8
    return [unit, 2 * unit, 2 * unit, 2 * unit, unit]


def pipeline(chunks):
    stage = {"T": 0, "R": 1, "S": 2, "P": 3, "C": 4, "F": 5}
    for iteration in range(chunks + 5):
        for kind in "SPTRCF":
            c = iteration - stage[kind]
            if 0 <= c < chunks:
                yield kind, c


def turns(group):
    at = np.arange(group * TILE)
    row, mode = at // group, at % group
    same = mode[:, None] == (at // TILE)[None, :]
    straight = same & (row[:, None] == (at % TILE)[None, :])
    reverse = same & (row[:, None] == TILE - 1 - (at % TILE)[None, :])
    to_rows = np.stack([straight, reverse])
    return jnp.asarray(to_rows, BF16), jnp.asarray(to_rows.transpose(0, 2, 1), BF16)


def on_device(field, diffusion, joule, basis, quad_weight, base_conductivity, thermal_slope):
    planes, modes, size, cols = field.shape
    half = size // 2
    spaces = lax.axis_size("space")
    side = lax.axis_index("space") % 2
    me = lax.axis_index("modes")
    pos = jnp.stack([side, me]).astype(jnp.int32)

    swap = [(i, i ^ 1) for i in range(spaces)]
    ahead = [(i, i + 4 * (i % 2) - 2) for i in range(spaces)]
    ahead = [(i, j) for i, j in ahead if 0 <= j < spaces]
    back = [(j, i) for i, j in ahead]

    def across(x):
        return lax.ppermute(x, "space", swap)

    def ahead_of(x):
        return lax.ppermute(x, "space", ahead)

    def behind_of(x):
        return lax.ppermute(x, "space", back)

    def exchange(x):
        return lax.all_to_all(x, "modes", split_axis=0, concat_axis=0, tiled=True)

    def logical(x, length, side, sent):
        rows_back, planes_back = jnp.flip(x, 1)[:, :length], jnp.flip(x, 0)[:, :length]
        own = jnp.where(side == 1, rows_back, planes_back)
        send = jnp.where(side == 1, planes_back, rows_back).astype(sent)
        return own, send

    lane = np.arange(cols)
    shift = jnp.asarray(np.abs(lane[:, None] - lane[None, :]) == 1, BF16)
    to_rows, to_modes = turns(min(modes, TILE))

    points_count = basis.shape[0]
    extra = -points_count % 32
    basis = jnp.pad(basis, ((0, extra), (0, 0)))
    level = quad_weight * base_conductivity
    spread_out = lambda v: jnp.broadcast_to(jnp.pad(v, (0, extra))[:, None], (points_count + extra, 128))
    flat, swing = spread_out(level), spread_out(level * thermal_slope)

    rows_of = chunk_rows(half)
    begins = [sum(rows_of[:c]) for c in range(len(rows_of))]
    own, other, before, blocks, cells, home, theirs = {}, {}, {}, {}, {}, {}, {}
    result = None
    for kind, c in pipeline(len(rows_of)):
        begin, rows = begins[c], rows_of[c]
        if kind == "T":
            skip = EDGE if c else 0
            after = ()
            if c == 1:
                own_rate, send_rate = logical(diffusion, half + EDGE, pos[0], F32)
                own_load, send_load = logical(joule, half, pos[0], BF16)
                other_rate, other_load = across(send_rate), across(send_load)
                after = (send_rate, send_load)
            own[c], send, pos = spread(pos, field, to_rows, after, begin, skip, rows + EDGE - skip, rows + TILE)
            other[c] = across(send)
            before[c] = ahead_of(own[c])
        elif kind == "R":
            if c == 0:
                other[c], other_rate, other_load, pos = relay(pos, (other[c], other_rate, other_load), (before[c],))
                edges = ahead_of(own_rate[-1:]), behind_of(other_rate[:1])
                rate = jnp.concatenate([edges[0], other_rate, own_rate, edges[1]], axis=0)
                rate = jnp.pad(rate, ((0, 0), (1, -(half + EDGE + 1) % 8), (0, 0)))
                load = jnp.concatenate([other_load.astype(F32), own_load], axis=0)
            else:
                other[c], pos = relay(pos, (other[c],), (before[c],))
            blocks[c] = (before[c], other[c], own[c], behind_of(other[c]))
        elif kind == "S":
            settled, pos = sweep(pos, rate, shift, blocks[c], blocks.get(c - 1, ()), begin, rows)
            cells[c] = exchange(settled)
        elif kind == "P":
            away, near, pos = points(pos, basis, basis.T, flat, swing, load, cells[c], begin)
            theirs[c], home[c] = exchange(away), exchange(near)
        elif kind == "C":
            away, pos = relay(pos, (theirs[c],), ())
            theirs[c] = across(away)
        else:
            result, pos = settle(pos, to_modes, result, home[c], theirs[c], begin, field.shape)
    return result


def solution(mesh):
    return jax.shard_map(
        on_device,
        mesh=mesh,
        in_specs=(
            P("space", "modes", None, None),
            P("space", None, None),
            P("space", None, None),
            P(),
            P(),
            P(),
            P(),
        ),
        out_specs=P("space", "modes", None, None),
        check_vma=False,
    )
```

```python
import functools

import jax
import jax.numpy as jnp
import numpy as np
from jax import lax
from jax.experimental import pallas as pl
from jax.experimental.pallas import tpu as pltpu
from jax.sharding import PartitionSpec as P

F32, BF16 = jnp.float32, jnp.bfloat16
ANY = pl.BlockSpec(memory_space=pl.ANY)
VMEM = pl.BlockSpec(memory_space=pltpu.VMEM)
HBM = pl.BlockSpec(memory_space=pltpu.HBM)
SMEM = pl.BlockSpec(memory_space=pltpu.SMEM)
TOKEN = jax.ShapeDtypeStruct((2,), jnp.int32)
COST = pl.CostEstimate(flops=1, bytes_accessed=1, transcendentals=0)
EDGE = 2
TILE = 16


def params(mebibytes):
    return pltpu.CompilerParams(vmem_limit_bytes=mebibytes * 1024 * 1024)


def from_rows(y, group):
    if group % 16 == 0:
        return y.astype(BF16).reshape(-1, group, y.shape[1])
    return y.reshape(-1, group, y.shape[1]).astype(BF16)


def to_bf16_rows(x):
    a, m, y = x.shape
    if m % 16 == 0:
        return x.astype(BF16).reshape(a * m, y)
    return x.astype(F32).reshape(a * m, y).astype(BF16)


def spread_kernel(pos, field, turn, *refs, begin, skip):
    own, send, token, window, sems = refs[-5:]
    side = pos[0]
    token[0], token[1] = pos[0], pos[1]
    _, planes, modes, depth, cols = window.shape
    size = field.shape[2]
    rows = own.shape[0]
    group = turn.shape[1] // TILE
    copies = []
    for a in range(2):
        far = 1 - side if a == 0 else side
        start = jnp.where(far == 1, size - depth - begin, begin)
        start = pl.multiple_of(start, TILE)
        copy = pltpu.make_async_copy(
            field.at[:, :, pl.ds(start, depth), :], window.at[a], sems.at[a]
        )
        copy.start()
        copies.append(copy)
    for a, out in ((0, send), (1, own)):
        far = 1 - side if a == 0 else side
        copies[a].wait()
        for z in range(planes):
            to = jnp.where(far == 1, z, planes - 1 - z)
            for g in range(depth // TILE):
                block = jnp.where(far == 1, depth // TILE - 1 - g, g)
                low, high = max(0, skip - g * TILE), min(TILE, rows + skip - g * TILE)
                if high <= low:
                    continue
                for h in range(modes // group):
                    there = pl.ds(h * group, group)
                    x = window[a, z, there, pl.ds(pl.multiple_of(block * TILE, TILE), TILE), :]
                    y = jnp.dot(turn[far], x.reshape(group * TILE, cols), preferred_element_type=F32)
                    y = from_rows(y, group)
                    out[pl.ds(g * TILE + low - skip, high - low), to, there, :] = y[low:high]


def spread(pos, field, turn, after, begin, skip, rows, depth):
    planes, modes, _, cols = field.shape
    piece = jax.ShapeDtypeStruct((rows, planes, modes, cols), BF16)
    return pl.pallas_call(
        functools.partial(spread_kernel, begin=begin, skip=skip),
        out_shape=(piece, piece, TOKEN),
        in_specs=[SMEM, HBM, VMEM] + [ANY] * len(after),
        out_specs=(VMEM, VMEM, SMEM),
        scratch_shapes=[
            pltpu.VMEM((2, planes, modes, depth, cols), BF16),
            pltpu.SemaphoreType.DMA((2,)),
        ],
        compiler_params=params(10),
        cost_estimate=COST,
        name="spread",
    )(pos, field, turn, *after)


def take_kernel(pos, both, *refs):
    out, token, sem = refs[-3:]
    token[0], token[1] = pos[0], pos[1]
    copy = pltpu.make_async_copy(both.at[1 - pos[0]], out, sem)
    copy.start()
    copy.wait()


def take(pos, both, after):
    return pl.pallas_call(
        take_kernel,
        out_shape=(jax.ShapeDtypeStruct(both.shape[1:], both.dtype), TOKEN),
        in_specs=[SMEM, HBM] + [ANY] * len(after),
        out_specs=(VMEM, SMEM),
        scratch_shapes=[pltpu.SemaphoreType.DMA],
        compiler_params=params(4),
        cost_estimate=COST,
        name="take",
    )(pos, both, *after)


def sweep_kernel(pos, rate, shift, *refs, begin, count, heads):
    group = 4
    blocks, refs = refs[:group], refs[group:]
    tails, refs = refs[:heads], refs[heads:]
    outs, (token, first, edge, sems) = refs[:count], refs[count:]
    token[0], token[1] = pos[0], pos[1]
    planes, modes, cols = blocks[0].shape[1:]
    mine = 2 * planes
    part = outs[0].shape[0]
    rows = part * count
    lead = 2 * EDGE if heads else EDGE
    copies = []
    for g in range(heads):
        length = tails[g].shape[0]
        copies.append(
            pltpu.make_async_copy(
                tails[g].at[pl.ds(length - lead, lead)], edge.at[:, pl.ds(g * planes, planes)], sems.at[g]
            )
        )
    for copy in copies:
        copy.start()
    for copy in copies:
        copy.wait()
    low = planes - 1
    wide = mine + 2
    piece = min(modes, 16)

    def field(row, p, some):
        if isinstance(row, int) and row < lead:
            if heads:
                return edge[row, p, some]
            return jnp.zeros((some.size, cols), BF16)
        return blocks[p // planes][row - lead, p % planes, some]

    def beside(parts, number):
        return jnp.dot(
            to_bf16_rows(jnp.stack(parts)), shift[...], preferred_element_type=F32
        ).reshape(number, -1, modes, cols)

    def once(i, number):
        every = pl.ds(0, modes)
        aside = beside([field(i + 1 + a, low + p, every) for a in range(number) for p in range(wide)], number)
        for a in range(number):
            speeds = [rate[p, pl.ds(begin + i + a, 1), :] for p in range(wide)]
            for h in range(modes // piece):
                some = pl.ds(h * piece, piece)
                line = [field(i + 1 + a, low - 1 + p, some).astype(F32) for p in range(wide + 2)]
                for p in range(wide):
                    centre = line[p + 1]
                    around = aside[a, p, h * piece : (h + 1) * piece] + (line[p] + line[p + 2])
                    around = around + (
                        field(i + a, low + p, some).astype(F32) + field(i + 2 + a, low + p, some).astype(F32)
                    )
                    first[i + a, p, some] = centre + speeds[p] * (around - 6.0 * centre)

    for i in range(0, lead, 2):
        once(i, 2)

    def pair(j, _):
        once(lead + 2 * j, 2)
        return 0

    lax.fori_loop(0, (rows + 2 - lead) // 2, pair, 0)
    number = 2 if part % 2 == 0 else 1
    for k in range(count):
        base = jnp.bitwise_xor(pos[1], k) * part

        def again(j, _):
            i = base + number * j
            aside = beside([first[i + 1 + a, 1 + p] for a in range(number) for p in range(mine)], number)
            for a in range(number):
                speeds = [rate[p + 1, pl.ds(begin + i + a + 1, 1), :] for p in range(mine)]
                for h in range(modes // piece):
                    some = pl.ds(h * piece, piece)
                    line = [first[i + 1 + a, p, some] for p in range(wide)]
                    for p in range(mine):
                        centre = line[p + 1]
                        around = aside[a, p, h * piece : (h + 1) * piece] + (line[p] + line[p + 2])
                        around = around + (first[i + a, p + 1, some] + first[i + 2 + a, p + 1, some])
                        outs[k][number * j + a, p, some] = (
                            centre + speeds[p] * (around - 6.0 * centre)
                        ).astype(BF16)
            return 0

        lax.fori_loop(0, part // number, again, 0)


def sweep(pos, rate, shift, blocks, tails, begin, rows, count):
    _, planes, modes, cols = blocks[0].shape
    mine = 2 * planes
    piece = jax.ShapeDtypeStruct((rows // count, mine, modes, cols), BF16)
    return pl.pallas_call(
        functools.partial(sweep_kernel, begin=begin, count=count, heads=len(tails)),
        out_shape=(piece,) * count + (TOKEN,),
        in_specs=[SMEM] + [VMEM] * 6 + [ANY] * len(tails),
        out_specs=(VMEM,) * count + (SMEM,),
        scratch_shapes=[
            pltpu.VMEM((rows + 2, mine + 2, modes, cols), F32),
            pltpu.VMEM((2 * EDGE, 4 * planes, modes, cols), BF16),
            pltpu.SemaphoreType.DMA((4,)),
        ],
        compiler_params=params(22),
        cost_estimate=COST,
        name="sweep",
    )(pos, rate, shift, *blocks, *tails)


def points_kernel(pos, basis, basis_t, flat, swing, load, *refs, begin):
    *refs, token = refs
    token[0], token[1] = pos[0], pos[1]
    count = len(refs) // 2
    blocks, outs = refs[:count], refs[count:]
    part, planes, modes, cols = blocks[0].shape
    copies = cols // flat.shape[1]

    def row(i, _):
        place = begin + pos[1] * part + i
        for p in range(planes):
            if modes % 16 == 0:
                cells = jnp.concatenate([block[i, p] for block in blocks], axis=0)
            else:
                cells = jnp.concatenate([block[i, p].astype(F32) for block in blocks], axis=0).astype(BF16)
            heat = jnp.tanh(jnp.dot(basis[...], cells, preferred_element_type=F32))
            offset = jnp.concatenate([flat[...]] * copies, axis=1)
            slope = jnp.concatenate([swing[...]] * copies, axis=1)
            weighted = (offset + slope * heat).astype(BF16)
            source = jnp.dot(basis_t[...], weighted, preferred_element_type=F32).astype(BF16).astype(F32)
            done = cells.astype(F32) + load[p, pl.ds(place, 1), :] * source
            for k in range(count):
                outs[k][i, p] = done[k * modes : (k + 1) * modes].astype(BF16)
        return 0

    lax.fori_loop(0, part, row, 0)


def points(pos, basis, basis_t, flat, swing, load, blocks, begin):
    count = len(blocks)
    return pl.pallas_call(
        functools.partial(points_kernel, begin=begin),
        out_shape=tuple(jax.ShapeDtypeStruct(block.shape, BF16) for block in blocks) + (TOKEN,),
        in_specs=[SMEM] + [VMEM] * (5 + count),
        out_specs=(VMEM,) * count + (SMEM,),
        compiler_params=params(14),
        cost_estimate=COST,
        name="points",
    )(pos, basis, basis_t, flat, swing, load, *blocks)


def collect_kernel(pos, *refs):
    *blocks, out, token, sems = refs
    token[0], token[1] = pos[0], pos[1]
    part, planes = blocks[0].shape[0], out.shape[1]
    copies = []
    for k, block in enumerate(blocks):
        base = jnp.bitwise_xor(pos[1], k) * part
        copies.append(
            pltpu.make_async_copy(block.at[:, pl.ds(0, planes)], out.at[pl.ds(base, part)], sems.at[k])
        )
    for copy in copies:
        copy.start()
    for copy in copies:
        copy.wait()


def collect(pos, blocks):
    part, planes, modes, cols = blocks[0].shape
    count = len(blocks)
    shape = (part * count, planes // 2, modes, cols)
    return pl.pallas_call(
        collect_kernel,
        out_shape=(jax.ShapeDtypeStruct(shape, BF16), TOKEN),
        in_specs=[SMEM] + [ANY] * count,
        out_specs=(VMEM, SMEM),
        scratch_shapes=[pltpu.SemaphoreType.DMA((count,))],
        compiler_params=params(6),
        cost_estimate=COST,
        name="collect",
    )(pos, *blocks)


def settle_kernel(pos, turn, *refs, begin, count, chained):
    if chained:
        refs = refs[1:]
    blocks, other = refs[:count], refs[count]
    out, token, both, final, sems = refs[count + 1 :]
    token[0], token[1] = pos[0], pos[1]
    side = pos[0]
    part = blocks[0].shape[0]
    _, rows, planes, modes, cols = both.shape
    size = out.shape[2]
    group = turn.shape[1] // TILE
    incoming = [pltpu.make_async_copy(other.at[1 - side], both.at[1], sems.at[count])]
    for k in range(count):
        base = jnp.bitwise_xor(pos[1], k) * part
        incoming.append(
            pltpu.make_async_copy(blocks[k].at[:, pl.ds(planes, planes)], both.at[0, pl.ds(base, part)], sems.at[k])
        )
    for copy in incoming:
        copy.start()
    outgoing = []
    for a in (1, 0):
        for copy in incoming[:1] if a else incoming[1:]:
            copy.wait()
        far = side if a == 0 else 1 - side
        for z in range(planes):
            to = jnp.where(far == 1, z, planes - 1 - z)
            for g in range(rows // TILE):
                block = jnp.where(far == 1, rows // TILE - 1 - g, g)
                for h in range(modes // group):
                    there = pl.ds(h * group, group)
                    x = both[a, pl.ds(g * TILE, TILE), z, there, :]
                    y = jnp.dot(turn[far], to_bf16_rows(x), preferred_element_type=F32).astype(BF16)
                    final[a, to, there, pl.ds(pl.multiple_of(block * TILE, TILE), TILE), :] = y.reshape(
                        group, TILE, cols
                    )
        start = pl.multiple_of(jnp.where(far == 1, size - rows - begin, begin), TILE)
        copy = pltpu.make_async_copy(final.at[a], out.at[:, :, pl.ds(start, rows), :], sems.at[count + 1 + a])
        copy.start()
        outgoing.append(copy)
    for copy in outgoing:
        copy.wait()


def settle(pos, turn, result, blocks, other, begin, shape):
    count = len(blocks)
    rows, planes, modes, cols = other.shape[1:]
    chained = result is not None
    return pl.pallas_call(
        functools.partial(settle_kernel, begin=begin, count=count, chained=chained),
        out_shape=(jax.ShapeDtypeStruct(shape, BF16), TOKEN),
        in_specs=[SMEM, VMEM] + [HBM] * chained + [ANY] * count + [HBM],
        out_specs=(HBM, SMEM),
        scratch_shapes=[
            pltpu.VMEM((2, rows, planes, modes, cols), BF16),
            pltpu.VMEM((2, planes, modes, rows, cols), BF16),
            pltpu.SemaphoreType.DMA((count + 3,)),
        ],
        input_output_aliases={2: 0} if chained else {},
        compiler_params=params(10),
        cost_estimate=COST,
        name="settle",
    )(pos, turn, *([result] if chained else []), *blocks, other)


def chunk_rows(half):
    unit = half // 8
    return [unit, 2 * unit, 2 * unit, 2 * unit, unit]


def pipeline(chunks):
    stage = {"T": 0, "R": 1, "S": 2, "P": 3, "C": 4, "F": 5}
    for iteration in range(chunks + 5):
        for kind in "SPTRCF":
            c = iteration - stage[kind]
            if 0 <= c < chunks:
                yield kind, c


def turns(group):
    at = np.arange(group * TILE)
    row, mode = at // group, at % group
    same = mode[:, None] == (at // TILE)[None, :]
    straight = same & (row[:, None] == (at % TILE)[None, :])
    reverse = same & (row[:, None] == TILE - 1 - (at % TILE)[None, :])
    to_rows = np.stack([straight, reverse])
    return jnp.asarray(to_rows, BF16), jnp.asarray(to_rows.transpose(0, 2, 1), BF16)


def on_device(field, diffusion, joule, basis, quad_weight, base_conductivity, thermal_slope):
    planes, modes, size, cols = field.shape
    half = size // 2
    spaces, count = lax.axis_size("space"), lax.axis_size("modes")
    side = lax.axis_index("space") % 2
    me = lax.axis_index("modes")
    pos = jnp.stack([side, me]).astype(jnp.int32)

    swap = [(i, i ^ 1) for i in range(spaces)]
    ahead = [(i, i + 4 * (i % 2) - 2) for i in range(spaces)]
    ahead = [(i, j) for i, j in ahead if 0 <= j < spaces]
    back = [(j, i) for i, j in ahead]

    def across(x):
        return lax.ppermute(x, "space", swap)

    pairs = [[i, i + 1] for i in range(0, spaces, 2)]

    def both_of(x):
        return lax.all_gather(x, "space", axis_index_groups=pairs)

    def ahead_of(x):
        return lax.ppermute(x, "space", ahead)

    def behind_of(x):
        return lax.ppermute(x, "space", back)

    def exchange(pieces):
        moved = [pieces[0]]
        for k in range(1, count):
            moved.append(lax.ppermute(pieces[k], "modes", [(j, j ^ k) for j in range(count)]))
        return moved

    def logical(x, length, side, sent):
        rows_back, planes_back = jnp.flip(x, 1)[:, :length], jnp.flip(x, 0)[:, :length]
        own = jnp.where(side == 1, rows_back, planes_back)
        send = jnp.where(side == 1, planes_back, rows_back).astype(sent)
        return own, send

    lane = np.arange(cols)
    shift = jnp.asarray(np.abs(lane[:, None] - lane[None, :]) == 1, BF16)
    to_rows, to_modes = turns(min(modes, TILE))

    points_count = basis.shape[0]
    extra = -points_count % 32
    turned = jnp.concatenate(
        [lax.dynamic_slice_in_dim(basis, (me ^ k) * modes, modes, axis=1) for k in range(count)], axis=1
    )
    turned = jnp.pad(turned, ((0, extra), (0, 0)))
    turned_t = turned.T
    level = quad_weight * base_conductivity
    spread_out = lambda v: jnp.broadcast_to(jnp.pad(v, (0, extra))[:, None], (points_count + extra, 128))
    flat, swing = spread_out(level), spread_out(level * thermal_slope)

    rows_of = chunk_rows(half)
    begins = [sum(rows_of[:c]) for c in range(len(rows_of))]
    own, other, before, blocks, cells, home, theirs = {}, {}, {}, {}, {}, {}, {}
    result = None
    for kind, c in pipeline(len(rows_of)):
        begin, rows = begins[c], rows_of[c]
        if kind == "T":
            skip = EDGE if c else 0
            after = ()
            if c == 1:
                own_rate, send_rate = logical(diffusion, half + EDGE, pos[0], F32)
                own_load, send_load = logical(joule, half, pos[0], BF16)
                other_rate, other_load = across(send_rate), across(send_load)
                after = (send_rate, send_load)
            own[c], send, pos = spread(pos, field, to_rows, after, begin, skip, rows + EDGE - skip, rows + TILE)
            other[c] = both_of(send)
            before[c] = ahead_of(own[c])
        elif kind == "R":
            after = (before[c],)
            if c == 0:
                after = (before[c], other_rate, other_load)
                edges = ahead_of(own_rate[-1:]), behind_of(other_rate[:1])
                rate = jnp.concatenate([edges[0], other_rate, own_rate, edges[1]], axis=0)
                rate = jnp.pad(rate, ((0, 0), (1, -(half + EDGE + 1) % 8), (0, 0)))
                load = jnp.concatenate([other_load.astype(F32), own_load], axis=0)
            other[c], pos = take(pos, other[c], after)
            blocks[c] = (before[c], other[c], own[c], behind_of(other[c]))
        elif kind == "S":
            *pieces, pos = sweep(pos, rate, shift, blocks[c], blocks.get(c - 1, ()), begin, rows, count)
            cells[c] = exchange(pieces)
        elif kind == "P":
            *stepped, pos = points(pos, turned, turned_t, flat, swing, load, cells[c], begin)
            home[c] = exchange(stepped)
        elif kind == "C":
            out, pos = collect(pos, home[c])
            theirs[c] = both_of(out)
        else:
            result, pos = settle(pos, to_modes, result, home[c], theirs[c], begin, field.shape)
    return result


def solution(mesh):
    return jax.shard_map(
        on_device,
        mesh=mesh,
        in_specs=(
            P("space", "modes", None, None),
            P("space", None, None),
            P("space", None, None),
            P(),
            P(),
            P(),
            P(),
        ),
        out_specs=P("space", "modes", None, None),
        check_vma=False,
    )
```

```python
import functools

import jax
import jax.numpy as jnp
import numpy as np
from jax import lax
from jax.experimental import pallas as pl
from jax.experimental.pallas import tpu as pltpu
from jax.sharding import PartitionSpec as P

F32, BF16 = jnp.float32, jnp.bfloat16
ANY = pl.BlockSpec(memory_space=pl.ANY)
VMEM = pl.BlockSpec(memory_space=pltpu.VMEM)
HBM = pl.BlockSpec(memory_space=pltpu.HBM)
SMEM = pl.BlockSpec(memory_space=pltpu.SMEM)
TOKEN = jax.ShapeDtypeStruct((2,), jnp.int32)
COST = pl.CostEstimate(flops=1, bytes_accessed=1, transcendentals=0)
EDGE = 2
TILE = 16


def params(mebibytes):
    return pltpu.CompilerParams(vmem_limit_bytes=mebibytes * 1024 * 1024)


def from_rows(y, group):
    if group % 16 == 0:
        return y.astype(BF16).reshape(-1, group, y.shape[1])
    return y.reshape(-1, group, y.shape[1]).astype(BF16)


def to_bf16_rows(x):
    a, m, y = x.shape
    if m % 16 == 0:
        return x.astype(BF16).reshape(a * m, y)
    return x.astype(F32).reshape(a * m, y).astype(BF16)


def spread_kernel(pos, field, turn, *refs, begin, skip):
    own, send, token, window, sems = refs[-5:]
    side = pos[0]
    token[0], token[1] = pos[0], pos[1]
    _, planes, modes, depth, cols = window.shape
    size = field.shape[2]
    rows = own.shape[0]
    group = turn.shape[1] // TILE
    copies = []
    for a in range(2):
        far = 1 - side if a == 0 else side
        start = jnp.where(far == 1, size - depth - begin, begin)
        start = pl.multiple_of(start, TILE)
        copy = pltpu.make_async_copy(
            field.at[:, :, pl.ds(start, depth), :], window.at[a], sems.at[a]
        )
        copy.start()
        copies.append(copy)
    for a, out in ((0, send), (1, own)):
        far = 1 - side if a == 0 else side
        copies[a].wait()
        for z in range(planes):
            to = jnp.where(far == 1, z, planes - 1 - z)
            for g in range(depth // TILE):
                block = jnp.where(far == 1, depth // TILE - 1 - g, g)
                low, high = max(0, skip - g * TILE), min(TILE, rows + skip - g * TILE)
                if high <= low:
                    continue
                for h in range(modes // group):
                    there = pl.ds(h * group, group)
                    x = window[a, z, there, pl.ds(pl.multiple_of(block * TILE, TILE), TILE), :]
                    y = jnp.dot(turn[far], x.reshape(group * TILE, cols), preferred_element_type=F32)
                    y = from_rows(y, group)
                    out[pl.ds(g * TILE + low - skip, high - low), to, there, :] = y[low:high]


def spread(pos, field, turn, after, begin, skip, rows, depth):
    planes, modes, _, cols = field.shape
    piece = jax.ShapeDtypeStruct((rows, planes, modes, cols), BF16)
    return pl.pallas_call(
        functools.partial(spread_kernel, begin=begin, skip=skip),
        out_shape=(piece, piece, TOKEN),
        in_specs=[SMEM, HBM, VMEM] + [ANY] * len(after),
        out_specs=(VMEM, VMEM, SMEM),
        scratch_shapes=[
            pltpu.VMEM((2, planes, modes, depth, cols), BF16),
            pltpu.SemaphoreType.DMA((2,)),
        ],
        compiler_params=params(10),
        cost_estimate=COST,
        name="spread",
    )(pos, field, turn, *after)


def relay_kernel(pos, *refs):
    token = refs[-1]
    token[0], token[1] = pos[0], pos[1]


def relay(pos, passed, after):
    count = len(passed)
    return pl.pallas_call(
        relay_kernel,
        out_shape=tuple(jax.ShapeDtypeStruct(x.shape, x.dtype) for x in passed) + (TOKEN,),
        in_specs=[SMEM] + [ANY] * (count + len(after)),
        out_specs=(ANY,) * count + (SMEM,),
        input_output_aliases={1 + i: i for i in range(count)},
        compiler_params=params(1),
        cost_estimate=COST,
        name="relay",
    )(pos, *passed, *after)


def sweep_kernel(pos, rate, shift, *refs, begin, count, heads):
    group = 4
    blocks, refs = refs[:group], refs[group:]
    tails, refs = refs[:heads], refs[heads:]
    outs, (token, first, edge, sems) = refs[:count], refs[count:]
    token[0], token[1] = pos[0], pos[1]
    planes, modes, cols = blocks[0].shape[1:]
    mine = 2 * planes
    part = outs[0].shape[0]
    rows = part * count
    lead = 2 * EDGE if heads else EDGE
    copies = []
    for g in range(heads):
        length = tails[g].shape[0]
        copies.append(
            pltpu.make_async_copy(
                tails[g].at[pl.ds(length - lead, lead)], edge.at[:, pl.ds(g * planes, planes)], sems.at[g]
            )
        )
    for copy in copies:
        copy.start()
    for copy in copies:
        copy.wait()
    low = planes - 1
    wide = mine + 2
    piece = min(modes, 16)

    def field(row, p, some):
        if isinstance(row, int) and row < lead:
            if heads:
                return edge[row, p, some]
            return jnp.zeros((some.size, cols), BF16)
        return blocks[p // planes][row - lead, p % planes, some]

    def beside(parts, number):
        return jnp.dot(
            to_bf16_rows(jnp.stack(parts)), shift[...], preferred_element_type=F32
        ).reshape(number, -1, modes, cols)

    def once(i, number):
        every = pl.ds(0, modes)
        aside = beside([field(i + 1 + a, low + p, every) for a in range(number) for p in range(wide)], number)
        for a in range(number):
            speeds = [rate[p, pl.ds(begin + i + a, 1), :] for p in range(wide)]
            for h in range(modes // piece):
                some = pl.ds(h * piece, piece)
                line = [field(i + 1 + a, low - 1 + p, some).astype(F32) for p in range(wide + 2)]
                for p in range(wide):
                    centre = line[p + 1]
                    around = aside[a, p, h * piece : (h + 1) * piece] + (line[p] + line[p + 2])
                    around = around + (
                        field(i + a, low + p, some).astype(F32) + field(i + 2 + a, low + p, some).astype(F32)
                    )
                    first[i + a, p, some] = centre + speeds[p] * (around - 6.0 * centre)

    for i in range(0, lead, 2):
        once(i, 2)

    def pair(j, _):
        once(lead + 2 * j, 2)
        return 0

    lax.fori_loop(0, (rows + 2 - lead) // 2, pair, 0)
    number = 2 if part % 2 == 0 else 1
    for k in range(count):
        base = jnp.bitwise_xor(pos[1], k) * part

        def again(j, _):
            i = base + number * j
            aside = beside([first[i + 1 + a, 1 + p] for a in range(number) for p in range(mine)], number)
            for a in range(number):
                speeds = [rate[p + 1, pl.ds(begin + i + a + 1, 1), :] for p in range(mine)]
                for h in range(modes // piece):
                    some = pl.ds(h * piece, piece)
                    line = [first[i + 1 + a, p, some] for p in range(wide)]
                    for p in range(mine):
                        centre = line[p + 1]
                        around = aside[a, p, h * piece : (h + 1) * piece] + (line[p] + line[p + 2])
                        around = around + (first[i + a, p + 1, some] + first[i + 2 + a, p + 1, some])
                        outs[k][number * j + a, p, some] = (
                            centre + speeds[p] * (around - 6.0 * centre)
                        ).astype(BF16)
            return 0

        lax.fori_loop(0, part // number, again, 0)


def sweep(pos, rate, shift, blocks, tails, begin, rows, count):
    _, planes, modes, cols = blocks[0].shape
    mine = 2 * planes
    piece = jax.ShapeDtypeStruct((rows // count, mine, modes, cols), BF16)
    return pl.pallas_call(
        functools.partial(sweep_kernel, begin=begin, count=count, heads=len(tails)),
        out_shape=(piece,) * count + (TOKEN,),
        in_specs=[SMEM] + [VMEM] * 6 + [ANY] * len(tails),
        out_specs=(VMEM,) * count + (SMEM,),
        scratch_shapes=[
            pltpu.VMEM((rows + 2, mine + 2, modes, cols), F32),
            pltpu.VMEM((2 * EDGE, 4 * planes, modes, cols), BF16),
            pltpu.SemaphoreType.DMA((4,)),
        ],
        compiler_params=params(22),
        cost_estimate=COST,
        name="sweep",
    )(pos, rate, shift, *blocks, *tails)


def points_kernel(pos, basis, basis_t, flat, swing, load, *refs, begin):
    *refs, token = refs
    token[0], token[1] = pos[0], pos[1]
    count = len(refs) // 2
    blocks, outs = refs[:count], refs[count:]
    part, planes, modes, cols = blocks[0].shape
    copies = cols // flat.shape[1]

    def row(i, _):
        place = begin + pos[1] * part + i
        for p in range(planes):
            if modes % 16 == 0:
                cells = jnp.concatenate([block[i, p] for block in blocks], axis=0)
            else:
                cells = jnp.concatenate([block[i, p].astype(F32) for block in blocks], axis=0).astype(BF16)
            heat = jnp.tanh(jnp.dot(basis[...], cells, preferred_element_type=F32))
            offset = jnp.concatenate([flat[...]] * copies, axis=1)
            slope = jnp.concatenate([swing[...]] * copies, axis=1)
            weighted = (offset + slope * heat).astype(BF16)
            source = jnp.dot(basis_t[...], weighted, preferred_element_type=F32).astype(BF16).astype(F32)
            done = cells.astype(F32) + load[p, pl.ds(place, 1), :] * source
            for k in range(count):
                outs[k][i, p] = done[k * modes : (k + 1) * modes].astype(BF16)
        return 0

    lax.fori_loop(0, part, row, 0)


def points(pos, basis, basis_t, flat, swing, load, blocks, begin):
    count = len(blocks)
    return pl.pallas_call(
        functools.partial(points_kernel, begin=begin),
        out_shape=tuple(jax.ShapeDtypeStruct(block.shape, BF16) for block in blocks) + (TOKEN,),
        in_specs=[SMEM] + [VMEM] * (5 + count),
        out_specs=(VMEM,) * count + (SMEM,),
        compiler_params=params(14),
        cost_estimate=COST,
        name="points",
    )(pos, basis, basis_t, flat, swing, load, *blocks)


def collect_kernel(pos, *refs):
    *blocks, out, token, sems = refs
    token[0], token[1] = pos[0], pos[1]
    part, planes = blocks[0].shape[0], out.shape[1]
    copies = []
    for k, block in enumerate(blocks):
        base = jnp.bitwise_xor(pos[1], k) * part
        copies.append(
            pltpu.make_async_copy(block.at[:, pl.ds(0, planes)], out.at[pl.ds(base, part)], sems.at[k])
        )
    for copy in copies:
        copy.start()
    for copy in copies:
        copy.wait()


def collect(pos, blocks):
    part, planes, modes, cols = blocks[0].shape
    count = len(blocks)
    shape = (part * count, planes // 2, modes, cols)
    return pl.pallas_call(
        collect_kernel,
        out_shape=(jax.ShapeDtypeStruct(shape, BF16), TOKEN),
        in_specs=[SMEM] + [ANY] * count,
        out_specs=(VMEM, SMEM),
        scratch_shapes=[pltpu.SemaphoreType.DMA((count,))],
        compiler_params=params(6),
        cost_estimate=COST,
        name="collect",
    )(pos, *blocks)


def settle_kernel(pos, turn, *refs, begin, count, chained):
    if chained:
        refs = refs[1:]
    blocks, other = refs[:count], refs[count]
    out, token, both, final, sems = refs[count + 1 :]
    token[0], token[1] = pos[0], pos[1]
    side = pos[0]
    part = blocks[0].shape[0]
    _, rows, planes, modes, cols = both.shape
    size = out.shape[2]
    group = turn.shape[1] // TILE
    incoming = [pltpu.make_async_copy(other, both.at[1], sems.at[count])]
    for k in range(count):
        base = jnp.bitwise_xor(pos[1], k) * part
        incoming.append(
            pltpu.make_async_copy(blocks[k].at[:, pl.ds(planes, planes)], both.at[0, pl.ds(base, part)], sems.at[k])
        )
    for copy in incoming:
        copy.start()
    outgoing = []
    for a in (1, 0):
        for copy in incoming[:1] if a else incoming[1:]:
            copy.wait()
        far = side if a == 0 else 1 - side
        for z in range(planes):
            to = jnp.where(far == 1, z, planes - 1 - z)
            for g in range(rows // TILE):
                block = jnp.where(far == 1, rows // TILE - 1 - g, g)
                for h in range(modes // group):
                    there = pl.ds(h * group, group)
                    x = both[a, pl.ds(g * TILE, TILE), z, there, :]
                    y = jnp.dot(turn[far], to_bf16_rows(x), preferred_element_type=F32).astype(BF16)
                    final[a, to, there, pl.ds(pl.multiple_of(block * TILE, TILE), TILE), :] = y.reshape(
                        group, TILE, cols
                    )
        start = pl.multiple_of(jnp.where(far == 1, size - rows - begin, begin), TILE)
        copy = pltpu.make_async_copy(final.at[a], out.at[:, :, pl.ds(start, rows), :], sems.at[count + 1 + a])
        copy.start()
        outgoing.append(copy)
    for copy in outgoing:
        copy.wait()


def settle(pos, turn, result, blocks, other, begin, shape):
    count = len(blocks)
    rows, planes, modes, cols = other.shape
    chained = result is not None
    return pl.pallas_call(
        functools.partial(settle_kernel, begin=begin, count=count, chained=chained),
        out_shape=(jax.ShapeDtypeStruct(shape, BF16), TOKEN),
        in_specs=[SMEM, VMEM] + [HBM] * chained + [ANY] * (count + 1),
        out_specs=(HBM, SMEM),
        scratch_shapes=[
            pltpu.VMEM((2, rows, planes, modes, cols), BF16),
            pltpu.VMEM((2, planes, modes, rows, cols), BF16),
            pltpu.SemaphoreType.DMA((count + 3,)),
        ],
        input_output_aliases={2: 0} if chained else {},
        compiler_params=params(10),
        cost_estimate=COST,
        name="settle",
    )(pos, turn, *([result] if chained else []), *blocks, other)


SIZES = (1, 1, 2, 2, 2)


def chunk_rows(half):
    unit = half // 8
    return [n * unit for n in SIZES]


ORDER = (
    ("T", 0), ("T", 1), ("R", 0), ("T", 2), ("R", 1), ("S", 0), ("T", 3), ("R", 2), ("S", 1), ("P", 0),
    ("T", 4), ("R", 3), ("S", 2), ("P", 1), ("C", 0), ("R", 4), ("S", 3), ("P", 2), ("C", 1), ("F", 0),
    ("S", 4), ("P", 3), ("C", 2), ("F", 1), ("P", 4), ("C", 3), ("F", 2), ("C", 4), ("F", 3), ("F", 4),
)


def turns(group):
    at = np.arange(group * TILE)
    row, mode = at // group, at % group
    same = mode[:, None] == (at // TILE)[None, :]
    straight = same & (row[:, None] == (at % TILE)[None, :])
    reverse = same & (row[:, None] == TILE - 1 - (at % TILE)[None, :])
    to_rows = np.stack([straight, reverse])
    return jnp.asarray(to_rows, BF16), jnp.asarray(to_rows.transpose(0, 2, 1), BF16)


def on_device(field, diffusion, joule, basis, quad_weight, base_conductivity, thermal_slope):
    planes, modes, size, cols = field.shape
    half = size // 2
    spaces, count = lax.axis_size("space"), lax.axis_size("modes")
    side = lax.axis_index("space") % 2
    me = lax.axis_index("modes")
    pos = jnp.stack([side, me]).astype(jnp.int32)

    swap = [(i, i ^ 1) for i in range(spaces)]
    ahead = [(i, i + 4 * (i % 2) - 2) for i in range(spaces)]
    ahead = [(i, j) for i, j in ahead if 0 <= j < spaces]
    back = [(j, i) for i, j in ahead]

    def across(x):
        return lax.ppermute(x, "space", swap)

    def ahead_of(x):
        return lax.ppermute(x, "space", ahead)

    def behind_of(x):
        return lax.ppermute(x, "space", back)

    def exchange(pieces):
        moved = [pieces[0]]
        for k in range(1, count):
            moved.append(lax.ppermute(pieces[k], "modes", [(j, j ^ k) for j in range(count)]))
        return moved

    def logical(x, length, side, sent):
        rows_back, planes_back = jnp.flip(x, 1)[:, :length], jnp.flip(x, 0)[:, :length]
        own = jnp.where(side == 1, rows_back, planes_back)
        send = jnp.where(side == 1, planes_back, rows_back).astype(sent)
        return own, send

    lane = np.arange(cols)
    shift = jnp.asarray(np.abs(lane[:, None] - lane[None, :]) == 1, BF16)
    to_rows, to_modes = turns(min(modes, TILE))

    points_count = basis.shape[0]
    extra = -points_count % 32
    turned = jnp.concatenate(
        [lax.dynamic_slice_in_dim(basis, (me ^ k) * modes, modes, axis=1) for k in range(count)], axis=1
    )
    turned = jnp.pad(turned, ((0, extra), (0, 0)))
    turned_t = turned.T
    level = quad_weight * base_conductivity
    spread_out = lambda v: jnp.broadcast_to(jnp.pad(v, (0, extra))[:, None], (points_count + extra, 128))
    flat, swing = spread_out(level), spread_out(level * thermal_slope)

    sent = []

    def coefficients(side):
        own_rate, send_rate = logical(diffusion, half + EDGE, side, F32)
        own_load, send_load = logical(joule, half, side, BF16)
        sent.extend((own_rate, own_load, across(send_rate), across(send_load)))
        return send_rate, send_load

    rows_of = chunk_rows(half)
    begins = [sum(rows_of[:c]) for c in range(len(rows_of))]
    own, other, before, blocks, cells, home, theirs = {}, {}, {}, {}, {}, {}, {}
    result = None
    for kind, c in ORDER:
        begin, rows = begins[c], rows_of[c]
        if kind == "T":
            skip = EDGE if c else 0
            after = ()
            if c == 1:
                after = coefficients(pos[0])
            own[c], send, pos = spread(pos, field, to_rows, after, begin, skip, rows + EDGE - skip, rows + TILE)
            other[c] = across(send)
            before[c] = ahead_of(own[c])
        elif kind == "R":
            if c == 0:
                if not sent:
                    coefficients(pos[0])
                own_rate, own_load, other_rate, other_load = sent
                other[c], other_rate, other_load, pos = relay(pos, (other[c], other_rate, other_load), (before[c],))
                edges = ahead_of(own_rate[-1:]), behind_of(other_rate[:1])
                rate = jnp.concatenate([edges[0], other_rate, own_rate, edges[1]], axis=0)
                rate = jnp.pad(rate, ((0, 0), (1, -(half + EDGE + 1) % 8), (0, 0)))
                load = jnp.concatenate([other_load.astype(F32), own_load], axis=0)
            else:
                other[c], pos = relay(pos, (other[c],), (before[c],))
            blocks[c] = (before[c], other[c], own[c], behind_of(other[c]))
        elif kind == "S":
            *pieces, pos = sweep(pos, rate, shift, blocks[c], blocks.get(c - 1, ()), begin, rows, count)
            cells[c] = exchange(pieces)
        elif kind == "P":
            *stepped, pos = points(pos, turned, turned_t, flat, swing, load, cells[c], begin)
            home[c] = exchange(stepped)
        elif kind == "C":
            out, pos = collect(pos, home[c])
            theirs[c] = across(out)
        else:
            result, pos = settle(pos, to_modes, result, home[c], theirs[c], begin, field.shape)
    return result


def solution(mesh):
    return jax.shard_map(
        on_device,
        mesh=mesh,
        in_specs=(
            P("space", "modes", None, None),
            P("space", None, None),
            P("space", None, None),
            P(),
            P(),
            P(),
            P(),
        ),
        out_specs=P("space", "modes", None, None),
        check_vma=False,
    )
```

```python
import functools

import jax
import jax.numpy as jnp
import numpy as np
from jax import lax
from jax.experimental import pallas as pl
from jax.experimental.pallas import tpu as pltpu
from jax.sharding import PartitionSpec as P

F32, BF16 = jnp.float32, jnp.bfloat16
ANY = pl.BlockSpec(memory_space=pl.ANY)
VMEM = pl.BlockSpec(memory_space=pltpu.VMEM)
HBM = pl.BlockSpec(memory_space=pltpu.HBM)
SMEM = pl.BlockSpec(memory_space=pltpu.SMEM)
TOKEN = jax.ShapeDtypeStruct((2,), jnp.int32)
COST = pl.CostEstimate(flops=1, bytes_accessed=1, transcendentals=0)
EDGE = 2
TILE = 16
LANES = 128


def params(mebibytes):
    return pltpu.CompilerParams(vmem_limit_bytes=mebibytes * 1024 * 1024)


def from_rows(y, group):
    if group % 16 == 0:
        return y.astype(BF16).reshape(-1, group, y.shape[1])
    return y.reshape(-1, group, y.shape[1]).astype(BF16)


def to_bf16_rows(x):
    a, m, y = x.shape
    if m % 16 == 0:
        return x.astype(BF16).reshape(a * m, y)
    return x.astype(F32).reshape(a * m, y).astype(BF16)


def spread_kernel(pos, field, turn, *refs, spans):
    outs, (token, window, sems) = refs[-3 - 2 * len(spans) : -3], refs[-3:]
    side = pos[0]
    token[0], token[1] = pos[0], pos[1]
    blocks, _, planes, modes, _, cols = window.shape
    base = spans[0][0] // TILE
    size = field.shape[2]
    group = turn.shape[1] // TILE
    copies = {}
    for g in range(blocks):
        for a in range(2):
            far = 1 - side if a == 0 else side
            begin = (base + g) * TILE
            start = pl.multiple_of(jnp.where(far == 1, size - TILE - begin, begin), TILE)
            copies[g, a] = pltpu.make_async_copy(
                field.at[:, :, pl.ds(start, TILE), :], window.at[g, a], sems.at[g, a]
            )
            copies[g, a].start()
    for g in range(blocks):
        for a in range(2):
            far = 1 - side if a == 0 else side
            copies[g, a].wait()
            for z in range(planes):
                to = jnp.where(far == 1, z, planes - 1 - z)
                for h in range(modes // group):
                    there = pl.ds(h * group, group)
                    x = window[g, a, z, there]
                    y = jnp.dot(turn[far], x.reshape(group * TILE, cols), preferred_element_type=F32)
                    y = from_rows(y, group)
                    for n, (first, last) in enumerate(spans):
                        low, high = (min(max(r - (base + g) * TILE, 0), TILE) for r in (first, last))
                        if low < high:
                            at = (base + g) * TILE + low - first
                            outs[2 * n + a][pl.ds(at, high - low), to, there, :] = y[low:high]


def spread(pos, field, turn, after, spans):
    planes, modes, _, cols = field.shape
    pieces = [jax.ShapeDtypeStruct((last - first, planes, modes, cols), BF16) for first, last in spans]
    pieces = [piece for piece in pieces for _ in range(2)]
    blocks = -(-spans[-1][1] // TILE) - spans[0][0] // TILE
    return pl.pallas_call(
        functools.partial(spread_kernel, spans=spans),
        out_shape=(*pieces, TOKEN),
        in_specs=[SMEM, HBM, VMEM] + [ANY] * len(after),
        out_specs=(VMEM,) * len(pieces) + (SMEM,),
        scratch_shapes=[
            pltpu.VMEM((blocks, 2, planes, modes, TILE, cols), BF16),
            pltpu.SemaphoreType.DMA((blocks, 2)),
        ],
        compiler_params=params(48),
        cost_estimate=COST,
        name="spread",
    )(pos, field, turn, *after)


def relay_kernel(pos, *refs):
    token = refs[-1]
    token[0], token[1] = pos[0], pos[1]


def relay(pos, passed, after):
    count = len(passed)
    return pl.pallas_call(
        relay_kernel,
        out_shape=tuple(jax.ShapeDtypeStruct(x.shape, x.dtype) for x in passed) + (TOKEN,),
        in_specs=[SMEM] + [ANY] * (count + len(after)),
        out_specs=(ANY,) * count + (SMEM,),
        input_output_aliases={1 + i: i for i in range(count)},
        compiler_params=params(1),
        cost_estimate=COST,
        name="relay",
    )(pos, *passed, *after)


def sweep_kernel(pos, rate, *refs, begin, count, heads):
    group = 4
    blocks, refs = refs[:group], refs[group:]
    tails, refs = refs[:heads], refs[heads:]
    outs, (token, first, edge, sems) = refs[:count], refs[count:]
    token[0], token[1] = pos[0], pos[1]
    planes, modes, cols = blocks[0].shape[1:]
    mine = 2 * planes
    part = outs[0].shape[0]
    rows = part * count
    lead = 2 * EDGE if heads else EDGE
    copies = []
    for g in range(heads):
        length = tails[g].shape[0]
        copies.append(
            pltpu.make_async_copy(
                tails[g].at[pl.ds(length - lead, lead)], edge.at[:, pl.ds(g * planes, planes)], sems.at[g]
            )
        )
    for copy in copies:
        copy.start()
    for copy in copies:
        copy.wait()
    low = planes - 1
    wide = mine + 2
    piece = min(modes, 16)

    def field(row, p, some):
        if isinstance(row, int) and row < lead:
            if heads:
                return edge[row, p, some]
            return jnp.zeros((some.size, cols), BF16)
        return blocks[p // planes][row - lead, p % planes, some]

    def beside(x):
        parts = [x[:, h * LANES : (h + 1) * LANES] for h in range(cols // LANES)]
        up = [pltpu.roll(part, 1, 1) for part in parts]
        down = [pltpu.roll(part, LANES - 1, 1) for part in parts]
        lane = lax.broadcasted_iota(jnp.int32, parts[0].shape, 1)
        nothing = jnp.zeros_like(parts[0])
        sums = []
        for h in range(len(parts)):
            left = jnp.where(lane == 0, up[h - 1] if h else nothing, up[h])
            right = jnp.where(lane == LANES - 1, down[h + 1] if h + 1 < len(parts) else nothing, down[h])
            sums.append(left + right)
        return jnp.concatenate(sums, axis=1)

    def once(i, number):
        for a in range(number):
            speeds = [rate[p, pl.ds(begin + i + a, 1), :] for p in range(wide)]
            for h in range(modes // piece):
                some = pl.ds(h * piece, piece)
                line = [field(i + 1 + a, low - 1 + p, some).astype(F32) for p in range(wide + 2)]
                for p in range(wide):
                    centre = line[p + 1]
                    around = beside(centre) + (line[p] + line[p + 2])
                    around = around + (
                        field(i + a, low + p, some).astype(F32) + field(i + 2 + a, low + p, some).astype(F32)
                    )
                    first[i + a, p, some] = centre + speeds[p] * (around - 6.0 * centre)

    for i in range(0, lead, 2):
        once(i, 2)

    def pair(j, _):
        once(lead + 2 * j, 2)
        return 0

    lax.fori_loop(0, (rows + 2 - lead) // 2, pair, 0)
    number = 2 if part % 2 == 0 else 1
    for k in range(count):
        base = jnp.bitwise_xor(pos[1], k) * part

        def again(j, _):
            i = base + number * j
            for a in range(number):
                speeds = [rate[p + 1, pl.ds(begin + i + a + 1, 1), :] for p in range(mine)]
                for h in range(modes // piece):
                    some = pl.ds(h * piece, piece)
                    line = [first[i + 1 + a, p, some] for p in range(wide)]
                    for p in range(mine):
                        centre = line[p + 1]
                        around = beside(centre) + (line[p] + line[p + 2])
                        around = around + (first[i + a, p + 1, some] + first[i + 2 + a, p + 1, some])
                        outs[k][number * j + a, p, some] = (
                            centre + speeds[p] * (around - 6.0 * centre)
                        ).astype(BF16)
            return 0

        lax.fori_loop(0, part // number, again, 0)


def sweep(pos, rate, blocks, tails, begin, rows, count):
    _, planes, modes, cols = blocks[0].shape
    mine = 2 * planes
    piece = jax.ShapeDtypeStruct((rows // count, mine, modes, cols), BF16)
    return pl.pallas_call(
        functools.partial(sweep_kernel, begin=begin, count=count, heads=len(tails)),
        out_shape=(piece,) * count + (TOKEN,),
        in_specs=[SMEM] + [VMEM] * 5 + [ANY] * len(tails),
        out_specs=(VMEM,) * count + (SMEM,),
        scratch_shapes=[
            pltpu.VMEM((rows + 2, mine + 2, modes, cols), F32),
            pltpu.VMEM((2 * EDGE, 4 * planes, modes, cols), BF16),
            pltpu.SemaphoreType.DMA((4,)),
        ],
        compiler_params=params(22),
        cost_estimate=COST,
        name="sweep",
    )(pos, rate, *blocks, *tails)


def points_kernel(pos, basis, basis_t, flat, swing, load, *refs, begin):
    *refs, token, gathered, stepped = refs
    token[0], token[1] = pos[0], pos[1]
    count = len(refs) // 2
    blocks, outs = refs[:count], refs[count:]
    part, planes, modes, cols = blocks[0].shape
    copies = cols // flat.shape[1]
    places = [pl.multiple_of(jnp.bitwise_xor(pos[1], k) * modes, modes) for k in range(count)]

    def row(i, _):
        place = begin + pos[1] * part + i
        for p in range(planes):
            for k in range(count):
                gathered[p, pl.ds(places[k], modes)] = blocks[k][i, p].astype(gathered.dtype)
            cells = gathered[p].astype(BF16)
            heat = jnp.tanh(jnp.dot(basis[...], cells, preferred_element_type=F32))
            offset = jnp.concatenate([flat[...]] * copies, axis=1)
            slope = jnp.concatenate([swing[...]] * copies, axis=1)
            weighted = (offset + slope * heat).astype(BF16)
            source = jnp.dot(basis_t[...], weighted, preferred_element_type=F32).astype(BF16).astype(F32)
            done = cells.astype(F32) + load[p, pl.ds(place, 1), :] * source
            stepped[p] = done.astype(stepped.dtype)
            for k in range(count):
                outs[k][i, p] = stepped[p, pl.ds(places[k], modes)].astype(BF16)
        return 0

    lax.fori_loop(0, part, row, 0)


def points(pos, basis, basis_t, flat, swing, load, blocks, begin):
    count = len(blocks)
    _, planes, modes, cols = blocks[0].shape
    kept = BF16 if modes % 16 == 0 else F32
    return pl.pallas_call(
        functools.partial(points_kernel, begin=begin),
        out_shape=tuple(jax.ShapeDtypeStruct(block.shape, BF16) for block in blocks) + (TOKEN,),
        in_specs=[SMEM] + [VMEM] * (5 + count),
        out_specs=(VMEM,) * count + (SMEM,),
        scratch_shapes=[pltpu.VMEM((planes, modes * count, cols), kept)] * 2,
        compiler_params=params(14),
        cost_estimate=COST,
        name="points",
    )(pos, basis, basis_t, flat, swing, load, *blocks)


def collect_kernel(pos, *refs):
    *blocks, out, token, sems = refs
    token[0], token[1] = pos[0], pos[1]
    part, planes = blocks[0].shape[0], out.shape[1]
    copies = []
    for k, block in enumerate(blocks):
        base = jnp.bitwise_xor(pos[1], k) * part
        copies.append(
            pltpu.make_async_copy(block.at[:, pl.ds(0, planes)], out.at[pl.ds(base, part)], sems.at[k])
        )
    for copy in copies:
        copy.start()
    for copy in copies:
        copy.wait()


def collect(pos, blocks):
    part, planes, modes, cols = blocks[0].shape
    count = len(blocks)
    shape = (part * count, planes // 2, modes, cols)
    return pl.pallas_call(
        collect_kernel,
        out_shape=(jax.ShapeDtypeStruct(shape, BF16), TOKEN),
        in_specs=[SMEM] + [ANY] * count,
        out_specs=(VMEM, SMEM),
        scratch_shapes=[pltpu.SemaphoreType.DMA((count,))],
        compiler_params=params(6),
        cost_estimate=COST,
        name="collect",
    )(pos, *blocks)


def settle_kernel(pos, turn, *refs, begin, count, chained):
    if chained:
        refs = refs[1:]
    blocks, other = refs[:count], refs[count]
    out, token, both, final, sems = refs[count + 1 :]
    token[0], token[1] = pos[0], pos[1]
    side = pos[0]
    part = blocks[0].shape[0]
    _, rows, planes, modes, cols = both.shape
    size = out.shape[2]
    group = turn.shape[1] // TILE
    incoming = [pltpu.make_async_copy(other, both.at[1], sems.at[count])]
    for k in range(count):
        base = jnp.bitwise_xor(pos[1], k) * part
        incoming.append(
            pltpu.make_async_copy(blocks[k].at[:, pl.ds(planes, planes)], both.at[0, pl.ds(base, part)], sems.at[k])
        )
    for copy in incoming:
        copy.start()
    outgoing = []
    for a in (1, 0):
        for copy in incoming[:1] if a else incoming[1:]:
            copy.wait()
        far = side if a == 0 else 1 - side
        for z in range(planes):
            to = jnp.where(far == 1, z, planes - 1 - z)
            for g in range(rows // TILE):
                block = jnp.where(far == 1, rows // TILE - 1 - g, g)
                for h in range(modes // group):
                    there = pl.ds(h * group, group)
                    x = both[a, pl.ds(g * TILE, TILE), z, there, :]
                    y = jnp.dot(turn[far], to_bf16_rows(x), preferred_element_type=F32).astype(BF16)
                    final[a, to, there, pl.ds(pl.multiple_of(block * TILE, TILE), TILE), :] = y.reshape(
                        group, TILE, cols
                    )
        start = pl.multiple_of(jnp.where(far == 1, size - rows - begin, begin), TILE)
        copy = pltpu.make_async_copy(final.at[a], out.at[:, :, pl.ds(start, rows), :], sems.at[count + 1 + a])
        copy.start()
        outgoing.append(copy)
    for copy in outgoing:
        copy.wait()


def settle(pos, turn, result, blocks, other, begin, shape):
    count = len(blocks)
    rows, planes, modes, cols = other.shape
    chained = result is not None
    return pl.pallas_call(
        functools.partial(settle_kernel, begin=begin, count=count, chained=chained),
        out_shape=(jax.ShapeDtypeStruct(shape, BF16), TOKEN),
        in_specs=[SMEM, VMEM] + [HBM] * chained + [ANY] * (count + 1),
        out_specs=(HBM, SMEM),
        scratch_shapes=[
            pltpu.VMEM((2, rows, planes, modes, cols), BF16),
            pltpu.VMEM((2, planes, modes, rows, cols), BF16),
            pltpu.SemaphoreType.DMA((count + 3,)),
        ],
        input_output_aliases={2: 0} if chained else {},
        compiler_params=params(10),
        cost_estimate=COST,
        name="settle",
    )(pos, turn, *([result] if chained else []), *blocks, other)


SIZES = (1, 1, 2, 2, 2)


def chunk_rows(half):
    unit = half // 8
    return [n * unit for n in SIZES]


ORDER = (
    ("T", 0), ("T", 1), ("R", 0), ("R", 1), ("S", 0), ("R", 2), ("S", 1), ("P", 0),
    ("R", 3), ("S", 2), ("P", 1), ("C", 0), ("R", 4), ("S", 3), ("P", 2), ("C", 1), ("F", 0),
    ("S", 4), ("P", 3), ("C", 2), ("F", 1), ("P", 4), ("C", 3), ("F", 2), ("C", 4), ("F", 3), ("F", 4),
)


def turns(group):
    at = np.arange(group * TILE)
    row, mode = at // group, at % group
    same = mode[:, None] == (at // TILE)[None, :]
    straight = same & (row[:, None] == (at % TILE)[None, :])
    reverse = same & (row[:, None] == TILE - 1 - (at % TILE)[None, :])
    to_rows = np.stack([straight, reverse])
    return jnp.asarray(to_rows, BF16), jnp.asarray(to_rows.transpose(0, 2, 1), BF16)


def on_device(field, diffusion, joule, basis, quad_weight, base_conductivity, thermal_slope):
    planes, modes, size, cols = field.shape
    half = size // 2
    spaces, count = lax.axis_size("space"), lax.axis_size("modes")
    side = lax.axis_index("space") % 2
    me = lax.axis_index("modes")
    pos = jnp.stack([side, me]).astype(jnp.int32)

    swap = [(i, i ^ 1) for i in range(spaces)]
    ahead = [(i, i + 4 * (i % 2) - 2) for i in range(spaces)]
    ahead = [(i, j) for i, j in ahead if 0 <= j < spaces]
    back = [(j, i) for i, j in ahead]

    beyond = [(i, i - 1 if i % 2 == 0 else i + 1) for i in range(spaces)]
    beyond = [(i, j) for i, j in beyond if 0 <= j < spaces]

    def across(x):
        return lax.ppermute(x, "space", swap)

    def ahead_of(x):
        return lax.ppermute(x, "space", ahead)

    def behind_of(x):
        return lax.ppermute(x, "space", back)

    def exchange(pieces):
        moved = [pieces[0]]
        for k in range(1, count):
            moved.append(lax.ppermute(pieces[k], "modes", [(j, j ^ k) for j in range(count)]))
        return moved

    def logical(x, length, side, sent):
        rows_back, planes_back = jnp.flip(x, 1)[:, :length], jnp.flip(x, 0)[:, :length]
        own = jnp.where(side == 1, rows_back, planes_back)
        send = jnp.where(side == 1, planes_back, rows_back).astype(sent)
        return own, send

    to_rows, to_modes = turns(min(modes, TILE))

    points_count = basis.shape[0]
    extra = -points_count % 32
    basis = jnp.pad(basis, ((0, extra), (0, 0)))
    basis_t = basis.T
    level = quad_weight * base_conductivity
    spread_out = lambda v: jnp.broadcast_to(jnp.pad(v, (0, extra))[:, None], (points_count + extra, 128))
    flat, swing = spread_out(level), spread_out(level * thermal_slope)

    def coefficients(side):
        own_rate, send_rate = logical(diffusion, half + EDGE, side, F32)
        own_load, send_load = logical(joule, half, side, BF16)
        edge_rate = lax.ppermute(send_rate[:1], "space", beyond)
        rates = ahead_of(own_rate[-1:]), across(send_rate), edge_rate
        return own_rate, own_load, rates, across(send_load), (send_rate, send_load)

    rows_of = chunk_rows(half)
    begins = [sum(rows_of[:c]) for c in range(len(rows_of))]
    edges = [(begin + EDGE * (begin > 0), begin + rows + EDGE) for begin, rows in zip(begins, rows_of)]
    own, other, before, blocks, cells, home, theirs = {}, {}, {}, {}, {}, {}, {}
    result = None
    for kind, c in ORDER:
        begin, rows = begins[c], rows_of[c]
        if kind == "T":
            after = ()
            if c:
                after = (*[rates[n] for n in (1,)], basis, basis_t, flat, swing)
            else:
                own_rate, own_load, rates, other_load, after = coefficients(pos[0])
            those = range(1, len(rows_of)) if c else (0,)
            *pieces, pos = spread(pos, field, to_rows, after, [edges[n] for n in those])
            for n in those:
                send, own[n], *pieces = pieces
                other[n], before[n] = across(send), ahead_of(own[n])
        elif kind == "R":
            if c == 0:
                after = (before[c], *[rates[n] for n in (0, 2)])
                other[c], pos = relay(pos, (other[c],), after)
                rate = jnp.concatenate([rates[0], rates[1], own_rate, rates[2]], axis=0)
                rate = jnp.pad(rate, ((0, 0), (1, -(half + EDGE + 1) % 8), (0, 0)))
            elif c == 1:
                other[c], other_load, pos = relay(pos, (other[c], other_load), (before[c],))
                load = jnp.concatenate([other_load.astype(F32), own_load], axis=0)
            else:
                other[c], pos = relay(pos, (other[c],), (before[c],))
            blocks[c] = (before[c], other[c], own[c], behind_of(other[c]))
        elif kind == "S":
            *pieces, pos = sweep(pos, rate, blocks[c], blocks.get(c - 1, ()), begin, rows, count)
            cells[c] = exchange(pieces)
        elif kind == "P":
            *stepped, pos = points(pos, basis, basis_t, flat, swing, load, cells[c], begin)
            home[c] = exchange(stepped)
        elif kind == "C":
            out, pos = collect(pos, home[c])
            theirs[c] = across(out)
        else:
            result, pos = settle(pos, to_modes, result, home[c], theirs[c], begin, field.shape)
    return result


def solution(mesh):
    return jax.shard_map(
        on_device,
        mesh=mesh,
        in_specs=(
            P("space", "modes", None, None),
            P("space", None, None),
            P("space", None, None),
            P(),
            P(),
            P(),
            P(),
        ),
        out_specs=P("space", "modes", None, None),
        check_vma=False,
    )
```

```python
import functools

import jax
import jax.numpy as jnp
import numpy as np
from jax import lax
from jax.experimental import pallas as pl
from jax.experimental.pallas import tpu as pltpu
from jax.sharding import PartitionSpec as P

F32, BF16 = jnp.float32, jnp.bfloat16
ANY = pl.BlockSpec(memory_space=pl.ANY)
VMEM = pl.BlockSpec(memory_space=pltpu.VMEM)
HBM = pl.BlockSpec(memory_space=pltpu.HBM)
SMEM = pl.BlockSpec(memory_space=pltpu.SMEM)
TOKEN = jax.ShapeDtypeStruct((3,), jnp.int32)
COST = pl.CostEstimate(flops=1, bytes_accessed=1, transcendentals=0)
EDGE = 2
TILE = 16
LANES = 128


def params(mebibytes):
    return pltpu.CompilerParams(vmem_limit_bytes=mebibytes * 1024 * 1024)


def from_rows(y, group):
    if group % 16 == 0:
        return y.astype(BF16).reshape(-1, group, y.shape[1])
    return y.reshape(-1, group, y.shape[1]).astype(BF16)


def hand_on(pos, token):
    for n in range(3):
        token[n] = pos[n]


def to_bf16_rows(x):
    a, m, y = x.shape
    if m % 16 == 0:
        return x.astype(BF16).reshape(a * m, y)
    return x.astype(F32).reshape(a * m, y).astype(BF16)


def spread_kernel(pos, field, raw, turn, *refs, spans, base):
    outs, (token, window, sems) = refs[-3 - 2 * len(spans) : -3], refs[-3:]
    side, core = pos[0], pos[2]
    hand_on(pos, token)
    blocks, _, planes, modes, _, cols = window.shape
    modes = modes // 2
    size = field.shape[2]
    quarter = size // 4
    depth = raw.shape[3]
    group = turn.shape[1] // TILE
    copies = {}
    for g in range(blocks):
        for a in range(2):
            far = 1 - side if a == 0 else side
            begin = core * quarter + (base + g) * TILE
            there = g if base >= 0 else g - 1 + core
            if base + g < 0:
                begin, there = jnp.maximum(begin, 0), jnp.maximum(there, 0)
            start = pl.multiple_of(jnp.where(far == 1, size - TILE - begin, begin), TILE)
            place = pl.multiple_of(jnp.where(far == 1, depth - TILE * (there + 1), TILE * there), TILE)
            copies[g, a] = (
                pltpu.make_async_copy(
                    field.at[:, :, pl.ds(start, TILE), :],
                    window.at[g, a, :, pl.ds(core * modes, modes)],
                    sems.at[g, a, 0],
                ),
                pltpu.make_async_copy(
                    raw.at[a, :, :, pl.ds(place, TILE), :],
                    window.at[g, a, :, pl.ds((1 - core) * modes, modes)],
                    sems.at[g, a, 1],
                ),
            )
            for copy in copies[g, a]:
                copy.start()
    for g in range(blocks):
        for a in range(2):
            far = 1 - side if a == 0 else side
            for copy in copies[g, a]:
                copy.wait()
            for z in range(planes):
                to = jnp.where(far == 1, z, planes - 1 - z)
                for h in range(2 * modes // group):
                    there = pl.ds(h * group, group)
                    x = window[g, a, z, there]
                    y = jnp.dot(turn[far], x.reshape(group * TILE, cols), preferred_element_type=F32)
                    if base + g < 0:
                        y = jnp.where(core == 1, y, 0.0)
                    y = from_rows(y, group)
                    for n, (first, last) in enumerate(spans):
                        low, high = (min(max(r - (base + g) * TILE, 0), TILE) for r in (first, last))
                        if low < high:
                            at = (base + g) * TILE + low - first
                            outs[2 * n + a][pl.ds(at, high - low), to, there, :] = y[low:high]


def blocks_of(spans):
    base = spans[0][0] // TILE
    return base, -(-spans[-1][1] // TILE) - base


def spread(pos, field, raw, turn, after, spans):
    planes, modes, _, cols = field.shape
    pieces = [jax.ShapeDtypeStruct((last - first, planes, 2 * modes, cols), BF16) for first, last in spans]
    pieces = [piece for piece in pieces for _ in range(2)]
    base, blocks = blocks_of(spans)
    return pl.pallas_call(
        functools.partial(spread_kernel, spans=spans, base=base),
        out_shape=(*pieces, TOKEN),
        in_specs=[SMEM, HBM, ANY, VMEM] + [ANY] * len(after),
        out_specs=(VMEM,) * len(pieces) + (SMEM,),
        scratch_shapes=[
            pltpu.VMEM((blocks, 2, planes, 2 * modes, TILE, cols), BF16),
            pltpu.SemaphoreType.DMA((blocks, 2, 2)),
        ],
        compiler_params=params(48),
        cost_estimate=COST,
        name="spread",
    )(pos, field, raw, turn, *after)


def relay_kernel(pos, *refs):
    token = refs[-1]
    hand_on(pos, token)


def relay(pos, passed, after):
    count = len(passed)
    return pl.pallas_call(
        relay_kernel,
        out_shape=tuple(jax.ShapeDtypeStruct(x.shape, x.dtype) for x in passed) + (TOKEN,),
        in_specs=[SMEM] + [ANY] * (count + len(after)),
        out_specs=(ANY,) * count + (SMEM,),
        input_output_aliases={1 + i: i for i in range(count)},
        compiler_params=params(1),
        cost_estimate=COST,
        name="relay",
    )(pos, *passed, *after)


def sweep_kernel(pos, rate, *refs, begin, count, heads):
    group = 4
    blocks, refs = refs[:group], refs[group:]
    tails, refs = refs[:heads], refs[heads:]
    outs, (token, first, edge, sems) = refs[:count], refs[count:]
    hand_on(pos, token)
    planes, modes, cols = blocks[0].shape[1:]
    mine = 2 * planes
    part = outs[0].shape[0]
    rows = part * count
    lead = 2 * EDGE if heads else 0
    copies = []
    for g in range(heads):
        length = tails[g].shape[0]
        copies.append(
            pltpu.make_async_copy(
                tails[g].at[pl.ds(length - lead, lead)], edge.at[:, pl.ds(g * planes, planes)], sems.at[g]
            )
        )
    for copy in copies:
        copy.start()
    for copy in copies:
        copy.wait()
    low = planes - 1
    wide = mine + 2
    piece = min(modes, 16)

    def field(row, p, some):
        if isinstance(row, int) and row < lead:
            return edge[row, p, some]
        return blocks[p // planes][row - lead, p % planes, some]

    def beside(x):
        parts = [x[:, h * LANES : (h + 1) * LANES] for h in range(cols // LANES)]
        up = [pltpu.roll(part, 1, 1) for part in parts]
        down = [pltpu.roll(part, LANES - 1, 1) for part in parts]
        lane = lax.broadcasted_iota(jnp.int32, parts[0].shape, 1)
        nothing = jnp.zeros_like(parts[0])
        sums = []
        for h in range(len(parts)):
            left = jnp.where(lane == 0, up[h - 1] if h else nothing, up[h])
            right = jnp.where(lane == LANES - 1, down[h + 1] if h + 1 < len(parts) else nothing, down[h])
            sums.append(left + right)
        return jnp.concatenate(sums, axis=1)

    def once(i, number):
        for a in range(number):
            speeds = [rate[p, pl.ds(begin + i + a, 1), :] for p in range(wide)]
            for h in range(modes // piece):
                some = pl.ds(h * piece, piece)
                line = [field(i + 1 + a, low - 1 + p, some).astype(F32) for p in range(wide + 2)]
                for p in range(wide):
                    centre = line[p + 1]
                    around = beside(centre) + (line[p] + line[p + 2])
                    around = around + (
                        field(i + a, low + p, some).astype(F32) + field(i + 2 + a, low + p, some).astype(F32)
                    )
                    first[i + a, p, some] = centre + speeds[p] * (around - 6.0 * centre)

    for i in range(0, lead, 2):
        once(i, 2)

    def pair(j, _):
        once(lead + 2 * j, 2)
        return 0

    lax.fori_loop(0, (rows + 2 - lead) // 2, pair, 0)
    number = 2 if part % 2 == 0 else 1
    for k in range(count):
        base = jnp.bitwise_xor(pos[1], k) * part

        def again(j, _):
            i = base + number * j
            for a in range(number):
                speeds = [rate[p + 1, pl.ds(begin + i + a + 1, 1), :] for p in range(mine)]
                for h in range(modes // piece):
                    some = pl.ds(h * piece, piece)
                    line = [first[i + 1 + a, p, some] for p in range(wide)]
                    for p in range(mine):
                        centre = line[p + 1]
                        around = beside(centre) + (line[p] + line[p + 2])
                        around = around + (first[i + a, p + 1, some] + first[i + 2 + a, p + 1, some])
                        outs[k][number * j + a, p, some] = (
                            centre + speeds[p] * (around - 6.0 * centre)
                        ).astype(BF16)
            return 0

        lax.fori_loop(0, part // number, again, 0)


def sweep(pos, rate, blocks, tails, begin, rows, count):
    _, planes, modes, cols = blocks[0].shape
    mine = 2 * planes
    piece = jax.ShapeDtypeStruct((rows // count, mine, modes, cols), BF16)
    return pl.pallas_call(
        functools.partial(sweep_kernel, begin=begin, count=count, heads=len(tails)),
        out_shape=(piece,) * count + (TOKEN,),
        in_specs=[SMEM] + [VMEM] * 5 + [ANY] * len(tails),
        out_specs=(VMEM,) * count + (SMEM,),
        scratch_shapes=[
            pltpu.VMEM((rows + 2, mine + 2, modes, cols), F32),
            pltpu.VMEM((2 * EDGE, 4 * planes, modes, cols), BF16),
            pltpu.SemaphoreType.DMA((4,)),
        ],
        compiler_params=params(22),
        cost_estimate=COST,
        name="sweep",
    )(pos, rate, *blocks, *tails)


def points_kernel(pos, basis, basis_t, flat, swing, load, *refs, begin):
    *refs, token, gathered, stepped = refs
    hand_on(pos, token)
    count = len(refs) // 2
    blocks, outs = refs[:count], refs[count:]
    part, planes, modes, cols = blocks[0].shape
    copies = cols // flat.shape[1]
    places = [pl.multiple_of(jnp.bitwise_xor(pos[1], k) * modes, modes) for k in range(count)]

    def row(i, _):
        place = begin + pos[1] * part + i
        for p in range(planes):
            for k in range(count):
                gathered[p, pl.ds(places[k], modes)] = blocks[k][i, p].astype(gathered.dtype)
            cells = gathered[p].astype(BF16)
            heat = jnp.tanh(jnp.dot(basis[...], cells, preferred_element_type=F32))
            offset = jnp.concatenate([flat[...]] * copies, axis=1)
            slope = jnp.concatenate([swing[...]] * copies, axis=1)
            weighted = (offset + slope * heat).astype(BF16)
            source = jnp.dot(basis_t[...], weighted, preferred_element_type=F32).astype(BF16).astype(F32)
            done = cells.astype(F32) + load[p, pl.ds(place, 1), :] * source
            stepped[p] = done.astype(stepped.dtype)
            for k in range(count):
                outs[k][i, p] = stepped[p, pl.ds(places[k], modes)].astype(BF16)
        return 0

    lax.fori_loop(0, part, row, 0)


def points(pos, basis, basis_t, flat, swing, load, blocks, begin):
    count = len(blocks)
    _, planes, modes, cols = blocks[0].shape
    kept = BF16 if modes % 16 == 0 else F32
    return pl.pallas_call(
        functools.partial(points_kernel, begin=begin),
        out_shape=tuple(jax.ShapeDtypeStruct(block.shape, BF16) for block in blocks) + (TOKEN,),
        in_specs=[SMEM] + [VMEM] * (5 + count),
        out_specs=(VMEM,) * count + (SMEM,),
        scratch_shapes=[pltpu.VMEM((planes, modes * count, cols), kept)] * 2,
        compiler_params=params(14),
        cost_estimate=COST,
        name="points",
    )(pos, basis, basis_t, flat, swing, load, *blocks)


def collect_kernel(pos, *refs):
    *blocks, out, token, sems = refs
    hand_on(pos, token)
    part, planes = blocks[0].shape[0], out.shape[1]
    copies = []
    for k, block in enumerate(blocks):
        base = jnp.bitwise_xor(pos[1], k) * part
        copies.append(
            pltpu.make_async_copy(block.at[:, pl.ds(0, planes)], out.at[pl.ds(base, part)], sems.at[k])
        )
    for copy in copies:
        copy.start()
    for copy in copies:
        copy.wait()


def collect(pos, blocks):
    part, planes, modes, cols = blocks[0].shape
    count = len(blocks)
    shape = (part * count, planes // 2, modes, cols)
    return pl.pallas_call(
        collect_kernel,
        out_shape=(jax.ShapeDtypeStruct(shape, BF16), TOKEN),
        in_specs=[SMEM] + [ANY] * count,
        out_specs=(VMEM, SMEM),
        scratch_shapes=[pltpu.SemaphoreType.DMA((count,))],
        compiler_params=params(6),
        cost_estimate=COST,
        name="collect",
    )(pos, *blocks)


def put(out, source, side, core, begin, sems):
    rows, size = source.shape[3], out.shape[2]
    begin = core * (size // 4) + begin
    copies = []
    for a in range(2):
        far = side if a == 0 else 1 - side
        start = pl.multiple_of(jnp.where(far == 1, size - rows - begin, begin), TILE)
        copies.append(pltpu.make_async_copy(source.at[a], out.at[:, :, pl.ds(start, rows), :], sems.at[a]))
    for copy in copies:
        copy.start()
    return copies


def settle_kernel(pos, turn, *refs, begin, old_begin, parts, arrivals):
    refs = refs[-len(parts) - 7 - arrivals :]
    pieces, arrived, refs = refs[: len(parts)], refs[len(parts) : len(parts) + arrivals], refs[-7:]
    away, out, token, both, final, sems, out_sems = refs
    hand_on(pos, token)
    side, core = pos[0], pos[2]
    _, rows, planes, modes, cols = both.shape
    modes = modes // 2
    group = turn.shape[1] // TILE
    outgoing = put(out, arrived[0], side, 1 - core, old_begin, out_sems.at[0]) if arrivals else []
    incoming = []
    for n, (piece, (a, at, xor, low)) in enumerate(zip(pieces, parts)):
        length = piece.shape[0]
        if xor is not None:
            at = at + jnp.bitwise_xor(pos[1], xor) * length
        copy = pltpu.make_async_copy(
            piece.at[:, pl.ds(low, planes)], both.at[a, pl.ds(at, length)], sems.at[n]
        )
        copy.start()
        incoming.append(copy)
    for a in (0, 1):
        for copy, part in zip(incoming, parts):
            if part[0] == a:
                copy.wait()
        far = side if a == 0 else 1 - side
        for z in range(planes):
            to = jnp.where(far == 1, z, planes - 1 - z)
            for g in range(rows // TILE):
                block = jnp.where(far == 1, rows // TILE - 1 - g, g)
                for h in range(2 * modes // group):
                    there = pl.ds(h * group, group)
                    x = both[a, pl.ds(g * TILE, TILE), z, there, :]
                    y = jnp.dot(turn[far], to_bf16_rows(x), preferred_element_type=F32).astype(BF16)
                    final[a, to, there, pl.ds(pl.multiple_of(block * TILE, TILE), TILE), :] = y.reshape(
                        group, TILE, cols
                    )
    copy = pltpu.make_async_copy(final.at[:, :, pl.ds((1 - core) * modes, modes)], away, sems.at[len(parts)])
    copy.start()
    outgoing.append(copy)
    outgoing += put(out, final.at[:, :, pl.ds(core * modes, modes)], side, core, begin, out_sems.at[1])
    for copy in outgoing:
        copy.wait()


def settle(pos, turn, result, pieces, parts, arrived, begin, old_begin, rows, shape):
    planes, modes, _, cols = shape
    chained = result is not None
    given = ([result] if chained else []) + list(pieces) + list(arrived)
    return pl.pallas_call(
        functools.partial(
            settle_kernel, begin=begin, old_begin=old_begin, parts=tuple(parts), arrivals=len(arrived)
        ),
        out_shape=(
            jax.ShapeDtypeStruct((2, planes, modes, rows, cols), BF16),
            jax.ShapeDtypeStruct(shape, BF16),
            TOKEN,
        ),
        in_specs=[SMEM, VMEM] + [HBM] * chained + [ANY] * len(pieces) + [VMEM] * len(arrived),
        out_specs=(ANY, HBM, SMEM),
        scratch_shapes=[
            pltpu.VMEM((2, rows, planes, 2 * modes, cols), BF16),
            pltpu.VMEM((2, planes, 2 * modes, rows, cols), BF16),
            pltpu.SemaphoreType.DMA((len(pieces) + 1,)),
            pltpu.SemaphoreType.DMA((2, 2)),
        ],
        input_output_aliases={2: 1} if chained else {},
        compiler_params=params(10),
        cost_estimate=COST,
        name="settle",
    )(pos, turn, *given)


def last_kernel(pos, result, arrived, out, sems, *, begin):
    for copy in put(out, arrived, pos[0], 1 - pos[2], begin, sems):
        copy.wait()


def last(pos, result, arrived, begin):
    return pl.pallas_call(
        functools.partial(last_kernel, begin=begin),
        out_shape=jax.ShapeDtypeStruct(result.shape, BF16),
        in_specs=[SMEM, HBM, VMEM],
        out_specs=HBM,
        scratch_shapes=[pltpu.SemaphoreType.DMA((2,))],
        input_output_aliases={1: 0},
        compiler_params=params(6),
        cost_estimate=COST,
        name="settle_last",
    )(pos, result, arrived)


SIZES = (1, 1, 2, 2, 1, 1)
GROUPS = ((0,), (1, 2, 3, 4, 5))
ENDS = ((0, 1), (2,), (3,), (4, 5))
EARLY = (1,)


def chunk_rows(quarter):
    return [n * (quarter // 8) for n in SIZES]


ORDER = (
    ("T", 0), ("T", 1), ("R", 0), ("R", 1), ("S", 0), ("R", 2), ("S", 1), ("P", 0),
    ("R", 3), ("S", 2), ("P", 1), ("C", 0), ("R", 4), ("S", 3), ("P", 2), ("C", 1), ("R", 5),
    ("S", 4), ("P", 3), ("C", 2), ("F", 0), ("S", 5), ("P", 4), ("C", 3), ("F", 1), ("P", 5), ("C", 4),
    ("F", 2), ("C", 5), ("F", 3),
)


def turns(group):
    at = np.arange(group * TILE)
    row, mode = at // group, at % group
    same = mode[:, None] == (at // TILE)[None, :]
    straight = same & (row[:, None] == (at % TILE)[None, :])
    reverse = same & (row[:, None] == TILE - 1 - (at % TILE)[None, :])
    to_rows = np.stack([straight, reverse])
    return jnp.asarray(to_rows, BF16), jnp.asarray(to_rows.transpose(0, 2, 1), BF16)


def on_device(field, diffusion, joule, basis, quad_weight, base_conductivity, thermal_slope):
    planes, modes, size, cols = field.shape
    half, quarter = size // 2, size // 4
    spaces, devices = lax.axis_size("space"), lax.axis_size("modes")
    chips = devices // 2
    pos = jnp.stack([lax.axis_index("space") % 2, lax.axis_index("modes") // 2, lax.axis_index("modes") % 2])
    pos = pos.astype(jnp.int32)

    swap = [(i, i ^ 1) for i in range(spaces)]
    ahead = [(i, i + 4 * (i % 2) - 2) for i in range(spaces)]
    ahead = [(i, j) for i, j in ahead if 0 <= j < spaces]
    back = [(j, i) for i, j in ahead]
    beyond = [(i, i - 1 if i % 2 == 0 else i + 1) for i in range(spaces)]
    beyond = [(i, j) for i, j in beyond if 0 <= j < spaces]

    def across(x):
        return lax.ppermute(x, "space", swap)

    def ahead_of(x):
        return lax.ppermute(x, "space", ahead)

    def behind_of(x):
        return lax.ppermute(x, "space", back)

    def by_core(x):
        return lax.ppermute(x, "modes", [(j, j ^ 1) for j in range(devices)])

    def exchange(pieces):
        moved = [pieces[0]]
        for k in range(1, chips):
            moved.append(lax.ppermute(pieces[k], "modes", [(j, j ^ (2 * k)) for j in range(devices)]))
        return moved

    def raw_rows(spans, pos):
        side, core = pos[0], pos[2]
        base, blocks = blocks_of(spans)
        begin = (1 - core) * (quarter + base * TILE if base < 0 else quarter)
        depth = blocks * TILE
        starts = [jnp.where(far == 1, size - depth - begin, begin) for far in (1 - side, side)]
        return jnp.stack(
            [lax.dynamic_slice(field, (0, 0, start, 0), (planes, modes, depth, cols)) for start in starts]
        )

    def logical(x, length, pos, sent):
        begin = pos[2] * quarter
        rows_back, planes_back = (
            lax.dynamic_slice_in_dim(y, begin, length, axis=1) for y in (jnp.flip(x, 1), jnp.flip(x, 0))
        )
        own = jnp.where(pos[0] == 1, rows_back, planes_back)
        return own, jnp.where(pos[0] == 1, planes_back, rows_back).astype(sent)

    def coefficients(pos):
        length = quarter + EDGE + 1
        length += -length % 8
        nothing = jnp.zeros((planes, 1, cols), F32)
        rows_back = jnp.concatenate([nothing, jnp.flip(diffusion, 1)], axis=1)
        planes_back = jnp.concatenate([nothing, jnp.flip(diffusion, 0)], axis=1)
        rows_back, planes_back = (
            lax.dynamic_slice_in_dim(x, pos[2] * quarter, length, axis=1) for x in (rows_back, planes_back)
        )
        own_rate = jnp.where(pos[0] == 1, rows_back, planes_back)
        send_rate = jnp.where(pos[0] == 1, planes_back, rows_back)
        own_load, send_load = logical(joule, quarter, pos, BF16)
        edge_rate = lax.ppermute(send_rate[:1], "space", beyond)
        rates = ahead_of(own_rate[-1:]), across(send_rate), edge_rate
        return own_rate, own_load, rates, across(send_load), (send_rate, send_load)

    to_rows, _ = turns(min(2 * modes, TILE))
    _, to_modes = turns(min(2 * modes, TILE))

    points_count = basis.shape[0]
    extra = -points_count % 32
    basis = jnp.pad(basis, ((0, extra), (0, 0)))
    basis_t = basis.T
    level = quad_weight * base_conductivity
    spread_out = lambda v: jnp.broadcast_to(jnp.pad(v, (0, extra))[:, None], (points_count + extra, LANES))
    flat, swing = spread_out(level), spread_out(level * thermal_slope)

    rows_of = chunk_rows(quarter)
    begins = [sum(rows_of[:c]) for c in range(len(rows_of))]
    edges = [(begin + EDGE if begin else -EDGE, begin + rows + EDGE) for begin, rows in zip(begins, rows_of)]
    groups = [[edges[n] for n in those] for those in GROUPS]
    raws = [by_core(raw_rows(spans, pos)) for spans in groups]
    own, other, before, blocks, cells, home, theirs = {}, {}, {}, {}, {}, {}, {}
    result, arrived, old_begin = None, (), 0
    for kind, c in ORDER:
        if kind == "T":
            after = ()
            if c == 0:
                own_rate, own_load, rates, other_load, after = coefficients(pos)
            elif c == 1:
                after = (*[rates[n] for n in EARLY], basis, basis_t, flat, swing)
            *pieces, pos = spread(pos, field, raws[c], to_rows, after, groups[c])
            for n in GROUPS[c]:
                send, own[n], *pieces = pieces
                other[n], before[n] = across(send), ahead_of(own[n])
        elif kind == "R":
            if c == 0:
                after = (before[c], *[rates[n] for n in range(3) if n not in EARLY])
                other[c], pos = relay(pos, (other[c],), after)
                rate = jnp.concatenate([rates[0], rates[1], own_rate, rates[2]], axis=0)
            elif c == 1:
                other[c], other_load, pos = relay(pos, (other[c], other_load), (before[c],))
                load = jnp.concatenate([other_load.astype(F32), own_load], axis=0)
            else:
                other[c], pos = relay(pos, (other[c],), (before[c],))
            blocks[c] = (before[c], other[c], own[c], behind_of(other[c]))
        elif kind == "S":
            *pieces, pos = sweep(pos, rate, blocks[c], blocks.get(c - 1, ()), begins[c], rows_of[c], chips)
            cells[c] = exchange(pieces)
        elif kind == "P":
            *stepped, pos = points(pos, basis, basis_t, flat, swing, load, cells[c], begins[c])
            home[c] = exchange(stepped)
        elif kind == "C":
            out, pos = collect(pos, home[c])
            theirs[c] = across(out)
        else:
            begin, rows = begins[ENDS[c][0]], sum(rows_of[n] for n in ENDS[c])
            pieces, parts = [], []
            for n in ENDS[c]:
                at = begins[n] - begin
                pieces += [*home[n], theirs[n]]
                parts += [(0, at, k, planes) for k in range(chips)] + [(1, at, None, 0)]
            away, result, pos = settle(
                pos, to_modes, result, pieces, parts, arrived, begin, old_begin, rows, field.shape
            )
            arrived, old_begin = (by_core(away),), begin
    return last(pos, result, arrived[0], old_begin)


def solution(mesh):
    return jax.shard_map(
        on_device,
        mesh=mesh,
        in_specs=(
            P("space", "modes", None, None),
            P("space", None, None),
            P("space", None, None),
            P(),
            P(),
            P(),
            P(),
        ),
        out_specs=P("space", "modes", None, None),
        check_vma=False,
    )
```

```python
import functools

import jax
import jax.numpy as jnp
import numpy as np
from jax import lax
from jax.experimental import pallas as pl
from jax.experimental.pallas import tpu as pltpu
from jax.sharding import PartitionSpec as P

F32, BF16 = jnp.float32, jnp.bfloat16
ANY = pl.BlockSpec(memory_space=pl.ANY)
VMEM = pl.BlockSpec(memory_space=pltpu.VMEM)
HBM = pl.BlockSpec(memory_space=pltpu.HBM)
SMEM = pl.BlockSpec(memory_space=pltpu.SMEM)
TOKEN = jax.ShapeDtypeStruct((3,), jnp.int32)
COST = pl.CostEstimate(flops=1, bytes_accessed=1, transcendentals=0)
EDGE = 2
TILE = 16
LANES = 128


def params(mebibytes):
    return pltpu.CompilerParams(vmem_limit_bytes=mebibytes * 1024 * 1024)


def from_rows(y, group):
    if group % 16 == 0:
        return y.astype(BF16).reshape(-1, group, y.shape[1])
    return y.reshape(-1, group, y.shape[1]).astype(BF16)


def hand_on(pos, token):
    for n in range(3):
        token[n] = pos[n]


def to_bf16_rows(x):
    a, m, y = x.shape
    if m % 16 == 0:
        return x.astype(BF16).reshape(a * m, y)
    return x.astype(F32).reshape(a * m, y).astype(BF16)


def raw_copies(pos, field, raw, sems, base):
    side, core = pos[0], pos[2]
    size, depth = field.shape[2], raw.shape[3]
    begin = (1 - core) * (size // 4 + min(base, 0) * TILE)
    copies = []
    for a in range(2):
        far = 1 - side if a == 0 else side
        start = pl.multiple_of(jnp.where(far == 1, size - depth - begin, begin), TILE)
        copies.append(pltpu.make_async_copy(field.at[:, :, pl.ds(start, depth), :], raw.at[a], sems.at[a]))
    for copy in copies:
        copy.start()
    return copies


def raw_kernel(pos, field, raw, token, sems, *, base):
    hand_on(pos, token)
    for copy in raw_copies(pos, field, raw, sems, base):
        copy.wait()


def prepare_kernel(pos, field, diffusion, joule, raw, own_rate, send_rate, own_load, send_load, token, sems, *, base):
    hand_on(pos, token)
    copies = raw_copies(pos, field, raw, sems, base)
    side, core = pos[0], pos[2]
    planes, size, _ = diffusion.shape
    begin = core * (size // 4)
    for far, rate, load in ((side, own_rate, own_load), (1 - side, send_rate, send_load)):
        for source, out, first in ((diffusion, rate, begin - 1), (joule, load, begin)):

            def row(r, _):
                place = jnp.maximum(first + r, 0)
                place = jnp.where(far == 1, size - 1 - place, place)
                for z in range(planes):
                    to = jnp.where(far == 1, z, planes - 1 - z)
                    out[to, pl.ds(r, 1), :] = source[z, pl.ds(place, 1), :]
                return 0

            lax.fori_loop(0, out.shape[1], row, 0)
        for z in range(planes):
            rate[z, pl.ds(0, 1), :] = jnp.where(core == 1, rate[z, pl.ds(0, 1), :], 0.0)
    for copy in copies:
        copy.wait()


def raw_shape(field, spans):
    planes, modes, _, cols = field.shape
    return jax.ShapeDtypeStruct((2, planes, modes, blocks_of(spans)[1] * TILE, cols), BF16)


def raw_rows(pos, field, spans):
    return pl.pallas_call(
        functools.partial(raw_kernel, base=blocks_of(spans)[0]),
        out_shape=(raw_shape(field, spans), TOKEN),
        in_specs=[SMEM, HBM],
        out_specs=(VMEM, SMEM),
        scratch_shapes=[pltpu.SemaphoreType.DMA((2,))],
        compiler_params=params(48),
        cost_estimate=COST,
        name="raw",
    )(pos, field)


def prepare(pos, field, diffusion, joule, spans):
    planes, size, cols = diffusion.shape
    length = size // 4 + EDGE + 1
    rate = jax.ShapeDtypeStruct((planes, length + -length % 8, cols), F32)
    load = jax.ShapeDtypeStruct((planes, size // 4, cols), F32)
    return pl.pallas_call(
        functools.partial(prepare_kernel, base=blocks_of(spans)[0]),
        out_shape=(raw_shape(field, spans), rate, rate, load, load, TOKEN),
        in_specs=[SMEM, HBM, VMEM, VMEM],
        out_specs=(VMEM,) * 5 + (SMEM,),
        scratch_shapes=[pltpu.SemaphoreType.DMA((2,))],
        compiler_params=params(48),
        cost_estimate=COST,
        name="prepare",
    )(pos, field, diffusion, joule)


def spread_kernel(pos, field, raw, turn, *refs, spans, base, raw_base):
    outs, (token, window, sems) = refs[-3 - 2 * len(spans) : -3], refs[-3:]
    side, core = pos[0], pos[2]
    hand_on(pos, token)
    blocks, _, planes, modes, _, cols = window.shape
    modes = modes // 2
    size = field.shape[2]
    quarter = size // 4
    depth = raw.shape[3]
    group = turn.shape[1] // TILE
    copies = {}
    for g in range(blocks):
        for a in range(2):
            far = 1 - side if a == 0 else side
            begin = core * quarter + (base + g) * TILE
            there = base + g + (core if raw_base < 0 else -raw_base)
            if base + g < 0:
                begin, there = jnp.maximum(begin, 0), jnp.maximum(there, 0)
            start = pl.multiple_of(jnp.where(far == 1, size - TILE - begin, begin), TILE)
            place = pl.multiple_of(jnp.where(far == 1, depth - TILE * (there + 1), TILE * there), TILE)
            copies[g, a] = (
                pltpu.make_async_copy(
                    field.at[:, :, pl.ds(start, TILE), :],
                    window.at[g, a, :, pl.ds(core * modes, modes)],
                    sems.at[g, a, 0],
                ),
                pltpu.make_async_copy(
                    raw.at[a, :, :, pl.ds(place, TILE), :],
                    window.at[g, a, :, pl.ds((1 - core) * modes, modes)],
                    sems.at[g, a, 1],
                ),
            )
            for copy in copies[g, a]:
                copy.start()
    for g in range(blocks):
        for a in range(2):
            far = 1 - side if a == 0 else side
            for copy in copies[g, a]:
                copy.wait()
            for z in range(planes):
                to = jnp.where(far == 1, z, planes - 1 - z)
                for h in range(2 * modes // group):
                    there = pl.ds(h * group, group)
                    x = window[g, a, z, there]
                    y = jnp.dot(turn[far], x.reshape(group * TILE, cols), preferred_element_type=F32)
                    if base + g < 0:
                        y = jnp.where(core == 1, y, 0.0)
                    y = from_rows(y, group)
                    for n, (first, last) in enumerate(spans):
                        low, high = (min(max(r - (base + g) * TILE, 0), TILE) for r in (first, last))
                        if low < high:
                            at = (base + g) * TILE + low - first
                            outs[2 * n + a][pl.ds(at, high - low), to, there, :] = y[low:high]


def blocks_of(spans):
    base = spans[0][0] // TILE
    return base, -(-spans[-1][1] // TILE) - base


def spread(pos, field, raw, turn, after, spans, raw_base):
    planes, modes, _, cols = field.shape
    pieces = [jax.ShapeDtypeStruct((last - first, planes, 2 * modes, cols), BF16) for first, last in spans]
    pieces = [piece for piece in pieces for _ in range(2)]
    base, blocks = blocks_of(spans)
    return pl.pallas_call(
        functools.partial(spread_kernel, spans=spans, base=base, raw_base=raw_base),
        out_shape=(*pieces, TOKEN),
        in_specs=[SMEM, HBM, ANY, VMEM] + [ANY] * len(after),
        out_specs=(VMEM,) * len(pieces) + (SMEM,),
        scratch_shapes=[
            pltpu.VMEM((blocks, 2, planes, 2 * modes, TILE, cols), BF16),
            pltpu.SemaphoreType.DMA((blocks, 2, 2)),
        ],
        compiler_params=params(48),
        cost_estimate=COST,
        name="spread",
    )(pos, field, raw, turn, *after)


def relay_kernel(pos, *refs):
    token = refs[-1]
    hand_on(pos, token)


def relay(pos, passed, after):
    count = len(passed)
    return pl.pallas_call(
        relay_kernel,
        out_shape=tuple(jax.ShapeDtypeStruct(x.shape, x.dtype) for x in passed) + (TOKEN,),
        in_specs=[SMEM] + [ANY] * (count + len(after)),
        out_specs=(ANY,) * count + (SMEM,),
        input_output_aliases={1 + i: i for i in range(count)},
        compiler_params=params(1),
        cost_estimate=COST,
        name="relay",
    )(pos, *passed, *after)


def sweep_kernel(pos, *refs, begin, count, heads):
    group = 4
    rates, refs = refs[:group], refs[group:]
    blocks, refs = refs[:group], refs[group:]
    tails, refs = refs[:heads], refs[heads:]
    outs, (token, first, edge, sems) = refs[:count], refs[count:]
    hand_on(pos, token)
    planes, modes, cols = blocks[0].shape[1:]
    mine = 2 * planes
    part = outs[0].shape[0]
    rows = part * count
    lead = 2 * EDGE if heads else 0
    copies = []
    for g in range(heads):
        length = tails[g].shape[0]
        copies.append(
            pltpu.make_async_copy(
                tails[g].at[pl.ds(length - lead, lead)], edge.at[:, pl.ds(g * planes, planes)], sems.at[g]
            )
        )
    for copy in copies:
        copy.start()
    for copy in copies:
        copy.wait()
    low = planes - 1
    wide = mine + 2
    piece = min(modes, 16)
    rate = [(rates[0], 0)] + [(rates[1 + p // planes], p % planes) for p in range(mine)] + [(rates[3], 0)]

    def speed(p, row):
        ref, plane = rate[p]
        return ref[plane, pl.ds(row, 1), :]

    def field(row, p, some):
        if isinstance(row, int) and row < lead:
            return edge[row, p, some]
        return blocks[p // planes][row - lead, p % planes, some]

    def beside(x):
        parts = [x[:, h * LANES : (h + 1) * LANES] for h in range(cols // LANES)]
        up = [pltpu.roll(part, 1, 1) for part in parts]
        down = [pltpu.roll(part, LANES - 1, 1) for part in parts]
        lane = lax.broadcasted_iota(jnp.int32, parts[0].shape, 1)
        nothing = jnp.zeros_like(parts[0])
        sums = []
        for h in range(len(parts)):
            left = jnp.where(lane == 0, up[h - 1] if h else nothing, up[h])
            right = jnp.where(lane == LANES - 1, down[h + 1] if h + 1 < len(parts) else nothing, down[h])
            sums.append(left + right)
        return jnp.concatenate(sums, axis=1)

    def once(i, number):
        for a in range(number):
            speeds = [speed(p, begin + i + a) for p in range(wide)]
            for h in range(modes // piece):
                some = pl.ds(h * piece, piece)
                line = [field(i + 1 + a, low - 1 + p, some).astype(F32) for p in range(wide + 2)]
                for p in range(wide):
                    centre = line[p + 1]
                    around = beside(centre) + (line[p] + line[p + 2])
                    around = around + (
                        field(i + a, low + p, some).astype(F32) + field(i + 2 + a, low + p, some).astype(F32)
                    )
                    first[i + a, p, some] = centre + speeds[p] * (around - 6.0 * centre)

    for i in range(0, lead, 2):
        once(i, 2)

    def pair(j, _):
        once(lead + 2 * j, 2)
        return 0

    lax.fori_loop(0, (rows + 2 - lead) // 2, pair, 0)
    number = 2 if part % 2 == 0 else 1
    for k in range(count):
        base = jnp.bitwise_xor(pos[1], k) * part

        def again(j, _):
            i = base + number * j
            for a in range(number):
                speeds = [speed(p + 1, begin + i + a + 1) for p in range(mine)]
                for h in range(modes // piece):
                    some = pl.ds(h * piece, piece)
                    line = [first[i + 1 + a, p, some] for p in range(wide)]
                    for p in range(mine):
                        centre = line[p + 1]
                        around = beside(centre) + (line[p] + line[p + 2])
                        around = around + (first[i + a, p + 1, some] + first[i + 2 + a, p + 1, some])
                        outs[k][number * j + a, p, some] = (
                            centre + speeds[p] * (around - 6.0 * centre)
                        ).astype(BF16)
            return 0

        lax.fori_loop(0, part // number, again, 0)


def sweep(pos, rates, blocks, tails, begin, rows, count):
    _, planes, modes, cols = blocks[0].shape
    mine = 2 * planes
    piece = jax.ShapeDtypeStruct((rows // count, mine, modes, cols), BF16)
    return pl.pallas_call(
        functools.partial(sweep_kernel, begin=begin, count=count, heads=len(tails)),
        out_shape=(piece,) * count + (TOKEN,),
        in_specs=[SMEM] + [VMEM] * 8 + [ANY] * len(tails),
        out_specs=(VMEM,) * count + (SMEM,),
        scratch_shapes=[
            pltpu.VMEM((rows + 2, mine + 2, modes, cols), F32),
            pltpu.VMEM((2 * EDGE, 4 * planes, modes, cols), BF16),
            pltpu.SemaphoreType.DMA((4,)),
        ],
        compiler_params=params(22),
        cost_estimate=COST,
        name="sweep",
    )(pos, *rates, *blocks, *tails)


def points_kernel(pos, basis, basis_t, flat, swing, other_load, own_load, *refs, begin):
    *refs, token, gathered, stepped = refs
    hand_on(pos, token)
    count = len(refs) // 2
    blocks, outs = refs[:count], refs[count:]
    part, planes, modes, cols = blocks[0].shape
    copies = cols // flat.shape[1]
    places = [pl.multiple_of(jnp.bitwise_xor(pos[1], k) * modes, modes) for k in range(count)]

    def row(i, _):
        place = begin + pos[1] * part + i
        for p in range(planes):
            for k in range(count):
                gathered[p, pl.ds(places[k], modes)] = blocks[k][i, p].astype(gathered.dtype)
            cells = gathered[p].astype(BF16)
            half = planes // 2
            load = other_load if p < half else own_load
            heat = jnp.tanh(jnp.dot(basis[...], cells, preferred_element_type=F32))
            offset = jnp.concatenate([flat[...]] * copies, axis=1)
            slope = jnp.concatenate([swing[...]] * copies, axis=1)
            weighted = (offset + slope * heat).astype(BF16)
            source = jnp.dot(basis_t[...], weighted, preferred_element_type=F32).astype(BF16).astype(F32)
            done = cells.astype(F32) + load[p % half, pl.ds(place, 1), :] * source
            stepped[p] = done.astype(stepped.dtype)
            for k in range(count):
                outs[k][i, p] = stepped[p, pl.ds(places[k], modes)].astype(BF16)
        return 0

    lax.fori_loop(0, part, row, 0)


def points(pos, basis, basis_t, flat, swing, loads, blocks, begin):
    count = len(blocks)
    _, planes, modes, cols = blocks[0].shape
    kept = BF16 if modes % 16 == 0 else F32
    return pl.pallas_call(
        functools.partial(points_kernel, begin=begin),
        out_shape=tuple(jax.ShapeDtypeStruct(block.shape, BF16) for block in blocks) + (TOKEN,),
        in_specs=[SMEM] + [VMEM] * (6 + count),
        out_specs=(VMEM,) * count + (SMEM,),
        scratch_shapes=[pltpu.VMEM((planes, modes * count, cols), kept)] * 2,
        compiler_params=params(14),
        cost_estimate=COST,
        name="points",
    )(pos, basis, basis_t, flat, swing, *loads, *blocks)


def collect_kernel(pos, *refs):
    *blocks, out, token, sems = refs
    hand_on(pos, token)
    part, planes = blocks[0].shape[0], out.shape[1]
    copies = []
    for k, block in enumerate(blocks):
        base = jnp.bitwise_xor(pos[1], k) * part
        copies.append(
            pltpu.make_async_copy(block.at[:, pl.ds(0, planes)], out.at[pl.ds(base, part)], sems.at[k])
        )
    for copy in copies:
        copy.start()
    for copy in copies:
        copy.wait()


def collect(pos, blocks):
    part, planes, modes, cols = blocks[0].shape
    count = len(blocks)
    shape = (part * count, planes // 2, modes, cols)
    return pl.pallas_call(
        collect_kernel,
        out_shape=(jax.ShapeDtypeStruct(shape, BF16), TOKEN),
        in_specs=[SMEM] + [ANY] * count,
        out_specs=(VMEM, SMEM),
        scratch_shapes=[pltpu.SemaphoreType.DMA((count,))],
        compiler_params=params(6),
        cost_estimate=COST,
        name="collect",
    )(pos, *blocks)


def put(out, source, side, core, begin, sems):
    rows, size = source.shape[3], out.shape[2]
    begin = core * (size // 4) + begin
    copies = []
    for a in range(2):
        far = side if a == 0 else 1 - side
        start = pl.multiple_of(jnp.where(far == 1, size - rows - begin, begin), TILE)
        copies.append(pltpu.make_async_copy(source.at[a], out.at[:, :, pl.ds(start, rows), :], sems.at[a]))
    for copy in copies:
        copy.start()
    return copies


def settle_kernel(pos, turn, *refs, begin, old_begin, parts, arrivals):
    refs = refs[-len(parts) - 7 - arrivals :]
    pieces, arrived, refs = refs[: len(parts)], refs[len(parts) : len(parts) + arrivals], refs[-7:]
    away, out, token, both, final, sems, out_sems = refs
    hand_on(pos, token)
    side, core = pos[0], pos[2]
    _, rows, planes, modes, cols = both.shape
    modes = modes // 2
    group = turn.shape[1] // TILE
    outgoing = put(out, arrived[0], side, 1 - core, old_begin, out_sems.at[0]) if arrivals else []
    incoming = []
    for n, (piece, (a, at, xor, low)) in enumerate(zip(pieces, parts)):
        length = piece.shape[0]
        if xor is not None:
            at = at + jnp.bitwise_xor(pos[1], xor) * length
        copy = pltpu.make_async_copy(
            piece.at[:, pl.ds(low, planes)], both.at[a, pl.ds(at, length)], sems.at[n]
        )
        copy.start()
        incoming.append(copy)
    for a in (0, 1):
        for copy, part in zip(incoming, parts):
            if part[0] == a:
                copy.wait()
        far = side if a == 0 else 1 - side
        for z in range(planes):
            to = jnp.where(far == 1, z, planes - 1 - z)
            for g in range(rows // TILE):
                block = jnp.where(far == 1, rows // TILE - 1 - g, g)
                for h in range(2 * modes // group):
                    there = pl.ds(h * group, group)
                    x = both[a, pl.ds(g * TILE, TILE), z, there, :]
                    y = jnp.dot(turn[far], to_bf16_rows(x), preferred_element_type=F32).astype(BF16)
                    final[a, to, there, pl.ds(pl.multiple_of(block * TILE, TILE), TILE), :] = y.reshape(
                        group, TILE, cols
                    )
    copy = pltpu.make_async_copy(final.at[:, :, pl.ds((1 - core) * modes, modes)], away, sems.at[len(parts)])
    copy.start()
    outgoing.append(copy)
    outgoing += put(out, final.at[:, :, pl.ds(core * modes, modes)], side, core, begin, out_sems.at[1])
    for copy in outgoing:
        copy.wait()


def settle(pos, turn, result, pieces, parts, arrived, begin, old_begin, rows, shape):
    planes, modes, _, cols = shape
    chained = result is not None
    given = ([result] if chained else []) + list(pieces) + list(arrived)
    return pl.pallas_call(
        functools.partial(
            settle_kernel, begin=begin, old_begin=old_begin, parts=tuple(parts), arrivals=len(arrived)
        ),
        out_shape=(
            jax.ShapeDtypeStruct((2, planes, modes, rows, cols), BF16),
            jax.ShapeDtypeStruct(shape, BF16),
            TOKEN,
        ),
        in_specs=[SMEM, VMEM] + [HBM] * chained + [ANY] * len(pieces) + [VMEM] * len(arrived),
        out_specs=(ANY, HBM, SMEM),
        scratch_shapes=[
            pltpu.VMEM((2, rows, planes, 2 * modes, cols), BF16),
            pltpu.VMEM((2, planes, 2 * modes, rows, cols), BF16),
            pltpu.SemaphoreType.DMA((len(pieces) + 1,)),
            pltpu.SemaphoreType.DMA((2, 2)),
        ],
        input_output_aliases={2: 1} if chained else {},
        compiler_params=params(10),
        cost_estimate=COST,
        name="settle",
    )(pos, turn, *given)


def last_kernel(pos, result, arrived, out, sems, *, begin):
    for copy in put(out, arrived, pos[0], 1 - pos[2], begin, sems):
        copy.wait()


def last(pos, result, arrived, begin):
    return pl.pallas_call(
        functools.partial(last_kernel, begin=begin),
        out_shape=jax.ShapeDtypeStruct(result.shape, BF16),
        in_specs=[SMEM, HBM, VMEM],
        out_specs=HBM,
        scratch_shapes=[pltpu.SemaphoreType.DMA((2,))],
        input_output_aliases={1: 0},
        compiler_params=params(6),
        cost_estimate=COST,
        name="settle_last",
    )(pos, result, arrived)


SIZES = (1, 1, 1, 1, 1, 1, 1, 1)
GROUPS = ((0,), (1,), (2, 3), (4, 5), (6, 7))
ENDS = ((0, 1), (2, 3), (4, 5), (6, 7))


def chunk_rows(quarter):
    return [n * (quarter // 8) for n in SIZES]


ORDER = (
    ("N", 0), ("T", 0), ("N", 1), ("T", 1), ("R", 0), ("T", 2), ("R", 1), ("S", 0), ("R", 2), ("S", 1),
    ("P", 0), ("T", 3), ("R", 3), ("S", 2), ("P", 1), ("C", 0), ("R", 4), ("S", 3), ("P", 2), ("C", 1),
    ("T", 4), ("R", 5), ("S", 4), ("P", 3), ("C", 2), ("F", 0), ("R", 6), ("S", 5), ("P", 4), ("C", 3),
    ("R", 7), ("S", 6), ("P", 5), ("C", 4), ("F", 1), ("S", 7), ("P", 6), ("C", 5), ("P", 7), ("C", 6),
    ("F", 2), ("C", 7), ("F", 3),
)


def turns(group):
    at = np.arange(group * TILE)
    row, mode = at // group, at % group
    same = mode[:, None] == (at // TILE)[None, :]
    straight = same & (row[:, None] == (at % TILE)[None, :])
    reverse = same & (row[:, None] == TILE - 1 - (at % TILE)[None, :])
    to_rows = np.stack([straight, reverse])
    return jnp.asarray(to_rows, BF16), jnp.asarray(to_rows.transpose(0, 2, 1), BF16)


def on_device(field, diffusion, joule, basis, quad_weight, base_conductivity, thermal_slope):
    planes, modes, size, cols = field.shape
    half, quarter = size // 2, size // 4
    spaces, devices = lax.axis_size("space"), lax.axis_size("modes")
    chips = devices // 2
    pos = jnp.stack([lax.axis_index("space") % 2, lax.axis_index("modes") // 2, lax.axis_index("modes") % 2])
    pos = pos.astype(jnp.int32)

    swap = [(i, i ^ 1) for i in range(spaces)]
    ahead = [(i, i + 4 * (i % 2) - 2) for i in range(spaces)]
    ahead = [(i, j) for i, j in ahead if 0 <= j < spaces]
    back = [(j, i) for i, j in ahead]
    beyond = [(i, i - 1 if i % 2 == 0 else i + 1) for i in range(spaces)]
    beyond = [(i, j) for i, j in beyond if 0 <= j < spaces]

    def across(x):
        return lax.ppermute(x, "space", swap)

    def ahead_of(x):
        return lax.ppermute(x, "space", ahead)

    def behind_of(x):
        return lax.ppermute(x, "space", back)

    def by_core(x):
        return lax.ppermute(x, "modes", [(j, j ^ 1) for j in range(devices)])

    def exchange(pieces):
        moved = [pieces[0]]
        for k in range(1, chips):
            moved.append(lax.ppermute(pieces[k], "modes", [(j, j ^ (2 * k)) for j in range(devices)]))
        return moved

    to_rows, _ = turns(min(2 * modes, TILE))
    _, to_modes = turns(min(2 * modes, TILE))

    points_count = basis.shape[0]
    extra = -points_count % 32
    basis = jnp.pad(basis, ((0, extra), (0, 0)))
    basis_t = basis.T
    level = quad_weight * base_conductivity
    spread_out = lambda v: jnp.broadcast_to(jnp.pad(v, (0, extra))[:, None], (points_count + extra, LANES))
    flat, swing = spread_out(level), spread_out(level * thermal_slope)

    rows_of = chunk_rows(quarter)
    begins = [sum(rows_of[:c]) for c in range(len(rows_of))]
    edges = [(begin + EDGE if begin else -EDGE, begin + rows + EDGE) for begin, rows in zip(begins, rows_of)]
    groups = [[edges[n] for n in those] for those in GROUPS]
    raw_groups = groups[0], edges[len(GROUPS[0]) :]
    raws, own, other, before, blocks, cells, home, theirs = {}, {}, {}, {}, {}, {}, {}, {}
    result, arrived, old_begin = None, (), 0
    for kind, c in ORDER:
        if kind == "N":
            if c == 0:
                raw, own_rate, send_rate, own_load, send_load, pos = prepare(pos, field, diffusion, joule, raw_groups[c])
                raws[c] = by_core(raw)
                rates = (ahead_of(own_rate[-1:]), across(send_rate), own_rate, lax.ppermute(send_rate[:1], "space", beyond))
            else:
                raw, pos = raw_rows(pos, field, raw_groups[c])
                raws[c] = by_core(raw)
        elif kind == "T":
            after = ((), rates, (basis, basis_t, flat, swing))[c + 1 if c < 2 else 0]
            *pieces, pos = spread(pos, field, raws[c > 0], to_rows, after, groups[c], blocks_of(raw_groups[c > 0])[0])
            for n in GROUPS[c]:
                send, own[n], *pieces = pieces
                other[n], before[n] = across(send), ahead_of(own[n])
            if c == 0:
                other_load = across(send_load)
        elif kind == "R":
            other[c], pos = relay(pos, (other[c],), (before[c],))
            blocks[c] = (before[c], other[c], own[c], behind_of(other[c]))
        elif kind == "S":
            *pieces, pos = sweep(pos, rates, blocks[c], blocks.get(c - 1, ()), begins[c], rows_of[c], chips)
            cells[c] = exchange(pieces)
        elif kind == "P":
            *stepped, pos = points(pos, basis, basis_t, flat, swing, (other_load, own_load), cells[c], begins[c])
            home[c] = exchange(stepped)
        elif kind == "C":
            out, pos = collect(pos, home[c])
            theirs[c] = across(out)
        else:
            begin, rows = begins[ENDS[c][0]], sum(rows_of[n] for n in ENDS[c])
            pieces, parts = [], []
            for n in ENDS[c]:
                at = begins[n] - begin
                pieces += [*home[n], theirs[n]]
                parts += [(0, at, k, planes) for k in range(chips)] + [(1, at, None, 0)]
            away, result, pos = settle(
                pos, to_modes, result, pieces, parts, arrived, begin, old_begin, rows, field.shape
            )
            arrived, old_begin = (by_core(away),), begin
    return last(pos, result, arrived[0], old_begin)


def solution(mesh):
    return jax.shard_map(
        on_device,
        mesh=mesh,
        in_specs=(
            P("space", "modes", None, None),
            P("space", None, None),
            P("space", None, None),
            P(),
            P(),
            P(),
            P(),
        ),
        out_specs=P("space", "modes", None, None),
        check_vma=False,
    )
```

```python
import functools

import jax
import jax.numpy as jnp
import numpy as np
from jax import lax
from jax.experimental import pallas as pl
from jax.experimental.pallas import tpu as pltpu
from jax.sharding import PartitionSpec as P

F32, BF16 = jnp.float32, jnp.bfloat16
ANY = pl.BlockSpec(memory_space=pl.ANY)
VMEM = pl.BlockSpec(memory_space=pltpu.VMEM)
HBM = pl.BlockSpec(memory_space=pltpu.HBM)
SMEM = pl.BlockSpec(memory_space=pltpu.SMEM)
TOKEN = jax.ShapeDtypeStruct((3,), jnp.int32)
COST = pl.CostEstimate(flops=1, bytes_accessed=1, transcendentals=0)
EDGE = 2
TILE = 16
LANES = 128


def params(mebibytes):
    return pltpu.CompilerParams(vmem_limit_bytes=mebibytes * 1024 * 1024)


def from_rows(y, group):
    if group % 16 == 0:
        return y.astype(BF16).reshape(-1, group, y.shape[1])
    return y.reshape(-1, group, y.shape[1]).astype(BF16)


def hand_on(pos, token):
    for n in range(3):
        token[n] = pos[n]


def to_bf16_rows(x):
    a, m, y = x.shape
    if m % 16 == 0:
        return x.astype(BF16).reshape(a * m, y)
    return x.astype(F32).reshape(a * m, y).astype(BF16)


def raw_copies(pos, field, raw, sems, base):
    side, core = pos[0], pos[2]
    size, depth = field.shape[2], raw.shape[3]
    begin = (1 - core) * (size // 4 + min(base, 0) * TILE) + max(base, 0) * TILE
    copies = []
    for a in range(2):
        far = 1 - side if a == 0 else side
        start = pl.multiple_of(jnp.where(far == 1, size - depth - begin, begin), TILE)
        copies.append(pltpu.make_async_copy(field.at[:, :, pl.ds(start, depth), :], raw.at[a], sems.at[a]))
    for copy in copies:
        copy.start()
    return copies


def prepare_kernel(pos, field, diffusion, joule, raw, own_rate, send_rate, own_load, send_load, token, sems, *, base):
    hand_on(pos, token)
    copies = raw_copies(pos, field, raw, sems, base)
    side, core = pos[0], pos[2]
    planes, size, _ = diffusion.shape
    begin = core * (size // 4)
    for far, rate, load in ((side, own_rate, own_load), (1 - side, send_rate, send_load)):
        for source, out, first in ((diffusion, rate, begin - 1), (joule, load, begin)):

            def row(r, _):
                place = jnp.maximum(first + r, 0)
                place = jnp.where(far == 1, size - 1 - place, place)
                for z in range(planes):
                    to = jnp.where(far == 1, z, planes - 1 - z)
                    out[to, pl.ds(r, 1), :] = source[z, pl.ds(place, 1), :]
                return 0

            lax.fori_loop(0, out.shape[1], row, 0)
        for z in range(planes):
            rate[z, pl.ds(0, 1), :] = jnp.where(core == 1, rate[z, pl.ds(0, 1), :], 0.0)
    for copy in copies:
        copy.wait()


def raw_shape(field, spans):
    planes, modes, _, cols = field.shape
    return jax.ShapeDtypeStruct((2, planes, modes, blocks_of(spans)[1] * TILE, cols), BF16)


def prepare(pos, field, diffusion, joule, spans):
    planes, size, cols = diffusion.shape
    length = size // 4 + EDGE + 1
    rate = jax.ShapeDtypeStruct((planes, length + -length % 8, cols), F32)
    load = jax.ShapeDtypeStruct((planes, size // 4, cols), F32)
    return pl.pallas_call(
        functools.partial(prepare_kernel, base=blocks_of(spans)[0]),
        out_shape=(raw_shape(field, spans), rate, rate, load, load, TOKEN),
        in_specs=[SMEM, HBM, VMEM, VMEM],
        out_specs=(VMEM,) * 5 + (SMEM,),
        scratch_shapes=[pltpu.SemaphoreType.DMA((2,))],
        compiler_params=params(48),
        cost_estimate=COST,
        name="prepare",
    )(pos, field, diffusion, joule)


def spread_kernel(pos, field, raw, turn, *refs, spans, base, raw_base, next_base):
    *refs, token, window, sems, raw_sems = refs
    coming = []
    if next_base is not None:
        *refs, coming = refs
        coming = raw_copies(pos, field, coming, raw_sems, next_base)
    outs = refs[-2 * len(spans) :]
    side, core = pos[0], pos[2]
    hand_on(pos, token)
    blocks, _, planes, modes, _, cols = window.shape
    modes = modes // 2
    size = field.shape[2]
    quarter = size // 4
    depth = raw.shape[3]
    group = turn.shape[1] // TILE
    copies = {}
    for g in range(blocks):
        for a in range(2):
            far = 1 - side if a == 0 else side
            begin = core * quarter + (base + g) * TILE
            there = base + g + (core if raw_base < 0 else -raw_base)
            if base + g < 0:
                begin, there = jnp.maximum(begin, 0), jnp.maximum(there, 0)
            start = pl.multiple_of(jnp.where(far == 1, size - TILE - begin, begin), TILE)
            place = pl.multiple_of(jnp.where(far == 1, depth - TILE * (there + 1), TILE * there), TILE)
            copies[g, a] = (
                pltpu.make_async_copy(
                    field.at[:, :, pl.ds(start, TILE), :],
                    window.at[g, a, :, pl.ds(core * modes, modes)],
                    sems.at[g, a, 0],
                ),
                pltpu.make_async_copy(
                    raw.at[a, :, :, pl.ds(place, TILE), :],
                    window.at[g, a, :, pl.ds((1 - core) * modes, modes)],
                    sems.at[g, a, 1],
                ),
            )
            for copy in copies[g, a]:
                copy.start()
    for g in range(blocks):
        for a in range(2):
            far = 1 - side if a == 0 else side
            for copy in copies[g, a]:
                copy.wait()
            for z in range(planes):
                to = jnp.where(far == 1, z, planes - 1 - z)
                for h in range(2 * modes // group):
                    there = pl.ds(h * group, group)
                    x = window[g, a, z, there]
                    y = jnp.dot(turn[far], x.reshape(group * TILE, cols), preferred_element_type=F32)
                    if base + g < 0:
                        y = jnp.where(core == 1, y, 0.0)
                    y = from_rows(y, group)
                    for n, (first, last) in enumerate(spans):
                        low, high = (min(max(r - (base + g) * TILE, 0), TILE) for r in (first, last))
                        if low < high:
                            at = (base + g) * TILE + low - first
                            outs[2 * n + a][pl.ds(at, high - low), to, there, :] = y[low:high]
    for copy in coming:
        copy.wait()


def blocks_of(spans):
    base = spans[0][0] // TILE
    return base, -(-spans[-1][1] // TILE) - base


def spread(pos, field, raw, turn, after, spans, raw_spans, next_spans):
    planes, modes, _, cols = field.shape
    pieces = [jax.ShapeDtypeStruct((last - first, planes, 2 * modes, cols), BF16) for first, last in spans]
    pieces = [piece for piece in pieces for _ in range(2)]
    if next_spans:
        pieces.append(raw_shape(field, next_spans))
    base, blocks = blocks_of(spans)
    next_base = blocks_of(next_spans)[0] if next_spans else None
    return pl.pallas_call(
        functools.partial(
            spread_kernel, spans=spans, base=base, raw_base=blocks_of(raw_spans)[0], next_base=next_base
        ),
        out_shape=(*pieces, TOKEN),
        in_specs=[SMEM, HBM, ANY, VMEM] + [ANY] * len(after),
        out_specs=(VMEM,) * len(pieces) + (SMEM,),
        scratch_shapes=[
            pltpu.VMEM((blocks, 2, planes, 2 * modes, TILE, cols), BF16),
            pltpu.SemaphoreType.DMA((blocks, 2, 2)),
            pltpu.SemaphoreType.DMA((2,)),
        ],
        compiler_params=params(48),
        cost_estimate=COST,
        name="spread",
    )(pos, field, raw, turn, *after)


def relay_kernel(pos, *refs):
    token = refs[-1]
    hand_on(pos, token)


def relay(pos, passed, after):
    count = len(passed)
    return pl.pallas_call(
        relay_kernel,
        out_shape=tuple(jax.ShapeDtypeStruct(x.shape, x.dtype) for x in passed) + (TOKEN,),
        in_specs=[SMEM] + [ANY] * (count + len(after)),
        out_specs=(ANY,) * count + (SMEM,),
        input_output_aliases={1 + i: i for i in range(count)},
        compiler_params=params(1),
        cost_estimate=COST,
        name="relay",
    )(pos, *passed, *after)


def sweep_kernel(pos, *refs, begin, count, heads):
    group = 4
    rates, refs = refs[:group], refs[group:]
    blocks, refs = refs[:group], refs[group:]
    tails, refs = refs[:heads], refs[heads:]
    outs, (token, first, edge, sems) = refs[:count], refs[count:]
    hand_on(pos, token)
    planes, modes, cols = blocks[0].shape[1:]
    mine = 2 * planes
    part = outs[0].shape[0]
    rows = part * count
    lead = 2 * EDGE if heads else 0
    copies = []
    for g in range(heads):
        length = tails[g].shape[0]
        copies.append(
            pltpu.make_async_copy(
                tails[g].at[pl.ds(length - lead, lead)], edge.at[:, pl.ds(g * planes, planes)], sems.at[g]
            )
        )
    for copy in copies:
        copy.start()
    for copy in copies:
        copy.wait()
    low = planes - 1
    wide = mine + 2
    piece = min(modes, 16)
    rate = [(rates[0], 0)] + [(rates[1 + p // planes], p % planes) for p in range(mine)] + [(rates[3], 0)]

    def speed(p, row):
        ref, plane = rate[p]
        return ref[plane, pl.ds(row, 1), :]

    def field(row, p, some):
        if isinstance(row, int) and row < lead:
            return edge[row, p, some]
        return blocks[p // planes][row - lead, p % planes, some]

    def beside(x):
        parts = [x[:, h * LANES : (h + 1) * LANES] for h in range(cols // LANES)]
        up = [pltpu.roll(part, 1, 1) for part in parts]
        down = [pltpu.roll(part, LANES - 1, 1) for part in parts]
        lane = lax.broadcasted_iota(jnp.int32, parts[0].shape, 1)
        nothing = jnp.zeros_like(parts[0])
        sums = []
        for h in range(len(parts)):
            left = jnp.where(lane == 0, up[h - 1] if h else nothing, up[h])
            right = jnp.where(lane == LANES - 1, down[h + 1] if h + 1 < len(parts) else nothing, down[h])
            sums.append(left.astype(F32) + right.astype(F32))
        return jnp.concatenate(sums, axis=1)

    def once(i, number):
        for a in range(number):
            speeds = [speed(p, begin + i + a) for p in range(wide)]
            for h in range(modes // piece):
                some = pl.ds(h * piece, piece)
                kept = [field(i + 1 + a, low - 1 + p, some) for p in range(wide + 2)]
                line = [x.astype(F32) for x in kept]
                for p in range(wide):
                    centre = line[p + 1]
                    around = beside(kept[p + 1]) + (line[p] + line[p + 2])
                    around = around + (
                        field(i + a, low + p, some).astype(F32) + field(i + 2 + a, low + p, some).astype(F32)
                    )
                    first[i + a, p, some] = centre + speeds[p] * (around - 6.0 * centre)

    for i in range(0, lead, 2):
        once(i, 2)

    def pair(j, _):
        once(lead + 2 * j, 2)
        return 0

    lax.fori_loop(0, (rows + 2 - lead) // 2, pair, 0)
    number = 2 if part % 2 == 0 else 1
    for k in range(count):
        base = jnp.bitwise_xor(pos[1], k) * part

        def again(j, _):
            i = base + number * j
            for a in range(number):
                speeds = [speed(p + 1, begin + i + a + 1) for p in range(mine)]
                for h in range(modes // piece):
                    some = pl.ds(h * piece, piece)
                    line = [first[i + 1 + a, p, some] for p in range(wide)]
                    for p in range(mine):
                        centre = line[p + 1]
                        around = beside(centre) + (line[p] + line[p + 2])
                        around = around + (first[i + a, p + 1, some] + first[i + 2 + a, p + 1, some])
                        outs[k][number * j + a, p, some] = (
                            centre + speeds[p] * (around - 6.0 * centre)
                        ).astype(BF16)
            return 0

        lax.fori_loop(0, part // number, again, 0)


def sweep(pos, rates, blocks, tails, begin, rows, count):
    _, planes, modes, cols = blocks[0].shape
    mine = 2 * planes
    piece = jax.ShapeDtypeStruct((rows // count, mine, modes, cols), BF16)
    return pl.pallas_call(
        functools.partial(sweep_kernel, begin=begin, count=count, heads=len(tails)),
        out_shape=(piece,) * count + (TOKEN,),
        in_specs=[SMEM] + [VMEM] * 8 + [ANY] * len(tails),
        out_specs=(VMEM,) * count + (SMEM,),
        scratch_shapes=[
            pltpu.VMEM((rows + 2, mine + 2, modes, cols), F32),
            pltpu.VMEM((2 * EDGE, 4 * planes, modes, cols), BF16),
            pltpu.SemaphoreType.DMA((4,)),
        ],
        compiler_params=params(22),
        cost_estimate=COST,
        name="sweep",
    )(pos, *rates, *blocks, *tails)


def points_kernel(pos, basis, basis_t, flat, swing, other_load, own_load, *refs, begin):
    *refs, token, gathered, stepped = refs
    hand_on(pos, token)
    count = len(refs) // 2
    blocks, outs = refs[:count], refs[count:]
    part, planes, modes, cols = blocks[0].shape
    copies = cols // flat.shape[1]
    places = [pl.multiple_of(jnp.bitwise_xor(pos[1], k) * modes, modes) for k in range(count)]

    def row(i, _):
        place = begin + pos[1] * part + i
        for p in range(planes):
            for k in range(count):
                gathered[p, pl.ds(places[k], modes)] = blocks[k][i, p].astype(gathered.dtype)
            cells = gathered[p].astype(BF16)
            half = planes // 2
            load = other_load if p < half else own_load
            heat = jnp.tanh(jnp.dot(basis[...], cells, preferred_element_type=F32).astype(BF16))
            offset = jnp.concatenate([flat[...]] * copies, axis=1)
            slope = jnp.concatenate([swing[...]] * copies, axis=1)
            weighted = offset + slope * heat
            source = jnp.dot(basis_t[...], weighted, preferred_element_type=F32)
            done = cells.astype(F32) + load[p % half, pl.ds(place, 1), :] * source
            stepped[p] = done.astype(stepped.dtype)
            for k in range(count):
                outs[k][i, p] = stepped[p, pl.ds(places[k], modes)].astype(BF16)
        return 0

    lax.fori_loop(0, part, row, 0)


def points(pos, basis, basis_t, flat, swing, loads, blocks, begin):
    count = len(blocks)
    _, planes, modes, cols = blocks[0].shape
    kept = BF16 if modes % 16 == 0 else F32
    return pl.pallas_call(
        functools.partial(points_kernel, begin=begin),
        out_shape=tuple(jax.ShapeDtypeStruct(block.shape, BF16) for block in blocks) + (TOKEN,),
        in_specs=[SMEM] + [VMEM] * (6 + count),
        out_specs=(VMEM,) * count + (SMEM,),
        scratch_shapes=[pltpu.VMEM((planes, modes * count, cols), kept)] * 2,
        compiler_params=params(14),
        cost_estimate=COST,
        name="points",
    )(pos, basis, basis_t, flat, swing, *loads, *blocks)


def collect_kernel(pos, *refs):
    *blocks, out, token, sems = refs
    hand_on(pos, token)
    part, planes = blocks[0].shape[0], out.shape[1]
    copies = []
    for k, block in enumerate(blocks):
        base = jnp.bitwise_xor(pos[1], k) * part
        copies.append(
            pltpu.make_async_copy(block.at[:, pl.ds(0, planes)], out.at[pl.ds(base, part)], sems.at[k])
        )
    for copy in copies:
        copy.start()
    for copy in copies:
        copy.wait()


def collect(pos, blocks):
    part, planes, modes, cols = blocks[0].shape
    count = len(blocks)
    shape = (part * count, planes // 2, modes, cols)
    return pl.pallas_call(
        collect_kernel,
        out_shape=(jax.ShapeDtypeStruct(shape, BF16), TOKEN),
        in_specs=[SMEM] + [ANY] * count,
        out_specs=(VMEM, SMEM),
        scratch_shapes=[pltpu.SemaphoreType.DMA((count,))],
        compiler_params=params(6),
        cost_estimate=COST,
        name="collect",
    )(pos, *blocks)


def put(out, source, side, core, begin, sems):
    rows, size = source.shape[3], out.shape[2]
    begin = core * (size // 4) + begin
    copies = []
    for a in range(2):
        far = side if a == 0 else 1 - side
        start = pl.multiple_of(jnp.where(far == 1, size - rows - begin, begin), TILE)
        copies.append(pltpu.make_async_copy(source.at[a], out.at[:, :, pl.ds(start, rows), :], sems.at[a]))
    for copy in copies:
        copy.start()
    return copies


def settle_kernel(pos, turn, *refs, begin, old_begin, parts, arrivals):
    refs = refs[-len(parts) - 7 - arrivals :]
    pieces, arrived, refs = refs[: len(parts)], refs[len(parts) : len(parts) + arrivals], refs[-7:]
    away, out, token, both, final, sems, out_sems = refs
    hand_on(pos, token)
    side, core = pos[0], pos[2]
    _, rows, planes, modes, cols = both.shape
    modes = modes // 2
    group = turn.shape[1] // TILE
    outgoing = put(out, arrived[0], side, 1 - core, old_begin, out_sems.at[0]) if arrivals else []
    incoming = []
    for n, (piece, (a, at, xor, low)) in enumerate(zip(pieces, parts)):
        length = piece.shape[0]
        if xor is not None:
            at = at + jnp.bitwise_xor(pos[1], xor) * length
        copy = pltpu.make_async_copy(
            piece.at[:, pl.ds(low, planes)], both.at[a, pl.ds(at, length)], sems.at[n]
        )
        copy.start()
        incoming.append(copy)
    for a in (0, 1):
        for copy, part in zip(incoming, parts):
            if part[0] == a:
                copy.wait()
        far = side if a == 0 else 1 - side
        for z in range(planes):
            to = jnp.where(far == 1, z, planes - 1 - z)
            for g in range(rows // TILE):
                block = jnp.where(far == 1, rows // TILE - 1 - g, g)
                for h in range(2 * modes // group):
                    there = pl.ds(h * group, group)
                    x = both[a, pl.ds(g * TILE, TILE), z, there, :]
                    y = jnp.dot(turn[far], to_bf16_rows(x), preferred_element_type=F32).astype(BF16)
                    final[a, to, there, pl.ds(pl.multiple_of(block * TILE, TILE), TILE), :] = y.reshape(
                        group, TILE, cols
                    )
    copy = pltpu.make_async_copy(final.at[:, :, pl.ds((1 - core) * modes, modes)], away, sems.at[len(parts)])
    copy.start()
    outgoing.append(copy)
    outgoing += put(out, final.at[:, :, pl.ds(core * modes, modes)], side, core, begin, out_sems.at[1])
    for copy in outgoing:
        copy.wait()


def settle(pos, turn, result, pieces, parts, arrived, begin, old_begin, rows, shape):
    planes, modes, _, cols = shape
    chained = result is not None
    given = ([result] if chained else []) + list(pieces) + list(arrived)
    return pl.pallas_call(
        functools.partial(
            settle_kernel, begin=begin, old_begin=old_begin, parts=tuple(parts), arrivals=len(arrived)
        ),
        out_shape=(
            jax.ShapeDtypeStruct((2, planes, modes, rows, cols), BF16),
            jax.ShapeDtypeStruct(shape, BF16),
            TOKEN,
        ),
        in_specs=[SMEM, VMEM] + [HBM] * chained + [ANY] * len(pieces) + [VMEM] * len(arrived),
        out_specs=(ANY, HBM, SMEM),
        scratch_shapes=[
            pltpu.VMEM((2, rows, planes, 2 * modes, cols), BF16),
            pltpu.VMEM((2, planes, 2 * modes, rows, cols), BF16),
            pltpu.SemaphoreType.DMA((len(pieces) + 1,)),
            pltpu.SemaphoreType.DMA((2, 2)),
        ],
        input_output_aliases={2: 1} if chained else {},
        compiler_params=params(10),
        cost_estimate=COST,
        name="settle",
    )(pos, turn, *given)


def last_kernel(pos, result, arrived, out, sems, *, begin):
    for copy in put(out, arrived, pos[0], 1 - pos[2], begin, sems):
        copy.wait()


def last(pos, result, arrived, begin):
    return pl.pallas_call(
        functools.partial(last_kernel, begin=begin),
        out_shape=jax.ShapeDtypeStruct(result.shape, BF16),
        in_specs=[SMEM, HBM, VMEM],
        out_specs=HBM,
        scratch_shapes=[pltpu.SemaphoreType.DMA((2,))],
        input_output_aliases={1: 0},
        compiler_params=params(6),
        cost_estimate=COST,
        name="settle_last",
    )(pos, result, arrived)


SIZES = (1, 1, 1, 1, 1, 1, 1, 1)
GROUPS = ((0,), (1,), (2, 3), (4, 5), (6, 7))
ENDS = ((0, 1), (2, 3), (4, 5), (6, 7))


def chunk_rows(quarter):
    return [n * (quarter // 8) for n in SIZES]


ORDER = (
    ("N", 0), ("T", 0), ("T", 1), ("R", 0), ("T", 2), ("R", 1), ("S", 0), ("R", 2), ("S", 1), ("R", 3),
    ("P", 0), ("S", 2), ("T", 3), ("P", 1), ("P", 2), ("C", 0), ("R", 4), ("C", 1), ("S", 3), ("S", 4),
    ("T", 4), ("R", 5), ("P", 3), ("C", 2), ("R", 6), ("S", 5), ("P", 4), ("F", 0), ("P", 5), ("R", 7),
    ("S", 6), ("C", 3), ("C", 4), ("S", 7), ("F", 1), ("P", 6), ("C", 5), ("P", 7), ("C", 6), ("F", 2),
    ("C", 7), ("F", 3),
)


def turns(group):
    at = np.arange(group * TILE)
    row, mode = at // group, at % group
    same = mode[:, None] == (at // TILE)[None, :]
    straight = same & (row[:, None] == (at % TILE)[None, :])
    reverse = same & (row[:, None] == TILE - 1 - (at % TILE)[None, :])
    to_rows = np.stack([straight, reverse])
    return jnp.asarray(to_rows, BF16), jnp.asarray(to_rows.transpose(0, 2, 1), BF16)


def on_device(field, diffusion, joule, basis, quad_weight, base_conductivity, thermal_slope):
    planes, modes, size, cols = field.shape
    half, quarter = size // 2, size // 4
    spaces, devices = lax.axis_size("space"), lax.axis_size("modes")
    chips = devices // 2
    pos = jnp.stack([lax.axis_index("space") % 2, lax.axis_index("modes") // 2, lax.axis_index("modes") % 2])
    pos = pos.astype(jnp.int32)

    swap = [(i, i ^ 1) for i in range(spaces)]
    ahead = [(i, i + 4 * (i % 2) - 2) for i in range(spaces)]
    ahead = [(i, j) for i, j in ahead if 0 <= j < spaces]
    back = [(j, i) for i, j in ahead]
    beyond = [(i, i - 1 if i % 2 == 0 else i + 1) for i in range(spaces)]
    beyond = [(i, j) for i, j in beyond if 0 <= j < spaces]

    def across(x):
        return lax.ppermute(x, "space", swap)

    def ahead_of(x):
        return lax.ppermute(x, "space", ahead)

    def behind_of(x):
        return lax.ppermute(x, "space", back)

    def by_core(x):
        return lax.ppermute(x, "modes", [(j, j ^ 1) for j in range(devices)])

    def exchange(pieces):
        moved = [pieces[0]]
        for k in range(1, chips):
            moved.append(lax.ppermute(pieces[k], "modes", [(j, j ^ (2 * k)) for j in range(devices)]))
        return moved

    to_rows, _ = turns(min(2 * modes, TILE))
    _, to_modes = turns(min(2 * modes, TILE))

    points_count = basis.shape[0]
    extra = -points_count % 32
    basis = jnp.pad(basis, ((0, extra), (0, 0)))
    basis_t = basis.T
    level = quad_weight * base_conductivity
    spread_out = lambda v: jnp.broadcast_to(jnp.pad(v, (0, extra))[:, None], (points_count + extra, LANES))
    flat, swing = spread_out(level).astype(BF16), spread_out(level * thermal_slope).astype(BF16)

    rows_of = chunk_rows(quarter)
    begins = [sum(rows_of[:c]) for c in range(len(rows_of))]
    edges = [(begin + EDGE if begin else -EDGE, begin + rows + EDGE) for begin, rows in zip(begins, rows_of)]
    groups = [[edges[n] for n in those] for those in GROUPS]
    raws, own, other, before, blocks, cells, home, theirs = {}, {}, {}, {}, {}, {}, {}, {}
    result, arrived, old_begin = None, (), 0
    for kind, c in ORDER:
        if kind == "N":
            raw, own_rate, send_rate, own_load, send_load, pos = prepare(pos, field, diffusion, joule, groups[0])
            raws[0] = by_core(raw)
            edge_rate = lax.ppermute(send_rate[:1], "space", beyond)
            rates = ahead_of(own_rate[-1:]), across(send_rate), own_rate, edge_rate
            other_load = across(send_load)
        elif kind == "T":
            after = (rates, (basis, basis_t, flat, swing), ())[min(c, 2)]
            rest = edges[len(GROUPS[0]) :]
            raw_spans, coming = (rest, None) if c else (groups[0], rest)
            *pieces, pos = spread(pos, field, raws[c > 0], to_rows, after, groups[c], raw_spans, coming)
            if coming:
                *pieces, raw = pieces
                raws[1] = by_core(raw)
            for n in GROUPS[c]:
                send, own[n], *pieces = pieces
                other[n], before[n] = across(send), ahead_of(own[n])
            if c == 0:
                other_load = across(send_load)
        elif kind == "R":
            other[c], pos = relay(pos, (other[c],), (before[c],))
            blocks[c] = (before[c], other[c], own[c], behind_of(other[c]))
        elif kind == "S":
            *pieces, pos = sweep(pos, rates, blocks[c], blocks.get(c - 1, ()), begins[c], rows_of[c], chips)
            cells[c] = exchange(pieces)
        elif kind == "P":
            *stepped, pos = points(pos, basis, basis_t, flat, swing, (other_load, own_load), cells[c], begins[c])
            home[c] = exchange(stepped)
        elif kind == "C":
            out, pos = collect(pos, home[c])
            theirs[c] = across(out)
        else:
            begin, rows = begins[ENDS[c][0]], sum(rows_of[n] for n in ENDS[c])
            pieces, parts = [], []
            for n in ENDS[c]:
                at = begins[n] - begin
                pieces += [*home[n], theirs[n]]
                parts += [(0, at, k, planes) for k in range(chips)] + [(1, at, None, 0)]
            away, result, pos = settle(
                pos, to_modes, result, pieces, parts, arrived, begin, old_begin, rows, field.shape
            )
            arrived, old_begin = (by_core(away),), begin
    return last(pos, result, arrived[0], old_begin)


def solution(mesh):
    return jax.shard_map(
        on_device,
        mesh=mesh,
        in_specs=(
            P("space", "modes", None, None),
            P("space", None, None),
            P("space", None, None),
            P(),
            P(),
            P(),
            P(),
        ),
        out_specs=P("space", "modes", None, None),
        check_vma=False,
    )
```

```python
import functools

import jax
import jax.numpy as jnp
import numpy as np
from jax import lax
from jax.experimental import pallas as pl
from jax.experimental.pallas import tpu as pltpu
from jax.sharding import PartitionSpec as P

F32, BF16 = jnp.float32, jnp.bfloat16
ANY = pl.BlockSpec(memory_space=pl.ANY)
VMEM = pl.BlockSpec(memory_space=pltpu.VMEM)
HBM = pl.BlockSpec(memory_space=pltpu.HBM)
SMEM = pl.BlockSpec(memory_space=pltpu.SMEM)
TOKEN = jax.ShapeDtypeStruct((3,), jnp.int32)
COST = pl.CostEstimate(flops=1, bytes_accessed=1, transcendentals=0)
EDGE = 2
TILE = 16
LANES = 128


def params(mebibytes):
    return pltpu.CompilerParams(vmem_limit_bytes=mebibytes * 1024 * 1024)


def from_rows(y, group):
    if group % 16 == 0:
        return y.astype(BF16).reshape(-1, group, y.shape[1])
    return y.reshape(-1, group, y.shape[1]).astype(BF16)


def hand_on(pos, token):
    for n in range(3):
        token[n] = pos[n]


def to_bf16_rows(x):
    a, m, y = x.shape
    if m % 16 == 0:
        return x.astype(BF16).reshape(a * m, y)
    return x.astype(F32).reshape(a * m, y).astype(BF16)


def raw_copies(pos, field, raw, sems, base):
    side, core = pos[0], pos[2]
    size, depth = field.shape[2], raw.shape[3]
    begin = (1 - core) * (size // 4 + min(base, 0) * TILE) + max(base, 0) * TILE
    copies = []
    for a in range(2):
        far = 1 - side if a == 0 else side
        start = pl.multiple_of(jnp.where(far == 1, size - depth - begin, begin), TILE)
        copies.append(pltpu.make_async_copy(field.at[:, :, pl.ds(start, depth), :], raw.at[a], sems.at[a]))
    for copy in copies:
        copy.start()
    return copies


def prepare_kernel(pos, field, diffusion, joule, raw, own_rate, send_rate, own_load, send_load, token, sems, *, base):
    hand_on(pos, token)
    copies = raw_copies(pos, field, raw, sems, base)
    side, core = pos[0], pos[2]
    planes, size, _ = diffusion.shape
    begin = core * (size // 4)
    for far, rate, load in ((side, own_rate, own_load), (1 - side, send_rate, send_load)):
        for source, out, first in ((diffusion, rate, begin - 1), (joule, load, begin)):

            def row(r, _):
                place = jnp.maximum(first + r, 0)
                place = jnp.where(far == 1, size - 1 - place, place)
                for z in range(planes):
                    to = jnp.where(far == 1, z, planes - 1 - z)
                    out[to, pl.ds(r, 1), :] = source[z, pl.ds(place, 1), :]
                return 0

            lax.fori_loop(0, out.shape[1], row, 0)
        for z in range(planes):
            rate[z, pl.ds(0, 1), :] = jnp.where(core == 1, rate[z, pl.ds(0, 1), :], 0.0)
    for copy in copies:
        copy.wait()


def raw_shape(field, spans):
    planes, modes, _, cols = field.shape
    return jax.ShapeDtypeStruct((2, planes, modes, blocks_of(spans)[1] * TILE, cols), BF16)


def prepare(pos, field, diffusion, joule, spans):
    planes, size, cols = diffusion.shape
    length = size // 4 + EDGE + 1
    rate = jax.ShapeDtypeStruct((planes, length + -length % 8, cols), F32)
    load = jax.ShapeDtypeStruct((planes, size // 4, cols), F32)
    return pl.pallas_call(
        functools.partial(prepare_kernel, base=blocks_of(spans)[0]),
        out_shape=(raw_shape(field, spans), rate, rate, load, load, TOKEN),
        in_specs=[SMEM, HBM, VMEM, VMEM],
        out_specs=(VMEM,) * 5 + (SMEM,),
        scratch_shapes=[pltpu.SemaphoreType.DMA((2,))],
        compiler_params=params(48),
        cost_estimate=COST,
        name="prepare",
    )(pos, field, diffusion, joule)


def spread_kernel(pos, field, raw, turn, *refs, spans, base, raw_base, next_base):
    *refs, token, window, sems, raw_sems = refs
    coming = []
    if next_base is not None:
        *refs, coming = refs
        coming = raw_copies(pos, field, coming, raw_sems, next_base)
    outs = refs[-2 * len(spans) :]
    side, core = pos[0], pos[2]
    hand_on(pos, token)
    blocks, _, planes, modes, _, cols = window.shape
    modes = modes // 2
    size = field.shape[2]
    quarter = size // 4
    depth = raw.shape[3]
    group = turn.shape[1] // TILE
    copies = {}
    for g in range(blocks):
        for a in range(2):
            far = 1 - side if a == 0 else side
            begin = core * quarter + (base + g) * TILE
            there = base + g + (core if raw_base < 0 else -raw_base)
            if base + g < 0:
                begin, there = jnp.maximum(begin, 0), jnp.maximum(there, 0)
            start = pl.multiple_of(jnp.where(far == 1, size - TILE - begin, begin), TILE)
            place = pl.multiple_of(jnp.where(far == 1, depth - TILE * (there + 1), TILE * there), TILE)
            copies[g, a] = (
                pltpu.make_async_copy(
                    field.at[:, :, pl.ds(start, TILE), :],
                    window.at[g, a, :, pl.ds(core * modes, modes)],
                    sems.at[g, a, 0],
                ),
                pltpu.make_async_copy(
                    raw.at[a, :, :, pl.ds(place, TILE), :],
                    window.at[g, a, :, pl.ds((1 - core) * modes, modes)],
                    sems.at[g, a, 1],
                ),
            )
            for copy in copies[g, a]:
                copy.start()
    for g in range(blocks):
        for a in range(2):
            far = 1 - side if a == 0 else side
            for copy in copies[g, a]:
                copy.wait()
            for z in range(planes):
                to = jnp.where(far == 1, z, planes - 1 - z)
                for h in range(2 * modes // group):
                    there = pl.ds(h * group, group)
                    x = window[g, a, z, there]
                    y = jnp.dot(turn[far], x.reshape(group * TILE, cols), preferred_element_type=F32)
                    if base + g < 0:
                        y = jnp.where(core == 1, y, 0.0)
                    y = from_rows(y, group)
                    for n, (first, last) in enumerate(spans):
                        low, high = (min(max(r - (base + g) * TILE, 0), TILE) for r in (first, last))
                        if low < high:
                            at = (base + g) * TILE + low - first
                            outs[2 * n + a][pl.ds(at, high - low), to, there, :] = y[low:high]
    for copy in coming:
        copy.wait()


def blocks_of(spans):
    base = spans[0][0] // TILE
    return base, -(-spans[-1][1] // TILE) - base


def spread(pos, field, raw, turn, after, spans, raw_spans, next_spans):
    planes, modes, _, cols = field.shape
    pieces = [jax.ShapeDtypeStruct((last - first, planes, 2 * modes, cols), BF16) for first, last in spans]
    pieces = [piece for piece in pieces for _ in range(2)]
    if next_spans:
        pieces.append(raw_shape(field, next_spans))
    base, blocks = blocks_of(spans)
    next_base = blocks_of(next_spans)[0] if next_spans else None
    return pl.pallas_call(
        functools.partial(
            spread_kernel, spans=spans, base=base, raw_base=blocks_of(raw_spans)[0], next_base=next_base
        ),
        out_shape=(*pieces, TOKEN),
        in_specs=[SMEM, HBM, ANY, VMEM] + [ANY] * len(after),
        out_specs=(VMEM,) * len(pieces) + (SMEM,),
        scratch_shapes=[
            pltpu.VMEM((blocks, 2, planes, 2 * modes, TILE, cols), BF16),
            pltpu.SemaphoreType.DMA((blocks, 2, 2)),
            pltpu.SemaphoreType.DMA((2,)),
        ],
        compiler_params=params(48),
        cost_estimate=COST,
        name="spread",
    )(pos, field, raw, turn, *after)


def relay_kernel(pos, *refs):
    token = refs[-1]
    hand_on(pos, token)


def relay(pos, passed, after):
    count = len(passed)
    return pl.pallas_call(
        relay_kernel,
        out_shape=tuple(jax.ShapeDtypeStruct(x.shape, x.dtype) for x in passed) + (TOKEN,),
        in_specs=[SMEM] + [ANY] * (count + len(after)),
        out_specs=(ANY,) * count + (SMEM,),
        input_output_aliases={1 + i: i for i in range(count)},
        compiler_params=params(1),
        cost_estimate=COST,
        name="relay",
    )(pos, *passed, *after)


def sweep_kernel(pos, *refs, begin, count, heads):
    group = 4
    rates, refs = refs[:group], refs[group:]
    blocks, refs = refs[:group], refs[group:]
    tails, refs = refs[:heads], refs[heads:]
    outs, (token, first, edge, sems) = refs[:count], refs[count:]
    hand_on(pos, token)
    planes, modes, cols = blocks[0].shape[1:]
    mine = 2 * planes
    part = outs[0].shape[0]
    rows = part * count
    lead = 2 * EDGE if heads else 0
    copies = []
    for g in range(heads):
        length = tails[g].shape[0]
        copies.append(
            pltpu.make_async_copy(
                tails[g].at[pl.ds(length - lead, lead)], edge.at[:, pl.ds(g * planes, planes)], sems.at[g]
            )
        )
    for copy in copies:
        copy.start()
    for copy in copies:
        copy.wait()
    low = planes - 1
    wide = mine + 2
    piece = min(modes, 16)
    rate = [(rates[0], 0)] + [(rates[1 + p // planes], p % planes) for p in range(mine)] + [(rates[3], 0)]

    def speed(p, row):
        ref, plane = rate[p]
        return ref[plane, pl.ds(row, 1), :]

    def field(row, p, some):
        if isinstance(row, int) and row < lead:
            return edge[row, p, some]
        return blocks[p // planes][row - lead, p % planes, some]

    def beside(x):
        parts = [x[:, h * LANES : (h + 1) * LANES] for h in range(cols // LANES)]
        up = [pltpu.roll(part, 1, 1) for part in parts]
        down = [pltpu.roll(part, LANES - 1, 1) for part in parts]
        lane = lax.broadcasted_iota(jnp.int32, parts[0].shape, 1)
        nothing = jnp.zeros_like(parts[0])
        sums = []
        for h in range(len(parts)):
            left = jnp.where(lane == 0, up[h - 1] if h else nothing, up[h])
            right = jnp.where(lane == LANES - 1, down[h + 1] if h + 1 < len(parts) else nothing, down[h])
            sums.append(left.astype(F32) + right.astype(F32))
        return jnp.concatenate(sums, axis=1)

    def once(i, number):
        for a in range(number):
            speeds = [speed(p, begin + i + a) for p in range(wide)]
            for h in range(modes // piece):
                some = pl.ds(h * piece, piece)
                kept = [field(i + 1 + a, low - 1 + p, some) for p in range(wide + 2)]
                line = [x.astype(F32) for x in kept]
                for p in range(wide):
                    centre = line[p + 1]
                    around = beside(kept[p + 1]) + (line[p] + line[p + 2])
                    around = around + (
                        field(i + a, low + p, some).astype(F32) + field(i + 2 + a, low + p, some).astype(F32)
                    )
                    first[i + a, p, some] = centre + speeds[p] * (around - 6.0 * centre)

    for i in range(0, lead, 2):
        once(i, 2)

    def pair(j, _):
        once(lead + 2 * j, 2)
        return 0

    lax.fori_loop(0, (rows + 2 - lead) // 2, pair, 0)
    number = 2 if part % 2 == 0 else 1
    for k in range(count):
        base = jnp.bitwise_xor(pos[1], k) * part

        def again(j, _):
            i = base + number * j
            for a in range(number):
                speeds = [speed(p + 1, begin + i + a + 1) for p in range(mine)]
                for h in range(modes // piece):
                    some = pl.ds(h * piece, piece)
                    line = [first[i + 1 + a, p, some] for p in range(wide)]
                    for p in range(mine):
                        centre = line[p + 1]
                        around = beside(centre) + (line[p] + line[p + 2])
                        around = around + (first[i + a, p + 1, some] + first[i + 2 + a, p + 1, some])
                        outs[k][number * j + a, p, some] = (
                            centre + speeds[p] * (around - 6.0 * centre)
                        ).astype(BF16)
            return 0

        lax.fori_loop(0, part // number, again, 0)


def sweep(pos, rates, blocks, tails, begin, rows, count):
    _, planes, modes, cols = blocks[0].shape
    mine = 2 * planes
    piece = jax.ShapeDtypeStruct((rows // count, mine, modes, cols), BF16)
    return pl.pallas_call(
        functools.partial(sweep_kernel, begin=begin, count=count, heads=len(tails)),
        out_shape=(piece,) * count + (TOKEN,),
        in_specs=[SMEM] + [VMEM] * 8 + [ANY] * len(tails),
        out_specs=(VMEM,) * count + (SMEM,),
        scratch_shapes=[
            pltpu.VMEM((rows + 2, mine + 2, modes, cols), F32),
            pltpu.VMEM((2 * EDGE, 4 * planes, modes, cols), BF16),
            pltpu.SemaphoreType.DMA((4,)),
        ],
        compiler_params=params(22),
        cost_estimate=COST,
        name="sweep",
    )(pos, *rates, *blocks, *tails)


def points_kernel(pos, basis, basis_t, flat, swing, other_load, own_load, *refs, begin):
    *refs, token, gathered, weighted, stepped = refs
    hand_on(pos, token)
    count = len(refs) // 2
    blocks, outs = refs[:count], refs[count:]
    part, planes, modes, cols = blocks[0].shape
    copies = cols // flat.shape[1]
    places = [pl.multiple_of(jnp.bitwise_xor(pos[1], k) * modes, modes) for k in range(count)]

    half = planes // 2

    def conduct(i, slot):
        for p in range(planes):
            for k in range(count):
                gathered[slot, p, pl.ds(places[k], modes)] = blocks[k][i, p].astype(gathered.dtype)
            cells = gathered[slot, p].astype(BF16)
            heat = jnp.tanh(jnp.dot(basis[...], cells, preferred_element_type=F32))
            offset = jnp.concatenate([flat[...]] * copies, axis=1)
            slope = jnp.concatenate([swing[...]] * copies, axis=1)
            weighted[slot, p] = (offset + slope * heat).astype(BF16)

    def advance(i, slot):
        place = begin + pos[1] * part + i
        for p in range(planes):
            source = jnp.dot(basis_t[...], weighted[slot, p], preferred_element_type=F32)
            load = other_load if p < half else own_load
            done = gathered[slot, p].astype(F32) + load[p % half, pl.ds(place, 1), :] * source.astype(BF16).astype(F32)
            stepped[p] = done.astype(stepped.dtype)
            for k in range(count):
                outs[k][i, p] = stepped[p, pl.ds(places[k], modes)].astype(BF16)

    conduct(0, 0)
    for i in range(part):
        if i + 1 < part:
            conduct(i + 1, (i + 1) % 2)
        advance(i, i % 2)


def points(pos, basis, basis_t, flat, swing, loads, blocks, begin):
    count = len(blocks)
    _, planes, modes, cols = blocks[0].shape
    kept = BF16 if modes % 16 == 0 else F32
    return pl.pallas_call(
        functools.partial(points_kernel, begin=begin),
        out_shape=tuple(jax.ShapeDtypeStruct(block.shape, BF16) for block in blocks) + (TOKEN,),
        in_specs=[SMEM] + [VMEM] * (6 + count),
        out_specs=(VMEM,) * count + (SMEM,),
        scratch_shapes=[
            pltpu.VMEM((2, planes, modes * count, cols), kept),
            pltpu.VMEM((2, planes, basis.shape[0], cols), BF16),
            pltpu.VMEM((planes, modes * count, cols), kept),
        ],
        compiler_params=params(16),
        cost_estimate=COST,
        name="points",
    )(pos, basis, basis_t, flat, swing, *loads, *blocks)


def collect_kernel(pos, *refs):
    *blocks, out, token, sems = refs
    hand_on(pos, token)
    part, planes = blocks[0].shape[0], out.shape[1]
    copies = []
    for k, block in enumerate(blocks):
        base = jnp.bitwise_xor(pos[1], k) * part
        copies.append(
            pltpu.make_async_copy(block.at[:, pl.ds(0, planes)], out.at[pl.ds(base, part)], sems.at[k])
        )
    for copy in copies:
        copy.start()
    for copy in copies:
        copy.wait()


def collect(pos, blocks):
    part, planes, modes, cols = blocks[0].shape
    count = len(blocks)
    shape = (part * count, planes // 2, modes, cols)
    return pl.pallas_call(
        collect_kernel,
        out_shape=(jax.ShapeDtypeStruct(shape, BF16), TOKEN),
        in_specs=[SMEM] + [ANY] * count,
        out_specs=(VMEM, SMEM),
        scratch_shapes=[pltpu.SemaphoreType.DMA((count,))],
        compiler_params=params(6),
        cost_estimate=COST,
        name="collect",
    )(pos, *blocks)


def put(out, source, side, core, begin, sems):
    rows, size = source.shape[3], out.shape[2]
    begin = core * (size // 4) + begin
    copies = []
    for a in range(2):
        far = side if a == 0 else 1 - side
        start = pl.multiple_of(jnp.where(far == 1, size - rows - begin, begin), TILE)
        copies.append(pltpu.make_async_copy(source.at[a], out.at[:, :, pl.ds(start, rows), :], sems.at[a]))
    for copy in copies:
        copy.start()
    return copies


def settle_kernel(pos, turn, *refs, begin, old_begin, parts, arrivals):
    refs = refs[-len(parts) - 7 - arrivals :]
    pieces, arrived, refs = refs[: len(parts)], refs[len(parts) : len(parts) + arrivals], refs[-7:]
    away, out, token, both, final, sems, out_sems = refs
    hand_on(pos, token)
    side, core = pos[0], pos[2]
    _, rows, planes, modes, cols = both.shape
    modes = modes // 2
    group = turn.shape[1] // TILE
    outgoing = put(out, arrived[0], side, 1 - core, old_begin, out_sems.at[0]) if arrivals else []
    incoming = []
    for n, (piece, (a, at, xor, low)) in enumerate(zip(pieces, parts)):
        length = piece.shape[0]
        if xor is not None:
            at = at + jnp.bitwise_xor(pos[1], xor) * length
        copy = pltpu.make_async_copy(
            piece.at[:, pl.ds(low, planes)], both.at[a, pl.ds(at, length)], sems.at[n]
        )
        copy.start()
        incoming.append(copy)
    for a in (0, 1):
        for copy, part in zip(incoming, parts):
            if part[0] == a:
                copy.wait()
        far = side if a == 0 else 1 - side
        for z in range(planes):
            to = jnp.where(far == 1, z, planes - 1 - z)
            for g in range(rows // TILE):
                block = jnp.where(far == 1, rows // TILE - 1 - g, g)
                for h in range(2 * modes // group):
                    there = pl.ds(h * group, group)
                    x = both[a, pl.ds(g * TILE, TILE), z, there, :]
                    y = jnp.dot(turn[far], to_bf16_rows(x), preferred_element_type=F32).astype(BF16)
                    final[a, to, there, pl.ds(pl.multiple_of(block * TILE, TILE), TILE), :] = y.reshape(
                        group, TILE, cols
                    )
    copy = pltpu.make_async_copy(final.at[:, :, pl.ds((1 - core) * modes, modes)], away, sems.at[len(parts)])
    copy.start()
    outgoing.append(copy)
    outgoing += put(out, final.at[:, :, pl.ds(core * modes, modes)], side, core, begin, out_sems.at[1])
    for copy in outgoing:
        copy.wait()


def settle(pos, turn, result, pieces, parts, arrived, begin, old_begin, rows, shape):
    planes, modes, _, cols = shape
    chained = result is not None
    given = ([result] if chained else []) + list(pieces) + list(arrived)
    return pl.pallas_call(
        functools.partial(
            settle_kernel, begin=begin, old_begin=old_begin, parts=tuple(parts), arrivals=len(arrived)
        ),
        out_shape=(
            jax.ShapeDtypeStruct((2, planes, modes, rows, cols), BF16),
            jax.ShapeDtypeStruct(shape, BF16),
            TOKEN,
        ),
        in_specs=[SMEM, VMEM] + [HBM] * chained + [ANY] * len(pieces) + [VMEM] * len(arrived),
        out_specs=(ANY, HBM, SMEM),
        scratch_shapes=[
            pltpu.VMEM((2, rows, planes, 2 * modes, cols), BF16),
            pltpu.VMEM((2, planes, 2 * modes, rows, cols), BF16),
            pltpu.SemaphoreType.DMA((len(pieces) + 1,)),
            pltpu.SemaphoreType.DMA((2, 2)),
        ],
        input_output_aliases={2: 1} if chained else {},
        compiler_params=params(10),
        cost_estimate=COST,
        name="settle",
    )(pos, turn, *given)


def last_kernel(pos, result, arrived, out, sems, *, begin):
    for copy in put(out, arrived, pos[0], 1 - pos[2], begin, sems):
        copy.wait()


def last(pos, result, arrived, begin):
    return pl.pallas_call(
        functools.partial(last_kernel, begin=begin),
        out_shape=jax.ShapeDtypeStruct(result.shape, BF16),
        in_specs=[SMEM, HBM, VMEM],
        out_specs=HBM,
        scratch_shapes=[pltpu.SemaphoreType.DMA((2,))],
        input_output_aliases={1: 0},
        compiler_params=params(6),
        cost_estimate=COST,
        name="settle_last",
    )(pos, result, arrived)


SIZES = (1, 1, 1, 1, 1, 1, 1, 1)
GROUPS = ((0,), (1,), (2, 3, 4), (5, 6, 7))
ENDS = ((0, 1), (2, 3), (4, 5), (6, 7))


def chunk_rows(quarter):
    return [n * (quarter // 8) for n in SIZES]


ORDER = (
    ("N", 0), ("T", 0), ("T", 1), ("R", 0), ("T", 2), ("R", 1), ("S", 0), ("R", 2), ("S", 1), ("R", 3),
    ("P", 0), ("S", 2), ("P", 1), ("C", 0), ("T", 3), ("R", 4), ("S", 3), ("P", 2), ("C", 1), ("R", 5),
    ("P", 3), ("S", 4), ("R", 6), ("C", 2), ("C", 3), ("F", 0), ("P", 4), ("S", 5), ("R", 7), ("C", 4),
    ("S", 6), ("P", 5), ("F", 1), ("S", 7), ("P", 6), ("C", 5), ("P", 7), ("F", 2), ("C", 6), ("C", 7),
    ("F", 3),
)


def turns(group):
    at = np.arange(group * TILE)
    row, mode = at // group, at % group
    same = mode[:, None] == (at // TILE)[None, :]
    straight = same & (row[:, None] == (at % TILE)[None, :])
    reverse = same & (row[:, None] == TILE - 1 - (at % TILE)[None, :])
    to_rows = np.stack([straight, reverse])
    return jnp.asarray(to_rows, BF16), jnp.asarray(to_rows.transpose(0, 2, 1), BF16)


def on_device(field, diffusion, joule, basis, quad_weight, base_conductivity, thermal_slope):
    planes, modes, size, cols = field.shape
    half, quarter = size // 2, size // 4
    spaces, devices = lax.axis_size("space"), lax.axis_size("modes")
    chips = devices // 2
    pos = jnp.stack([lax.axis_index("space") % 2, lax.axis_index("modes") // 2, lax.axis_index("modes") % 2])
    pos = pos.astype(jnp.int32)

    swap = [(i, i ^ 1) for i in range(spaces)]
    ahead = [(i, i + 4 * (i % 2) - 2) for i in range(spaces)]
    ahead = [(i, j) for i, j in ahead if 0 <= j < spaces]
    back = [(j, i) for i, j in ahead]
    beyond = [(i, i - 1 if i % 2 == 0 else i + 1) for i in range(spaces)]
    beyond = [(i, j) for i, j in beyond if 0 <= j < spaces]

    def across(x):
        return lax.ppermute(x, "space", swap)

    def ahead_of(x):
        return lax.ppermute(x, "space", ahead)

    def behind_of(x):
        return lax.ppermute(x, "space", back)

    def by_core(x):
        return lax.ppermute(x, "modes", [(j, j ^ 1) for j in range(devices)])

    def exchange(pieces):
        moved = [pieces[0]]
        for k in range(1, chips):
            moved.append(lax.ppermute(pieces[k], "modes", [(j, j ^ (2 * k)) for j in range(devices)]))
        return moved

    to_rows, _ = turns(min(2 * modes, TILE))
    _, to_modes = turns(min(2 * modes, TILE))

    points_count = basis.shape[0]
    extra = -points_count % 32
    basis = jnp.pad(basis, ((0, extra), (0, 0)))
    basis_t = basis.T
    level = quad_weight * base_conductivity
    spread_out = lambda v: jnp.broadcast_to(jnp.pad(v, (0, extra))[:, None], (points_count + extra, LANES))
    flat, swing = spread_out(level), spread_out(level * thermal_slope)

    rows_of = chunk_rows(quarter)
    begins = [sum(rows_of[:c]) for c in range(len(rows_of))]
    edges = [(begin + EDGE if begin else -EDGE, begin + rows + EDGE) for begin, rows in zip(begins, rows_of)]
    groups = [[edges[n] for n in those] for those in GROUPS]
    raws, own, other, before, blocks, cells, home, theirs = {}, {}, {}, {}, {}, {}, {}, {}
    result, arrived, old_begin = None, (), 0
    for kind, c in ORDER:
        if kind == "N":
            raw, own_rate, send_rate, own_load, send_load, pos = prepare(pos, field, diffusion, joule, groups[0])
            raws[0] = by_core(raw)
            edge_rate = lax.ppermute(send_rate[:1], "space", beyond)
            rates = ahead_of(own_rate[-1:]), across(send_rate), own_rate, edge_rate
            other_load = across(send_load)
        elif kind == "T":
            after = (rates, (basis, basis_t, flat, swing), ())[min(c, 2)]
            rest = edges[len(GROUPS[0]) :]
            raw_spans, coming = (rest, None) if c else (groups[0], rest)
            *pieces, pos = spread(pos, field, raws[c > 0], to_rows, after, groups[c], raw_spans, coming)
            if coming:
                *pieces, raw = pieces
                raws[1] = by_core(raw)
            for n in GROUPS[c]:
                send, own[n], *pieces = pieces
                other[n], before[n] = across(send), ahead_of(own[n])
            if c == 0:
                other_load = across(send_load)
        elif kind == "R":
            other[c], pos = relay(pos, (other[c],), (before[c],))
            blocks[c] = (before[c], other[c], own[c], behind_of(other[c]))
        elif kind == "S":
            *pieces, pos = sweep(pos, rates, blocks[c], blocks.get(c - 1, ()), begins[c], rows_of[c], chips)
            cells[c] = exchange(pieces)
        elif kind == "P":
            *stepped, pos = points(pos, basis, basis_t, flat, swing, (other_load, own_load), cells[c], begins[c])
            home[c] = exchange(stepped)
        elif kind == "C":
            out, pos = collect(pos, home[c])
            theirs[c] = across(out)
        else:
            begin, rows = begins[ENDS[c][0]], sum(rows_of[n] for n in ENDS[c])
            pieces, parts = [], []
            for n in ENDS[c]:
                at = begins[n] - begin
                pieces += [*home[n], theirs[n]]
                parts += [(0, at, k, planes) for k in range(chips)] + [(1, at, None, 0)]
            away, result, pos = settle(
                pos, to_modes, result, pieces, parts, arrived, begin, old_begin, rows, field.shape
            )
            arrived, old_begin = (by_core(away),), begin
    return last(pos, result, arrived[0], old_begin)


def solution(mesh):
    return jax.shard_map(
        on_device,
        mesh=mesh,
        in_specs=(
            P("space", "modes", None, None),
            P("space", None, None),
            P("space", None, None),
            P(),
            P(),
            P(),
            P(),
        ),
        out_specs=P("space", "modes", None, None),
        check_vma=False,
    )
```

```python
import functools

import jax
import jax.numpy as jnp
import numpy as np
from jax import lax
from jax.experimental import pallas as pl
from jax.experimental.pallas import tpu as pltpu
from jax.sharding import PartitionSpec as P

F32, BF16 = jnp.float32, jnp.bfloat16
ANY = pl.BlockSpec(memory_space=pl.ANY)
VMEM = pl.BlockSpec(memory_space=pltpu.VMEM)
HBM = pl.BlockSpec(memory_space=pltpu.HBM)
SMEM = pl.BlockSpec(memory_space=pltpu.SMEM)
TOKEN = jax.ShapeDtypeStruct((3,), jnp.int32)
COST = pl.CostEstimate(flops=1, bytes_accessed=1, transcendentals=0)
EDGE = 2
TILE = 16
LANES = 128


def params(mebibytes):
    return pltpu.CompilerParams(vmem_limit_bytes=mebibytes * 1024 * 1024)


def from_rows(y, group):
    if group % 16 == 0:
        return y.astype(BF16).reshape(-1, group, y.shape[1])
    return y.reshape(-1, group, y.shape[1]).astype(BF16)


def hand_on(pos, token):
    for n in range(3):
        token[n] = pos[n]


def to_bf16_rows(x):
    a, m, y = x.shape
    if m % 16 == 0:
        return x.astype(BF16).reshape(a * m, y)
    return x.astype(F32).reshape(a * m, y).astype(BF16)


def raw_copies(pos, field, raw, sems, base):
    side, core = pos[0], pos[2]
    size, depth = field.shape[2], raw.shape[3]
    begin = (1 - core) * (size // 4 + min(base, 0) * TILE) + max(base, 0) * TILE
    copies = []
    for a in range(2):
        far = 1 - side if a == 0 else side
        start = pl.multiple_of(jnp.where(far == 1, size - depth - begin, begin), TILE)
        copies.append(pltpu.make_async_copy(field.at[:, :, pl.ds(start, depth), :], raw.at[a], sems.at[a]))
    for copy in copies:
        copy.start()
    return copies


def prepare_kernel(
    pos, field, far_diffusion, far_joule, raw, own_rate, send_rate, own_load, send_load, token,
    diffusion, joule, sems, near_sems, *, base
):
    hand_on(pos, token)
    near = [
        pltpu.make_async_copy(source, to, near_sems.at[n])
        for n, (source, to) in enumerate(((far_diffusion, diffusion), (far_joule, joule)))
    ]
    for copy in near:
        copy.start()
    copies = raw_copies(pos, field, raw, sems, base)
    for copy in near:
        copy.wait()
    side, core = pos[0], pos[2]
    planes, size, _ = diffusion.shape
    begin = core * (size // 4)
    for far, rate, load in ((side, own_rate, own_load), (1 - side, send_rate, send_load)):
        for source, out, first in ((diffusion, rate, begin - 1), (joule, load, begin)):

            def row(r, _):
                place = jnp.maximum(first + r, 0)
                place = jnp.where(far == 1, size - 1 - place, place)
                for z in range(planes):
                    to = jnp.where(far == 1, z, planes - 1 - z)
                    out[to, pl.ds(r, 1), :] = source[z, pl.ds(place, 1), :]
                return 0

            lax.fori_loop(0, out.shape[1], row, 0)
        for z in range(planes):
            rate[z, pl.ds(0, 1), :] = jnp.where(core == 1, rate[z, pl.ds(0, 1), :], 0.0)
    for copy in copies:
        copy.wait()


def raw_shape(field, spans):
    planes, modes, _, cols = field.shape
    return jax.ShapeDtypeStruct((2, planes, modes, blocks_of(spans)[1] * TILE, cols), BF16)


def prepare(pos, field, diffusion, joule, spans):
    planes, size, cols = diffusion.shape
    length = size // 4 + EDGE + 1
    rate = jax.ShapeDtypeStruct((planes, length + -length % 8, cols), F32)
    load = jax.ShapeDtypeStruct((planes, size // 4, cols), F32)
    return pl.pallas_call(
        functools.partial(prepare_kernel, base=blocks_of(spans)[0]),
        out_shape=(raw_shape(field, spans), rate, rate, load, load, TOKEN),
        in_specs=[SMEM, HBM, HBM, HBM],
        out_specs=(VMEM,) * 5 + (SMEM,),
        scratch_shapes=[
            pltpu.VMEM(diffusion.shape, F32),
            pltpu.VMEM(joule.shape, F32),
            pltpu.SemaphoreType.DMA((2,)),
            pltpu.SemaphoreType.DMA((2,)),
        ],
        compiler_params=params(48),
        cost_estimate=COST,
        name="prepare",
    )(pos, field, diffusion, joule)


def spread_kernel(pos, field, raw, turn, *refs, spans, base, raw_base, next_base):
    *refs, token, window, sems, raw_sems = refs
    coming = []
    if next_base is not None:
        *refs, coming = refs
        coming = raw_copies(pos, field, coming, raw_sems, next_base)
    outs = refs[-2 * len(spans) :]
    side, core = pos[0], pos[2]
    hand_on(pos, token)
    blocks, _, planes, modes, _, cols = window.shape
    modes = modes // 2
    size = field.shape[2]
    quarter = size // 4
    depth = raw.shape[3]
    group = turn.shape[1] // TILE
    copies = {}
    for g in range(blocks):
        for a in range(2):
            far = 1 - side if a == 0 else side
            begin = core * quarter + (base + g) * TILE
            there = base + g + (core if raw_base < 0 else -raw_base)
            if base + g < 0:
                begin, there = jnp.maximum(begin, 0), jnp.maximum(there, 0)
            start = pl.multiple_of(jnp.where(far == 1, size - TILE - begin, begin), TILE)
            place = pl.multiple_of(jnp.where(far == 1, depth - TILE * (there + 1), TILE * there), TILE)
            copies[g, a] = (
                pltpu.make_async_copy(
                    field.at[:, :, pl.ds(start, TILE), :],
                    window.at[g, a, :, pl.ds(core * modes, modes)],
                    sems.at[g, a, 0],
                ),
                pltpu.make_async_copy(
                    raw.at[a, :, :, pl.ds(place, TILE), :],
                    window.at[g, a, :, pl.ds((1 - core) * modes, modes)],
                    sems.at[g, a, 1],
                ),
            )
            for copy in copies[g, a]:
                copy.start()
    for g in range(blocks):
        for a in range(2):
            far = 1 - side if a == 0 else side
            for copy in copies[g, a]:
                copy.wait()
            for z in range(planes):
                to = jnp.where(far == 1, z, planes - 1 - z)
                for h in range(2 * modes // group):
                    there = pl.ds(h * group, group)
                    x = window[g, a, z, there]
                    y = jnp.dot(turn[far], x.reshape(group * TILE, cols), preferred_element_type=F32)
                    if base + g < 0:
                        y = jnp.where(core == 1, y, 0.0)
                    y = from_rows(y, group)
                    for n, (first, last) in enumerate(spans):
                        low, high = (min(max(r - (base + g) * TILE, 0), TILE) for r in (first, last))
                        if low < high:
                            at = (base + g) * TILE + low - first
                            outs[2 * n + a][pl.ds(at, high - low), to, there, :] = y[low:high]
    for copy in coming:
        copy.wait()


def blocks_of(spans):
    base = spans[0][0] // TILE
    return base, -(-spans[-1][1] // TILE) - base


def spread(pos, field, raw, turn, after, spans, raw_spans, next_spans):
    planes, modes, _, cols = field.shape
    pieces = [jax.ShapeDtypeStruct((last - first, planes, 2 * modes, cols), BF16) for first, last in spans]
    pieces = [piece for piece in pieces for _ in range(2)]
    if next_spans:
        pieces.append(raw_shape(field, next_spans))
    base, blocks = blocks_of(spans)
    next_base = blocks_of(next_spans)[0] if next_spans else None
    return pl.pallas_call(
        functools.partial(
            spread_kernel, spans=spans, base=base, raw_base=blocks_of(raw_spans)[0], next_base=next_base
        ),
        out_shape=(*pieces, TOKEN),
        in_specs=[SMEM, HBM, ANY, VMEM] + [ANY] * len(after),
        out_specs=(VMEM,) * len(pieces) + (SMEM,),
        scratch_shapes=[
            pltpu.VMEM((blocks, 2, planes, 2 * modes, TILE, cols), BF16),
            pltpu.SemaphoreType.DMA((blocks, 2, 2)),
            pltpu.SemaphoreType.DMA((2,)),
        ],
        compiler_params=params(48),
        cost_estimate=COST,
        name="spread",
    )(pos, field, raw, turn, *after)


def relay_kernel(pos, *refs):
    token = refs[-1]
    hand_on(pos, token)


def relay(pos, passed, after):
    count = len(passed)
    return pl.pallas_call(
        relay_kernel,
        out_shape=tuple(jax.ShapeDtypeStruct(x.shape, x.dtype) for x in passed) + (TOKEN,),
        in_specs=[SMEM] + [ANY] * (count + len(after)),
        out_specs=(ANY,) * count + (SMEM,),
        input_output_aliases={1 + i: i for i in range(count)},
        compiler_params=params(1),
        cost_estimate=COST,
        name="relay",
    )(pos, *passed, *after)


def sweep_kernel(pos, *refs, begin, count, heads):
    group = 4
    rates, refs = refs[:group], refs[group:]
    blocks, refs = refs[:group], refs[group:]
    tails, refs = refs[:heads], refs[heads:]
    outs, (token, first, edge, sems) = refs[:count], refs[count:]
    hand_on(pos, token)
    planes, modes, cols = blocks[0].shape[1:]
    mine = 2 * planes
    part = outs[0].shape[0]
    rows = part * count
    lead = 2 * EDGE if heads else 0
    copies = []
    for g in range(heads):
        length = tails[g].shape[0]
        copies.append(
            pltpu.make_async_copy(
                tails[g].at[pl.ds(length - lead, lead)], edge.at[:, pl.ds(g * planes, planes)], sems.at[g]
            )
        )
    for copy in copies:
        copy.start()
    for copy in copies:
        copy.wait()
    low = planes - 1
    wide = mine + 2
    piece = min(modes, 16)
    rate = [(rates[0], 0)] + [(rates[1 + p // planes], p % planes) for p in range(mine)] + [(rates[3], 0)]

    def speed(p, row):
        ref, plane = rate[p]
        return ref[plane, pl.ds(row, 1), :]

    def field(row, p, some):
        if isinstance(row, int) and row < lead:
            return edge[row, p, some]
        return blocks[p // planes][row - lead, p % planes, some]

    def beside(x):
        parts = [x[:, h * LANES : (h + 1) * LANES] for h in range(cols // LANES)]
        up = [pltpu.roll(part, 1, 1) for part in parts]
        down = [pltpu.roll(part, LANES - 1, 1) for part in parts]
        lane = lax.broadcasted_iota(jnp.int32, parts[0].shape, 1)
        nothing = jnp.zeros_like(parts[0])
        sums = []
        for h in range(len(parts)):
            left = jnp.where(lane == 0, up[h - 1] if h else nothing, up[h])
            right = jnp.where(lane == LANES - 1, down[h + 1] if h + 1 < len(parts) else nothing, down[h])
            sums.append(left.astype(F32) + right.astype(F32))
        return jnp.concatenate(sums, axis=1)

    def once(i, number):
        for a in range(number):
            speeds = [speed(p, begin + i + a) for p in range(wide)]
            for h in range(modes // piece):
                some = pl.ds(h * piece, piece)
                kept = [field(i + 1 + a, low - 1 + p, some) for p in range(wide + 2)]
                line = [x.astype(F32) for x in kept]
                for p in range(wide):
                    centre = line[p + 1]
                    around = beside(kept[p + 1]) + (line[p] + line[p + 2])
                    around = around + (
                        field(i + a, low + p, some).astype(F32) + field(i + 2 + a, low + p, some).astype(F32)
                    )
                    first[i + a, p, some] = centre + speeds[p] * (around - 6.0 * centre)

    for i in range(0, lead, 2):
        once(i, 2)

    def pair(j, _):
        once(lead + 2 * j, 2)
        return 0

    lax.fori_loop(0, (rows + 2 - lead) // 2, pair, 0)
    number = 2 if part % 2 == 0 else 1
    for k in range(count):
        base = jnp.bitwise_xor(pos[1], k) * part

        def again(j, _):
            i = base + number * j
            for a in range(number):
                speeds = [speed(p + 1, begin + i + a + 1) for p in range(mine)]
                for h in range(modes // piece):
                    some = pl.ds(h * piece, piece)
                    line = [first[i + 1 + a, p, some] for p in range(wide)]
                    for p in range(mine):
                        centre = line[p + 1]
                        around = beside(centre) + (line[p] + line[p + 2])
                        around = around + (first[i + a, p + 1, some] + first[i + 2 + a, p + 1, some])
                        outs[k][number * j + a, p, some] = (
                            centre + speeds[p] * (around - 6.0 * centre)
                        ).astype(BF16)
            return 0

        lax.fori_loop(0, part // number, again, 0)


def sweep(pos, rates, blocks, tails, begin, rows, count):
    _, planes, modes, cols = blocks[0].shape
    mine = 2 * planes
    piece = jax.ShapeDtypeStruct((rows // count, mine, modes, cols), BF16)
    return pl.pallas_call(
        functools.partial(sweep_kernel, begin=begin, count=count, heads=len(tails)),
        out_shape=(piece,) * count + (TOKEN,),
        in_specs=[SMEM] + [VMEM] * 8 + [ANY] * len(tails),
        out_specs=(VMEM,) * count + (SMEM,),
        scratch_shapes=[
            pltpu.VMEM((rows + 2, mine + 2, modes, cols), F32),
            pltpu.VMEM((2 * EDGE, 4 * planes, modes, cols), BF16),
            pltpu.SemaphoreType.DMA((4,)),
        ],
        compiler_params=params(22),
        cost_estimate=COST,
        name="sweep",
    )(pos, *rates, *blocks, *tails)


def points_kernel(pos, basis, basis_t, flat, swing, other_load, own_load, *refs, begin):
    *refs, token, gathered, weighted, stepped = refs
    hand_on(pos, token)
    count = len(refs) // 2
    blocks, outs = refs[:count], refs[count:]
    part, planes, modes, cols = blocks[0].shape
    copies = cols // flat.shape[1]
    places = [pl.multiple_of(jnp.bitwise_xor(pos[1], k) * modes, modes) for k in range(count)]

    half = planes // 2

    def conduct(i, slot):
        for p in range(planes):
            for k in range(count):
                gathered[slot, p, pl.ds(places[k], modes)] = blocks[k][i, p].astype(gathered.dtype)
            cells = gathered[slot, p].astype(BF16)
            heat = jnp.tanh(jnp.dot(basis[...], cells, preferred_element_type=F32))
            offset = jnp.concatenate([flat[...]] * copies, axis=1)
            slope = jnp.concatenate([swing[...]] * copies, axis=1)
            weighted[slot, p] = (offset + slope * heat).astype(BF16)

    def advance(i, slot):
        place = begin + pos[1] * part + i
        for p in range(planes):
            source = jnp.dot(basis_t[...], weighted[slot, p], preferred_element_type=F32)
            load = other_load if p < half else own_load
            done = gathered[slot, p].astype(F32) + load[p % half, pl.ds(place, 1), :] * source.astype(BF16).astype(F32)
            stepped[p] = done.astype(stepped.dtype)
            for k in range(count):
                outs[k][i, p] = stepped[p, pl.ds(places[k], modes)].astype(BF16)

    conduct(0, 0)
    for i in range(part):
        if i + 1 < part:
            conduct(i + 1, (i + 1) % 2)
        advance(i, i % 2)


def points(pos, basis, basis_t, flat, swing, loads, blocks, begin):
    count = len(blocks)
    _, planes, modes, cols = blocks[0].shape
    kept = BF16 if modes % 16 == 0 else F32
    return pl.pallas_call(
        functools.partial(points_kernel, begin=begin),
        out_shape=tuple(jax.ShapeDtypeStruct(block.shape, BF16) for block in blocks) + (TOKEN,),
        in_specs=[SMEM] + [VMEM] * (6 + count),
        out_specs=(VMEM,) * count + (SMEM,),
        scratch_shapes=[
            pltpu.VMEM((2, planes, modes * count, cols), kept),
            pltpu.VMEM((2, planes, basis.shape[0], cols), BF16),
            pltpu.VMEM((planes, modes * count, cols), kept),
        ],
        compiler_params=params(16),
        cost_estimate=COST,
        name="points",
    )(pos, basis, basis_t, flat, swing, *loads, *blocks)


def collect_kernel(pos, *refs):
    *blocks, out, token, sems = refs
    hand_on(pos, token)
    part, planes = blocks[0].shape[0], out.shape[1]
    copies = []
    for k, block in enumerate(blocks):
        base = jnp.bitwise_xor(pos[1], k) * part
        copies.append(
            pltpu.make_async_copy(block.at[:, pl.ds(0, planes)], out.at[pl.ds(base, part)], sems.at[k])
        )
    for copy in copies:
        copy.start()
    for copy in copies:
        copy.wait()


def collect(pos, blocks):
    part, planes, modes, cols = blocks[0].shape
    count = len(blocks)
    shape = (part * count, planes // 2, modes, cols)
    return pl.pallas_call(
        collect_kernel,
        out_shape=(jax.ShapeDtypeStruct(shape, BF16), TOKEN),
        in_specs=[SMEM] + [ANY] * count,
        out_specs=(VMEM, SMEM),
        scratch_shapes=[pltpu.SemaphoreType.DMA((count,))],
        compiler_params=params(6),
        cost_estimate=COST,
        name="collect",
    )(pos, *blocks)


def put(out, source, side, core, begin, sems):
    rows, size = source.shape[3], out.shape[2]
    begin = core * (size // 4) + begin
    copies = []
    for a in range(2):
        far = side if a == 0 else 1 - side
        start = pl.multiple_of(jnp.where(far == 1, size - rows - begin, begin), TILE)
        copies.append(pltpu.make_async_copy(source.at[a], out.at[:, :, pl.ds(start, rows), :], sems.at[a]))
    for copy in copies:
        copy.start()
    return copies


def settle_kernel(pos, turn, *refs, begin, old_begin, parts, arrivals):
    refs = refs[-len(parts) - 7 - arrivals :]
    pieces, arrived, refs = refs[: len(parts)], refs[len(parts) : len(parts) + arrivals], refs[-7:]
    away, out, token, both, final, sems, out_sems = refs
    hand_on(pos, token)
    side, core = pos[0], pos[2]
    _, rows, planes, modes, cols = both.shape
    modes = modes // 2
    group = turn.shape[1] // TILE
    outgoing = put(out, arrived[0], side, 1 - core, old_begin, out_sems.at[0]) if arrivals else []
    incoming = []
    for n, (piece, (a, at, xor, low)) in enumerate(zip(pieces, parts)):
        length = piece.shape[0]
        if xor is not None:
            at = at + jnp.bitwise_xor(pos[1], xor) * length
        copy = pltpu.make_async_copy(
            piece.at[:, pl.ds(low, planes)], both.at[a, pl.ds(at, length)], sems.at[n]
        )
        copy.start()
        incoming.append(copy)
    for a in (0, 1):
        for copy, part in zip(incoming, parts):
            if part[0] == a:
                copy.wait()
        far = side if a == 0 else 1 - side
        for z in range(planes):
            to = jnp.where(far == 1, z, planes - 1 - z)
            for g in range(rows // TILE):
                block = jnp.where(far == 1, rows // TILE - 1 - g, g)
                for h in range(2 * modes // group):
                    there = pl.ds(h * group, group)
                    x = both[a, pl.ds(g * TILE, TILE), z, there, :]
                    y = jnp.dot(turn[far], to_bf16_rows(x), preferred_element_type=F32).astype(BF16)
                    final[a, to, there, pl.ds(pl.multiple_of(block * TILE, TILE), TILE), :] = y.reshape(
                        group, TILE, cols
                    )
    copy = pltpu.make_async_copy(final.at[:, :, pl.ds((1 - core) * modes, modes)], away, sems.at[len(parts)])
    copy.start()
    outgoing.append(copy)
    outgoing += put(out, final.at[:, :, pl.ds(core * modes, modes)], side, core, begin, out_sems.at[1])
    for copy in outgoing:
        copy.wait()


def settle(pos, turn, result, pieces, parts, arrived, begin, old_begin, rows, shape):
    planes, modes, _, cols = shape
    chained = result is not None
    given = ([result] if chained else []) + list(pieces) + list(arrived)
    return pl.pallas_call(
        functools.partial(
            settle_kernel, begin=begin, old_begin=old_begin, parts=tuple(parts), arrivals=len(arrived)
        ),
        out_shape=(
            jax.ShapeDtypeStruct((2, planes, modes, rows, cols), BF16),
            jax.ShapeDtypeStruct(shape, BF16),
            TOKEN,
        ),
        in_specs=[SMEM, VMEM] + [HBM] * chained + [ANY] * len(pieces) + [VMEM] * len(arrived),
        out_specs=(ANY, HBM, SMEM),
        scratch_shapes=[
            pltpu.VMEM((2, rows, planes, 2 * modes, cols), BF16),
            pltpu.VMEM((2, planes, 2 * modes, rows, cols), BF16),
            pltpu.SemaphoreType.DMA((len(pieces) + 1,)),
            pltpu.SemaphoreType.DMA((2, 2)),
        ],
        input_output_aliases={2: 1} if chained else {},
        compiler_params=params(10),
        cost_estimate=COST,
        name="settle",
    )(pos, turn, *given)


def last_kernel(pos, result, arrived, out, sems, *, begin):
    for copy in put(out, arrived, pos[0], 1 - pos[2], begin, sems):
        copy.wait()


def last(pos, result, arrived, begin):
    return pl.pallas_call(
        functools.partial(last_kernel, begin=begin),
        out_shape=jax.ShapeDtypeStruct(result.shape, BF16),
        in_specs=[SMEM, HBM, VMEM],
        out_specs=HBM,
        scratch_shapes=[pltpu.SemaphoreType.DMA((2,))],
        input_output_aliases={1: 0},
        compiler_params=params(6),
        cost_estimate=COST,
        name="settle_last",
    )(pos, result, arrived)


SIZES = (1, 1, 1, 1, 1, 1, 1, 1)
GROUPS = ((0,), (1,), (2, 3, 4), (5, 6, 7))
ENDS = ((0, 1), (2, 3), (4, 5), (6, 7))


def chunk_rows(quarter):
    return [n * (quarter // 8) for n in SIZES]


ORDER = (
    ("N", 0), ("T", 0), ("T", 1), ("R", 0), ("T", 2), ("R", 1), ("S", 0), ("R", 2), ("S", 1), ("R", 3),
    ("T", 3), ("P", 0), ("R", 4), ("P", 1), ("C", 0), ("S", 2), ("S", 3), ("C", 1), ("R", 5), ("P", 2),
    ("R", 6), ("P", 3), ("S", 4), ("C", 2), ("S", 5), ("F", 0), ("P", 4), ("C", 3), ("R", 7), ("S", 6),
    ("P", 5), ("F", 1), ("C", 4), ("S", 7), ("P", 6), ("C", 5), ("P", 7), ("F", 2), ("C", 6), ("C", 7),
    ("F", 3),
)


def turns(group):
    at = np.arange(group * TILE)
    row, mode = at // group, at % group
    same = mode[:, None] == (at // TILE)[None, :]
    straight = same & (row[:, None] == (at % TILE)[None, :])
    reverse = same & (row[:, None] == TILE - 1 - (at % TILE)[None, :])
    to_rows = np.stack([straight, reverse])
    return jnp.asarray(to_rows, BF16), jnp.asarray(to_rows.transpose(0, 2, 1), BF16)


def on_device(field, diffusion, joule, basis, quad_weight, base_conductivity, thermal_slope):
    planes, modes, size, cols = field.shape
    half, quarter = size // 2, size // 4
    spaces, devices = lax.axis_size("space"), lax.axis_size("modes")
    chips = devices // 2
    pos = jnp.stack([lax.axis_index("space") % 2, lax.axis_index("modes") // 2, lax.axis_index("modes") % 2])
    pos = pos.astype(jnp.int32)

    swap = [(i, i ^ 1) for i in range(spaces)]
    ahead = [(i, i + 4 * (i % 2) - 2) for i in range(spaces)]
    ahead = [(i, j) for i, j in ahead if 0 <= j < spaces]
    back = [(j, i) for i, j in ahead]
    beyond = [(i, i - 1 if i % 2 == 0 else i + 1) for i in range(spaces)]
    beyond = [(i, j) for i, j in beyond if 0 <= j < spaces]

    def across(x):
        return lax.ppermute(x, "space", swap)

    def ahead_of(x):
        return lax.ppermute(x, "space", ahead)

    def behind_of(x):
        return lax.ppermute(x, "space", back)

    def by_core(x):
        return lax.ppermute(x, "modes", [(j, j ^ 1) for j in range(devices)])

    def exchange(pieces):
        moved = [pieces[0]]
        for k in range(1, chips):
            moved.append(lax.ppermute(pieces[k], "modes", [(j, j ^ (2 * k)) for j in range(devices)]))
        return moved

    to_rows, _ = turns(min(2 * modes, TILE))
    _, to_modes = turns(min(2 * modes, TILE))

    points_count = basis.shape[0]
    extra = -points_count % 32
    basis = jnp.pad(basis, ((0, extra), (0, 0)))
    basis_t = basis.T
    level = quad_weight * base_conductivity
    spread_out = lambda v: jnp.broadcast_to(jnp.pad(v, (0, extra))[:, None], (points_count + extra, LANES))
    flat, swing = spread_out(level), spread_out(level * thermal_slope)

    rows_of = chunk_rows(quarter)
    begins = [sum(rows_of[:c]) for c in range(len(rows_of))]
    edges = [(begin + EDGE if begin else -EDGE, begin + rows + EDGE) for begin, rows in zip(begins, rows_of)]
    groups = [[edges[n] for n in those] for those in GROUPS]
    raws, own, other, before, blocks, cells, home, theirs = {}, {}, {}, {}, {}, {}, {}, {}
    result, arrived, old_begin = None, (), 0
    for kind, c in ORDER:
        if kind == "N":
            raw, own_rate, send_rate, own_load, send_load, pos = prepare(pos, field, diffusion, joule, groups[0])
            raws[0] = by_core(raw)
            edge_rate = lax.ppermute(send_rate[:1], "space", beyond)
            rates = ahead_of(own_rate[-1:]), across(send_rate), own_rate, edge_rate
            other_load = across(send_load)
        elif kind == "T":
            after = (rates, (basis, basis_t, flat, swing), ())[min(c, 2)]
            rest = edges[len(GROUPS[0]) :]
            raw_spans, coming = (rest, None) if c else (groups[0], rest)
            *pieces, pos = spread(pos, field, raws[c > 0], to_rows, after, groups[c], raw_spans, coming)
            if coming:
                *pieces, raw = pieces
                raws[1] = by_core(raw)
            for n in GROUPS[c]:
                send, own[n], *pieces = pieces
                other[n], before[n] = across(send), ahead_of(own[n])
            if c == 0:
                other_load = across(send_load)
        elif kind == "R":
            other[c], pos = relay(pos, (other[c],), (before[c],))
            blocks[c] = (before[c], other[c], own[c], behind_of(other[c]))
        elif kind == "S":
            *pieces, pos = sweep(pos, rates, blocks[c], blocks.get(c - 1, ()), begins[c], rows_of[c], chips)
            cells[c] = exchange(pieces)
        elif kind == "P":
            *stepped, pos = points(pos, basis, basis_t, flat, swing, (other_load, own_load), cells[c], begins[c])
            home[c] = exchange(stepped)
        elif kind == "C":
            out, pos = collect(pos, home[c])
            theirs[c] = across(out)
        else:
            begin, rows = begins[ENDS[c][0]], sum(rows_of[n] for n in ENDS[c])
            pieces, parts = [], []
            for n in ENDS[c]:
                at = begins[n] - begin
                pieces += [*home[n], theirs[n]]
                parts += [(0, at, k, planes) for k in range(chips)] + [(1, at, None, 0)]
            away, result, pos = settle(
                pos, to_modes, result, pieces, parts, arrived, begin, old_begin, rows, field.shape
            )
            arrived, old_begin = (by_core(away),), begin
    return last(pos, result, arrived[0], old_begin)


def solution(mesh):
    return jax.shard_map(
        on_device,
        mesh=mesh,
        in_specs=(
            P("space", "modes", None, None),
            P("space", None, None),
            P("space", None, None),
            P(),
            P(),
            P(),
            P(),
        ),
        out_specs=P("space", "modes", None, None),
        check_vma=False,
    )
```

```python
import functools

import jax
import jax.numpy as jnp
import numpy as np
from jax import lax
from jax.experimental import pallas as pl
from jax.experimental.pallas import tpu as pltpu
from jax.sharding import PartitionSpec as P

F32, BF16 = jnp.float32, jnp.bfloat16
ANY = pl.BlockSpec(memory_space=pl.ANY)
VMEM = pl.BlockSpec(memory_space=pltpu.VMEM)
HBM = pl.BlockSpec(memory_space=pltpu.HBM)
SMEM = pl.BlockSpec(memory_space=pltpu.SMEM)
TOKEN = jax.ShapeDtypeStruct((3,), jnp.int32)
COST = pl.CostEstimate(flops=1, bytes_accessed=1, transcendentals=0)
EDGE = 2
TILE = 16
LANES = 128


def params(mebibytes):
    return pltpu.CompilerParams(vmem_limit_bytes=mebibytes * 1024 * 1024)


def from_rows(y, group):
    if group % 16 == 0:
        return y.astype(BF16).reshape(-1, group, y.shape[1])
    return y.reshape(-1, group, y.shape[1]).astype(BF16)


def hand_on(pos, token):
    for n in range(3):
        token[n] = pos[n]


def to_bf16_rows(x):
    a, m, y = x.shape
    if m % 16 == 0:
        return x.astype(BF16).reshape(a * m, y)
    return x.astype(F32).reshape(a * m, y).astype(BF16)


def raw_copies(pos, field, raw, sems, base):
    side, core = pos[0], pos[2]
    size, depth = field.shape[2], raw.shape[3]
    begin = (1 - core) * (size // 4 + min(base, 0) * TILE) + max(base, 0) * TILE
    copies = []
    for a in range(2):
        far = 1 - side if a == 0 else side
        start = pl.multiple_of(jnp.where(far == 1, size - depth - begin, begin), TILE)
        copies.append(pltpu.make_async_copy(field.at[:, :, pl.ds(start, depth), :], raw.at[a], sems.at[a]))
    for copy in copies:
        copy.start()
    return copies


def prepare_kernel(
    pos, field, far_diffusion, far_joule, raw, own_rate, send_rate, own_load, send_load, token,
    diffusion, joule, sems, near_sems, *, base
):
    hand_on(pos, token)
    near = [
        pltpu.make_async_copy(source, to, near_sems.at[n])
        for n, (source, to) in enumerate(((far_diffusion, diffusion), (far_joule, joule)))
    ]
    for copy in near:
        copy.start()
    copies = raw_copies(pos, field, raw, sems, base)
    for copy in near:
        copy.wait()
    side, core = pos[0], pos[2]
    planes, size, _ = diffusion.shape
    begin = core * (size // 4)
    for far, rate, load in ((side, own_rate, own_load), (1 - side, send_rate, send_load)):
        for source, out, first in ((diffusion, rate, begin - 1), (joule, load, begin)):

            def row(r, _):
                place = jnp.maximum(first + r, 0)
                place = jnp.where(far == 1, size - 1 - place, place)
                for z in range(planes):
                    to = jnp.where(far == 1, z, planes - 1 - z)
                    out[to, pl.ds(r, 1), :] = source[z, pl.ds(place, 1), :]
                return 0

            lax.fori_loop(0, out.shape[1], row, 0)
        for z in range(planes):
            rate[z, pl.ds(0, 1), :] = jnp.where(core == 1, rate[z, pl.ds(0, 1), :], 0.0)
    for copy in copies:
        copy.wait()


def raw_shape(field, spans):
    planes, modes, _, cols = field.shape
    return jax.ShapeDtypeStruct((2, planes, modes, blocks_of(spans)[1] * TILE, cols), BF16)


def prepare(pos, field, diffusion, joule, spans):
    planes, size, cols = diffusion.shape
    length = size // 4 + EDGE + 1
    rate = jax.ShapeDtypeStruct((planes, length + -length % 8, cols), F32)
    load = jax.ShapeDtypeStruct((planes, size // 4, cols), F32)
    return pl.pallas_call(
        functools.partial(prepare_kernel, base=blocks_of(spans)[0]),
        out_shape=(raw_shape(field, spans), rate, rate, load, load, TOKEN),
        in_specs=[SMEM, HBM, HBM, HBM],
        out_specs=(VMEM,) * 5 + (SMEM,),
        scratch_shapes=[
            pltpu.VMEM(diffusion.shape, F32),
            pltpu.VMEM(joule.shape, F32),
            pltpu.SemaphoreType.DMA((2,)),
            pltpu.SemaphoreType.DMA((2,)),
        ],
        compiler_params=params(48),
        cost_estimate=COST,
        name="prepare",
    )(pos, field, diffusion, joule)


def spread_kernel(pos, field, raw, turn, *refs, spans, base, raw_base, next_base):
    *refs, token, window, sems, raw_sems = refs
    coming = []
    if next_base is not None:
        *refs, coming = refs
        coming = raw_copies(pos, field, coming, raw_sems, next_base)
    outs = refs[-2 * len(spans) :]
    side, core = pos[0], pos[2]
    hand_on(pos, token)
    blocks, _, planes, modes, _, cols = window.shape
    modes = modes // 2
    size = field.shape[2]
    quarter = size // 4
    depth = raw.shape[3]
    group = turn.shape[1] // TILE
    copies = {}
    for g in range(blocks):
        for a in range(2):
            far = 1 - side if a == 0 else side
            begin = core * quarter + (base + g) * TILE
            there = base + g + (core if raw_base < 0 else -raw_base)
            if base + g < 0:
                begin, there = jnp.maximum(begin, 0), jnp.maximum(there, 0)
            start = pl.multiple_of(jnp.where(far == 1, size - TILE - begin, begin), TILE)
            place = pl.multiple_of(jnp.where(far == 1, depth - TILE * (there + 1), TILE * there), TILE)
            copies[g, a] = (
                pltpu.make_async_copy(
                    field.at[:, :, pl.ds(start, TILE), :],
                    window.at[g, a, :, pl.ds(core * modes, modes)],
                    sems.at[g, a, 0],
                ),
                pltpu.make_async_copy(
                    raw.at[a, :, :, pl.ds(place, TILE), :],
                    window.at[g, a, :, pl.ds((1 - core) * modes, modes)],
                    sems.at[g, a, 1],
                ),
            )
            for copy in copies[g, a]:
                copy.start()
    for g in range(blocks):
        for a in range(2):
            far = 1 - side if a == 0 else side
            for copy in copies[g, a]:
                copy.wait()
            for z in range(planes):
                to = jnp.where(far == 1, z, planes - 1 - z)
                for h in range(2 * modes // group):
                    there = pl.ds(h * group, group)
                    x = window[g, a, z, there]
                    y = jnp.dot(turn[far], x.reshape(group * TILE, cols), preferred_element_type=F32)
                    if base + g < 0:
                        y = jnp.where(core == 1, y, 0.0)
                    y = from_rows(y, group)
                    for n, (first, last) in enumerate(spans):
                        low, high = (min(max(r - (base + g) * TILE, 0), TILE) for r in (first, last))
                        if low < high:
                            at = (base + g) * TILE + low - first
                            outs[2 * n + a][pl.ds(at, high - low), to, there, :] = y[low:high]
    for copy in coming:
        copy.wait()


def blocks_of(spans):
    base = spans[0][0] // TILE
    return base, -(-spans[-1][1] // TILE) - base


def spread(pos, field, raw, turn, after, spans, raw_spans, next_spans):
    planes, modes, _, cols = field.shape
    pieces = [jax.ShapeDtypeStruct((last - first, planes, 2 * modes, cols), BF16) for first, last in spans]
    pieces = [piece for piece in pieces for _ in range(2)]
    if next_spans:
        pieces.append(raw_shape(field, next_spans))
    base, blocks = blocks_of(spans)
    next_base = blocks_of(next_spans)[0] if next_spans else None
    return pl.pallas_call(
        functools.partial(
            spread_kernel, spans=spans, base=base, raw_base=blocks_of(raw_spans)[0], next_base=next_base
        ),
        out_shape=(*pieces, TOKEN),
        in_specs=[SMEM, HBM, ANY, VMEM] + [ANY] * len(after),
        out_specs=(VMEM,) * len(pieces) + (SMEM,),
        scratch_shapes=[
            pltpu.VMEM((blocks, 2, planes, 2 * modes, TILE, cols), BF16),
            pltpu.SemaphoreType.DMA((blocks, 2, 2)),
            pltpu.SemaphoreType.DMA((2,)),
        ],
        compiler_params=params(48),
        cost_estimate=COST,
        name="spread",
    )(pos, field, raw, turn, *after)


def relay_kernel(pos, *refs):
    token = refs[-1]
    hand_on(pos, token)


def relay(pos, passed, after):
    count = len(passed)
    return pl.pallas_call(
        relay_kernel,
        out_shape=tuple(jax.ShapeDtypeStruct(x.shape, x.dtype) for x in passed) + (TOKEN,),
        in_specs=[SMEM] + [ANY] * (count + len(after)),
        out_specs=(ANY,) * count + (SMEM,),
        input_output_aliases={1 + i: i for i in range(count)},
        compiler_params=params(1),
        cost_estimate=COST,
        name="relay",
    )(pos, *passed, *after)


def sweep_kernel(pos, *refs, begin, count, heads):
    group = 4
    rates, refs = refs[:group], refs[group:]
    blocks, refs = refs[:group], refs[group:]
    tails, refs = refs[:heads], refs[heads:]
    outs, (token, first, edge, sems) = refs[:count], refs[count:]
    hand_on(pos, token)
    planes, modes, cols = blocks[0].shape[1:]
    mine = 2 * planes
    part = outs[0].shape[0]
    rows = part * count
    lead = 2 * EDGE if heads else 0
    copies = []
    for g in range(heads):
        length = tails[g].shape[0]
        copies.append(
            pltpu.make_async_copy(
                tails[g].at[pl.ds(length - lead, lead)], edge.at[:, pl.ds(g * planes, planes)], sems.at[g]
            )
        )
    for copy in copies:
        copy.start()
    for copy in copies:
        copy.wait()
    low = planes - 1
    wide = mine + 2
    piece = min(modes, 16)
    rate = [(rates[0], 0)] + [(rates[1 + p // planes], p % planes) for p in range(mine)] + [(rates[3], 0)]

    def speed(p, row):
        ref, plane = rate[p]
        return ref[plane, pl.ds(row, 1), :]

    def field(row, p, some):
        if isinstance(row, int) and row < lead:
            return edge[row, p, some]
        return blocks[p // planes][row - lead, p % planes, some]

    def beside(x):
        parts = [x[:, h * LANES : (h + 1) * LANES] for h in range(cols // LANES)]
        up = [pltpu.roll(part, 1, 1) for part in parts]
        down = [pltpu.roll(part, LANES - 1, 1) for part in parts]
        lane = lax.broadcasted_iota(jnp.int32, parts[0].shape, 1)
        nothing = jnp.zeros_like(parts[0])
        sums = []
        for h in range(len(parts)):
            left = jnp.where(lane == 0, up[h - 1] if h else nothing, up[h])
            right = jnp.where(lane == LANES - 1, down[h + 1] if h + 1 < len(parts) else nothing, down[h])
            sums.append(left.astype(F32) + right.astype(F32))
        return jnp.concatenate(sums, axis=1)

    def once(i, number):
        for a in range(number):
            speeds = [speed(p, begin + i + a) for p in range(wide)]
            for h in range(modes // piece):
                some = pl.ds(h * piece, piece)
                kept = [field(i + 1 + a, low - 1 + p, some) for p in range(wide + 2)]
                line = [x.astype(F32) for x in kept]
                for p in range(wide):
                    centre = line[p + 1]
                    around = beside(kept[p + 1]) + (line[p] + line[p + 2])
                    around = around + (
                        field(i + a, low + p, some).astype(F32) + field(i + 2 + a, low + p, some).astype(F32)
                    )
                    first[i + a, p, some] = centre + speeds[p] * (around - 6.0 * centre)

    for i in range(0, lead, 2):
        once(i, 2)

    def pair(j, _):
        once(lead + 2 * j, 2)
        return 0

    lax.fori_loop(0, (rows + 2 - lead) // 2, pair, 0)
    number = 2 if part % 2 == 0 else 1
    for k in range(count):
        base = jnp.bitwise_xor(pos[1], k) * part

        def again(j, _):
            i = base + number * j
            for a in range(number):
                speeds = [speed(p + 1, begin + i + a + 1) for p in range(mine)]
                for h in range(modes // piece):
                    some = pl.ds(h * piece, piece)
                    line = [first[i + 1 + a, p, some] for p in range(wide)]
                    for p in range(mine):
                        centre = line[p + 1]
                        around = beside(centre) + (line[p] + line[p + 2])
                        around = around + (first[i + a, p + 1, some] + first[i + 2 + a, p + 1, some])
                        outs[k][number * j + a, p, some] = (
                            centre + speeds[p] * (around - 6.0 * centre)
                        ).astype(BF16)
            return 0

        lax.fori_loop(0, part // number, again, 0)


def sweep(pos, rates, blocks, tails, begin, rows, count):
    _, planes, modes, cols = blocks[0].shape
    mine = 2 * planes
    piece = jax.ShapeDtypeStruct((rows // count, mine, modes, cols), BF16)
    return pl.pallas_call(
        functools.partial(sweep_kernel, begin=begin, count=count, heads=len(tails)),
        out_shape=(piece,) * count + (TOKEN,),
        in_specs=[SMEM] + [VMEM] * 8 + [ANY] * len(tails),
        out_specs=(VMEM,) * count + (SMEM,),
        scratch_shapes=[
            pltpu.VMEM((rows + 2, mine + 2, modes, cols), F32),
            pltpu.VMEM((2 * EDGE, 4 * planes, modes, cols), BF16),
            pltpu.SemaphoreType.DMA((4,)),
        ],
        compiler_params=params(22),
        cost_estimate=COST,
        name="sweep",
    )(pos, *rates, *blocks, *tails)


def points_kernel(pos, basis, basis_t, flat, swing, other_load, own_load, *refs, begin):
    *refs, token, gathered, weighted, stepped = refs
    hand_on(pos, token)
    count = len(refs) // 2
    blocks, outs = refs[:count], refs[count:]
    part, planes, modes, cols = blocks[0].shape
    copies = cols // flat.shape[1]
    places = [pl.multiple_of(jnp.bitwise_xor(pos[1], k) * modes, modes) for k in range(count)]

    half = planes // 2

    def conduct(i, slot):
        for p in range(planes):
            for k in range(count):
                gathered[slot, p, pl.ds(places[k], modes)] = blocks[k][i, p].astype(gathered.dtype)
            cells = gathered[slot, p].astype(BF16)
            heat = jnp.tanh(jnp.dot(basis[...], cells, preferred_element_type=F32))
            offset = jnp.concatenate([flat[...]] * copies, axis=1)
            slope = jnp.concatenate([swing[...]] * copies, axis=1)
            weighted[slot, p] = (offset + slope * heat).astype(BF16)

    def advance(i, slot):
        place = begin + pos[1] * part + i
        for p in range(planes):
            source = jnp.dot(basis_t[...], weighted[slot, p], preferred_element_type=F32)
            load = other_load if p < half else own_load
            done = gathered[slot, p].astype(F32) + load[p % half, pl.ds(place, 1), :] * source.astype(BF16).astype(F32)
            stepped[p] = done.astype(stepped.dtype)
            for k in range(count):
                outs[k][i, p] = stepped[p, pl.ds(places[k], modes)].astype(BF16)

    conduct(0, 0)
    for i in range(part):
        if i + 1 < part:
            conduct(i + 1, (i + 1) % 2)
        advance(i, i % 2)


def points(pos, basis, basis_t, flat, swing, loads, blocks, begin):
    count = len(blocks)
    _, planes, modes, cols = blocks[0].shape
    kept = BF16 if modes % 16 == 0 else F32
    return pl.pallas_call(
        functools.partial(points_kernel, begin=begin),
        out_shape=tuple(jax.ShapeDtypeStruct(block.shape, BF16) for block in blocks) + (TOKEN,),
        in_specs=[SMEM] + [VMEM] * (6 + count),
        out_specs=(VMEM,) * count + (SMEM,),
        scratch_shapes=[
            pltpu.VMEM((2, planes, modes * count, cols), kept),
            pltpu.VMEM((2, planes, basis.shape[0], cols), BF16),
            pltpu.VMEM((planes, modes * count, cols), kept),
        ],
        compiler_params=params(16),
        cost_estimate=COST,
        name="points",
    )(pos, basis, basis_t, flat, swing, *loads, *blocks)


def collect_kernel(pos, *refs):
    *blocks, out, token, sems = refs
    hand_on(pos, token)
    part, planes = blocks[0].shape[0], out.shape[1]
    copies = []
    for k, block in enumerate(blocks):
        base = jnp.bitwise_xor(pos[1], k) * part
        copies.append(
            pltpu.make_async_copy(block.at[:, pl.ds(0, planes)], out.at[pl.ds(base, part)], sems.at[k])
        )
    for copy in copies:
        copy.start()
    for copy in copies:
        copy.wait()


def collect(pos, blocks):
    part, planes, modes, cols = blocks[0].shape
    count = len(blocks)
    shape = (part * count, planes // 2, modes, cols)
    return pl.pallas_call(
        collect_kernel,
        out_shape=(jax.ShapeDtypeStruct(shape, BF16), TOKEN),
        in_specs=[SMEM] + [ANY] * count,
        out_specs=(VMEM, SMEM),
        scratch_shapes=[pltpu.SemaphoreType.DMA((count,))],
        compiler_params=params(6),
        cost_estimate=COST,
        name="collect",
    )(pos, *blocks)


def put(out, source, side, core, begin, sems):
    rows, size = source.shape[3], out.shape[2]
    begin = core * (size // 4) + begin
    copies = []
    for a in range(2):
        far = side if a == 0 else 1 - side
        start = pl.multiple_of(jnp.where(far == 1, size - rows - begin, begin), TILE)
        copies.append(pltpu.make_async_copy(source.at[a], out.at[:, :, pl.ds(start, rows), :], sems.at[a]))
    for copy in copies:
        copy.start()
    return copies


def settle_kernel(pos, turn, *refs, begin, old_begin, parts, arrivals):
    refs = refs[-len(parts) - 7 - arrivals :]
    pieces, arrived, refs = refs[: len(parts)], refs[len(parts) : len(parts) + arrivals], refs[-7:]
    away, out, token, both, final, sems, out_sems = refs
    hand_on(pos, token)
    side, core = pos[0], pos[2]
    _, rows, planes, modes, cols = both.shape
    modes = modes // 2
    group = turn.shape[1] // TILE
    outgoing = put(out, arrived[0], side, 1 - core, old_begin, out_sems.at[0]) if arrivals else []
    incoming = []
    for n, (piece, (a, at, xor, low)) in enumerate(zip(pieces, parts)):
        length = piece.shape[0]
        if xor is not None:
            at = at + jnp.bitwise_xor(pos[1], xor) * length
        copy = pltpu.make_async_copy(
            piece.at[:, pl.ds(low, planes)], both.at[a, pl.ds(at, length)], sems.at[n]
        )
        copy.start()
        incoming.append(copy)
    for a in (0, 1):
        for copy, part in zip(incoming, parts):
            if part[0] == a:
                copy.wait()
        far = side if a == 0 else 1 - side
        for z in range(planes):
            to = jnp.where(far == 1, z, planes - 1 - z)
            for g in range(rows // TILE):
                block = jnp.where(far == 1, rows // TILE - 1 - g, g)
                for h in range(2 * modes // group):
                    there = pl.ds(h * group, group)
                    x = both[a, pl.ds(g * TILE, TILE), z, there, :]
                    y = jnp.dot(turn[far], to_bf16_rows(x), preferred_element_type=F32).astype(BF16)
                    final[a, to, there, pl.ds(pl.multiple_of(block * TILE, TILE), TILE), :] = y.reshape(
                        group, TILE, cols
                    )
    copy = pltpu.make_async_copy(final.at[:, :, pl.ds((1 - core) * modes, modes)], away, sems.at[len(parts)])
    copy.start()
    outgoing.append(copy)
    outgoing += put(out, final.at[:, :, pl.ds(core * modes, modes)], side, core, begin, out_sems.at[1])
    for copy in outgoing:
        copy.wait()


def settle(pos, turn, result, pieces, parts, arrived, begin, old_begin, rows, shape):
    planes, modes, _, cols = shape
    chained = result is not None
    given = ([result] if chained else []) + list(pieces) + list(arrived)
    return pl.pallas_call(
        functools.partial(
            settle_kernel, begin=begin, old_begin=old_begin, parts=tuple(parts), arrivals=len(arrived)
        ),
        out_shape=(
            jax.ShapeDtypeStruct((2, planes, modes, rows, cols), BF16),
            jax.ShapeDtypeStruct(shape, BF16),
            TOKEN,
        ),
        in_specs=[SMEM, VMEM] + [HBM] * chained + [ANY] * len(pieces) + [VMEM] * len(arrived),
        out_specs=(ANY, HBM, SMEM),
        scratch_shapes=[
            pltpu.VMEM((2, rows, planes, 2 * modes, cols), BF16),
            pltpu.VMEM((2, planes, 2 * modes, rows, cols), BF16),
            pltpu.SemaphoreType.DMA((len(pieces) + 1,)),
            pltpu.SemaphoreType.DMA((2, 2)),
        ],
        input_output_aliases={2: 1} if chained else {},
        compiler_params=params(10),
        cost_estimate=COST,
        name="settle",
    )(pos, turn, *given)


def last_kernel(pos, result, arrived, out, sems, *, begin):
    for copy in put(out, arrived, pos[0], 1 - pos[2], begin, sems):
        copy.wait()


def last(pos, result, arrived, begin):
    return pl.pallas_call(
        functools.partial(last_kernel, begin=begin),
        out_shape=jax.ShapeDtypeStruct(result.shape, BF16),
        in_specs=[SMEM, HBM, VMEM],
        out_specs=HBM,
        scratch_shapes=[pltpu.SemaphoreType.DMA((2,))],
        input_output_aliases={1: 0},
        compiler_params=params(6),
        cost_estimate=COST,
        name="settle_last",
    )(pos, result, arrived)


SIZES = (1, 1, 1, 1, 1, 1, 1, 1)
GROUPS = ((0,), (1,), (2, 3, 4), (5, 6, 7))
ENDS = ((0, 1), (2, 3), (4, 5), (6, 7))


def chunk_rows(quarter):
    return [n * (quarter // 8) for n in SIZES]


ORDER = (
    ("N", 0), ("T", 0), ("T", 1), ("R", 0), ("T", 2), ("R", 1), ("S", 0), ("R", 2), ("S", 1), ("R", 3),
    ("T", 3), ("P", 0), ("R", 4), ("P", 1), ("C", 0), ("S", 2), ("S", 3), ("P", 2), ("C", 1), ("R", 5),
    ("R", 6), ("P", 3), ("S", 4), ("C", 2), ("S", 5), ("F", 0), ("P", 4), ("C", 3), ("S", 6), ("R", 7),
    ("P", 5), ("F", 1), ("C", 4), ("S", 7), ("P", 6), ("C", 5), ("P", 7), ("F", 2), ("C", 6), ("C", 7),
    ("F", 3),
)


def turns(group):
    at = np.arange(group * TILE)
    row, mode = at // group, at % group
    same = mode[:, None] == (at // TILE)[None, :]
    straight = same & (row[:, None] == (at % TILE)[None, :])
    reverse = same & (row[:, None] == TILE - 1 - (at % TILE)[None, :])
    to_rows = np.stack([straight, reverse])
    return jnp.asarray(to_rows, BF16), jnp.asarray(to_rows.transpose(0, 2, 1), BF16)


def on_device(field, diffusion, joule, basis, quad_weight, base_conductivity, thermal_slope):
    planes, modes, size, cols = field.shape
    half, quarter = size // 2, size // 4
    spaces, devices = lax.axis_size("space"), lax.axis_size("modes")
    chips = devices // 2
    pos = jnp.stack([lax.axis_index("space") % 2, lax.axis_index("modes") // 2, lax.axis_index("modes") % 2])
    pos = pos.astype(jnp.int32)

    swap = [(i, i ^ 1) for i in range(spaces)]
    ahead = [(i, i + 4 * (i % 2) - 2) for i in range(spaces)]
    ahead = [(i, j) for i, j in ahead if 0 <= j < spaces]
    back = [(j, i) for i, j in ahead]
    beyond = [(i, i - 1 if i % 2 == 0 else i + 1) for i in range(spaces)]
    beyond = [(i, j) for i, j in beyond if 0 <= j < spaces]

    def across(x):
        return lax.ppermute(x, "space", swap)

    def ahead_of(x):
        return lax.ppermute(x, "space", ahead)

    def behind_of(x):
        return lax.ppermute(x, "space", back)

    def by_core(x):
        return lax.ppermute(x, "modes", [(j, j ^ 1) for j in range(devices)])

    def exchange(pieces):
        moved = [pieces[0]]
        for k in range(1, chips):
            moved.append(lax.ppermute(pieces[k], "modes", [(j, j ^ (2 * k)) for j in range(devices)]))
        return moved

    to_rows, _ = turns(min(2 * modes, TILE))
    _, to_modes = turns(min(2 * modes, TILE))

    points_count = basis.shape[0]
    extra = -points_count % 32
    basis = jnp.pad(basis, ((0, extra), (0, 0)))
    basis_t = basis.T
    level = quad_weight * base_conductivity
    spread_out = lambda v: jnp.broadcast_to(jnp.pad(v, (0, extra))[:, None], (points_count + extra, LANES))
    flat, swing = spread_out(level), spread_out(level * thermal_slope)

    rows_of = chunk_rows(quarter)
    begins = [sum(rows_of[:c]) for c in range(len(rows_of))]
    edges = [(begin + EDGE if begin else -EDGE, begin + rows + EDGE) for begin, rows in zip(begins, rows_of)]
    groups = [[edges[n] for n in those] for those in GROUPS]
    raws, own, other, before, blocks, cells, home, theirs = {}, {}, {}, {}, {}, {}, {}, {}
    result, arrived, old_begin = None, (), 0
    for kind, c in ORDER:
        if kind == "N":
            raw, own_rate, send_rate, own_load, send_load, pos = prepare(pos, field, diffusion, joule, groups[0])
            raws[0] = by_core(raw)
            edge_rate = lax.ppermute(send_rate[:1], "space", beyond)
            rates = ahead_of(own_rate[-1:]), across(send_rate), own_rate, edge_rate
            other_load = across(send_load)
        elif kind == "T":
            after = (rates[1:3], (rates[0], rates[3], basis, basis_t, flat, swing), ())[min(c, 2)]
            rest = edges[len(GROUPS[0]) :]
            raw_spans, coming = (rest, None) if c else (groups[0], rest)
            *pieces, pos = spread(pos, field, raws[c > 0], to_rows, after, groups[c], raw_spans, coming)
            if coming:
                *pieces, raw = pieces
                raws[1] = by_core(raw)
            for n in GROUPS[c]:
                send, own[n], *pieces = pieces
                other[n], before[n] = across(send), ahead_of(own[n])
            if c == 0:
                other_load = across(send_load)
        elif kind == "R":
            other[c], pos = relay(pos, (other[c],), (before[c],) if c else ())
            blocks[c] = (before[c], other[c], own[c], behind_of(other[c]))
        elif kind == "S":
            *pieces, pos = sweep(pos, rates, blocks[c], blocks.get(c - 1, ()), begins[c], rows_of[c], chips)
            cells[c] = exchange(pieces)
        elif kind == "P":
            *stepped, pos = points(pos, basis, basis_t, flat, swing, (other_load, own_load), cells[c], begins[c])
            home[c] = exchange(stepped)
        elif kind == "C":
            out, pos = collect(pos, home[c])
            theirs[c] = across(out)
        else:
            begin, rows = begins[ENDS[c][0]], sum(rows_of[n] for n in ENDS[c])
            pieces, parts = [], []
            for n in ENDS[c]:
                at = begins[n] - begin
                pieces += [*home[n], theirs[n]]
                parts += [(0, at, k, planes) for k in range(chips)] + [(1, at, None, 0)]
            away, result, pos = settle(
                pos, to_modes, result, pieces, parts, arrived, begin, old_begin, rows, field.shape
            )
            arrived, old_begin = (by_core(away),), begin
    return last(pos, result, arrived[0], old_begin)


def solution(mesh):
    return jax.shard_map(
        on_device,
        mesh=mesh,
        in_specs=(
            P("space", "modes", None, None),
            P("space", None, None),
            P("space", None, None),
            P(),
            P(),
            P(),
            P(),
        ),
        out_specs=P("space", "modes", None, None),
        check_vma=False,
    )
```
